128 devices in a mesh: group: 4 (over z), depth: 8 (over x, core), image: 4 (over y).
Axes of the slice: x: 4, y: 4, z: 4, core: 2. Of those that a mesh axis runs over, the one named last changes fastest.
Arguments:
- density: float32 [64, 192, 512], P('depth', 'group', 'image'), may hold values from 0.5 to 1.5
- velocity: float32 [3, 64, 192, 512], P(None, 'depth', 'group', 'image'), may hold values from -1.2 to 1.2
- pressure: float32 [64, 192, 512], P('depth', 'group', 'image'), may hold values from 0.5 to 1.5
- palette: float32 [4, 256], replicated, may hold values from 0.2 to 2
- palette_index: int32 [8, 256], replicated, may hold values from 0 to 255
Outputs:
- fluid_state: float32 [5, 64, 192, 512], P(None, 'depth', 'group', 'image')
- picture: float32 [8, 3, 192, 512], P('depth', None, 'group', 'image')
The draws below stay inside these ranges and needn't reach their ends.
All inputs are finite; a program needn't handle non-finite values.
Results may differ from the reference program's by a relative error of at most 0.0003.
Values sent between devices are 32-bit elements; how exact they have to be, the bound alone decides.
A program may use at most 128 MiB of HBM per device.

```python
import math
import jax
import jax.numpy as jnp
from jax import lax

NTF = 8
BINS = 256
PALETTE = 256
CX = 64
NX = 192
NY = 512
NZ = 64


def set_ends(drawn, own_key, least, largest):
    index_at = [jax.random.randint(jax.random.fold_in(own_key, axis), (), 0, length) for axis, length in enumerate(drawn.shape)]
    widest = drawn.shape.index(max(drawn.shape))
    neighbour = index_at[:widest] + [(index_at[widest] + 1) % drawn.shape[widest]] + index_at[widest + 1:]
    return drawn.at[tuple(index_at)].set(least).at[tuple(neighbour)].set(largest)


def steps_of(key, extent, shards, smallest, high):
    def one(axis_at, shards_of):
        heights = jax.random.uniform(jax.random.fold_in(jax.random.fold_in(key, 6), axis_at), (shards_of,), jnp.float32, smallest / len(shards), high / len(shards))
        return jnp.repeat(jnp.exp(heights), extent[axis_at] // shards_of).reshape((-1,) + (1,) * (len(extent) - axis_at - 1))

    gain = one(*shards[0])
    for cut in shards[1:]:
        gain = gain * one(*cut)
    return gain


def noise(own_key, shape, deviation, reach, cuts=(), kind=jnp.bfloat16):
    values = jax.random.normal(own_key, shape, jnp.float32) * deviation
    if len(cuts) > 0:
        values = steps_of(own_key, shape, cuts, -0.22, 0.18) * values
    return jnp.clip(values, min=-reach, max=reach).astype(kind)


def setup_inputs(seed: int = 0) -> dict:
    key_of = jax.random.split(jax.random.key(seed), 6)
    density = jnp.clip(0.5 + 1.0 * jax.random.uniform(key_of[0], (NZ, NX, NY), jnp.float32) ** steps_of(key_of[0], (NZ, NX, NY), ((0, 8), (1, 4), (2, 4)), -0.2, 0.2), 0.5, 1.5)
    velocity = noise(key_of[1], (3, NZ, NX, NY), 0.3, 1.2, ((1, 8), (2, 4), (3, 4)), jnp.float32)
    pressure = jnp.clip(0.5 + 1.0 * jax.random.uniform(key_of[2], (NZ, NX, NY), jnp.float32) ** steps_of(key_of[2], (NZ, NX, NY), ((0, 8), (1, 4), (2, 4)), -0.2, 0.2), 0.5, 1.5)
    palette = jnp.clip(jnp.exp(jax.random.uniform(key_of[3], (4, PALETTE), jnp.float32, math.log(0.2), math.log(2.0))), 0.2, 2.0)
    palette_index = set_ends(jax.random.randint(key_of[4], (NTF, BINS), 0, PALETTE), jax.random.fold_in(key_of[4], 1), 0, PALETTE - 1).astype(jnp.int32)
    return {"density": density, "velocity": velocity, "pressure": pressure, "palette": palette, "palette_index": palette_index}


HEAT_RATIO = 1.4
COURANT = 0.8

def leading(values, direction):
    return lax.slice_in_dim(values, 0, values.shape[direction] - 1, axis=direction)

def trailing(values, direction):
    return lax.slice_in_dim(values, 1, values.shape[direction], axis=direction)

def conserved(density, velocity, pressure):
    momentum = density[None] * velocity
    kinetic = 0.5 * density * lax.optimization_barrier(jnp.sum(velocity * velocity, axis=0))
    return jnp.concatenate([density[None], momentum, (pressure / (HEAT_RATIO - 1.0) + kinetic)[None]], axis=0)

def primitives(fluid_state):
    density = fluid_state[0]
    velocities = fluid_state[1:4] / density[None]
    kinetic = 0.5 * lax.optimization_barrier(jnp.sum(fluid_state[1:4] * velocities, axis=0))
    pressures = (HEAT_RATIO - 1.0) * (fluid_state[4] - kinetic)
    return (density, velocities, pressures)

def euler_flux(fluid_state, component):
    density, velocities, pressures = primitives(fluid_state)
    normal = velocities[component - 1]
    rows = [fluid_state[0] * normal, fluid_state[1] * normal, fluid_state[2] * normal, fluid_state[3] * normal, (fluid_state[4] + pressures) * normal]
    rows[component] = rows[component] + pressures
    signal = jnp.abs(normal) + jnp.sqrt(HEAT_RATIO * pressures / density)
    return (jnp.stack(rows), signal)

def tendency(padded):
    summed = None
    for direction, component in ((1, 3), (2, 1), (3, 2)):
        strip_cells = padded
        for across in (1, 2, 3):
            if across != direction:
                strip_cells = lax.slice_in_dim(strip_cells, 1, strip_cells.shape[across] - 1, axis=across)
        fluxes, signal = euler_flux(strip_cells, component)
        fastest_face = jnp.maximum(leading(signal, direction - 1), trailing(signal, direction - 1))
        face_flux = 0.5 * (leading(fluxes, direction) + trailing(fluxes, direction)) - 0.5 * fastest_face[None] * (trailing(strip_cells, direction) - leading(strip_cells, direction))
        change = trailing(face_flux, direction) - leading(face_flux, direction)
        summed = change if summed is None else summed + change
    return -summed

def wave_bound(fluid_state):
    density, velocities, pressures = primitives(fluid_state)
    return jnp.max(lax.optimization_barrier(jnp.sum(jnp.abs(velocities), axis=0)) + 3.0 * jnp.sqrt(HEAT_RATIO * pressures / density))

def mirror_sign():
    return jnp.array([1.0, -1.0, 1.0, 1.0, 1.0], jnp.float32)[:, None, None, None]

def colour_table(palette, palette_index):
    count_tf = palette_index.shape[0]
    count_bins = palette_index.shape[1]
    onehot = (jnp.arange(palette.shape[1], dtype=jnp.int32)[:, None] == palette_index.reshape(-1)[None, :]).astype(jnp.float32)
    table = jnp.dot(palette, onehot, precision=lax.Precision.HIGHEST)
    return table.reshape(4, count_tf, count_bins).transpose(1, 0, 2).reshape(count_tf * 4, count_bins)

def sheet_shares(screen_shades, unrolled_mass_per_volume, thermal_grid_quantity, ray_increment_distance):
    count_bins = screen_shades.shape[1]
    position = jnp.clip(unrolled_mass_per_volume - 0.5, 0.0, 1.0) * (count_bins - 1)
    hat_weights = jnp.maximum(0.0, 1.0 - jnp.abs(position[None, :] - jnp.arange(count_bins, dtype=jnp.float32)[:, None]))
    shade_mapping_index = jnp.dot(screen_shades, hat_weights, precision=lax.Precision.HIGHEST).reshape(screen_shades.shape[0] // 4, 4, unrolled_mass_per_volume.shape[0])
    extinct = shade_mapping_index[:, 3] * unrolled_mass_per_volume[None] * ray_increment_distance
    absorbance_entries = 1.0 - jnp.exp(-extinct)
    radiance_source = shade_mapping_index[:, :3] * (absorbance_entries * thermal_grid_quantity[None])[:, None]
    return (extinct, radiance_source)

def march_slab(screen_shades, density_field, heat_field, ray_increment_distance):
    count_tf = screen_shades.shape[0] // 4
    planes = density_field.shape[0]
    cell_count = density_field.shape[1] * density_field.shape[2]

    def march_plane(carried, slab):
        optical, colour = carried
        extinct, radiance_source = sheet_shares(screen_shades, slab[0], slab[1], ray_increment_distance)
        return ((optical + extinct, colour + jnp.exp(-optical)[:, None] * radiance_source), None)
    initial = (jnp.zeros((count_tf, cell_count), jnp.float32), jnp.zeros((count_tf, 3, cell_count), jnp.float32))
    (optical, colour), unused = lax.scan(march_plane, initial, (density_field.reshape(planes, cell_count), heat_field.reshape(planes, cell_count)))
    return (optical, colour)

def reference(density, velocity, pressure, palette, palette_index):
    initial_state = conserved(density, velocity, pressure)
    time_step = COURANT / wave_bound(initial_state)

    def full_tendency(values):
        walled = jnp.concatenate([values[:, :, :1] * mirror_sign(), values, values[:, :, -1:] * mirror_sign()], axis=2)
        padded = jnp.pad(walled, ((0, 0), (1, 1), (0, 0), (1, 1)), mode='wrap')

        def block_tendency(block):
            return tendency(lax.dynamic_slice_in_dim(padded, block * CX, CX + 2, axis=2))
        pieces = lax.map(block_tendency, jnp.arange(NX // CX, dtype=jnp.int32))
        return jnp.moveaxis(pieces, 0, 2).reshape(values.shape)
    section_one = initial_state + time_step * full_tendency(initial_state)
    section_two = 0.75 * initial_state + 0.25 * (section_one + time_step * full_tendency(section_one))
    section_three = initial_state / 3.0 + 2.0 / 3.0 * (section_two + time_step * full_tendency(section_two))
    screen_shades = colour_table(palette, palette_index)
    field_density, velocities, pressures = primitives(section_three)
    optical, colour = march_slab(screen_shades, field_density, pressures / field_density, 2.0 / NZ)
    return (section_three, colour.reshape(NTF, 3, NX, NY))
```

```python
import jax
import jax.numpy as jnp
from jax import lax
from jax.experimental import pallas as pl
from jax.experimental.pallas import tpu as pltpu
from jax.sharding import PartitionSpec as P

MESH = pl.DeviceIdType.MESH
HEAT_RATIO = 1.4
COURANT = 0.8
NG, ND, NI = 4, 8, 4
PZ, PX, PY = 8, 48, 128
NB = PX // 8
TOP = 8
PAIRS = [(g, i) for g in range(NG) for i in range(NI) if (g, i) != (0, 0)]


def take(table, index):
    return jnp.take_along_axis(table, index, axis=1, mode="promise_in_bounds")


def primitives(state):
    inverse = 1.0 / state[0]
    u, v, w = state[1] * inverse, state[2] * inverse, state[3] * inverse
    kinetic = 0.5 * (state[1] * u + state[2] * v + state[3] * w)
    p = (HEAT_RATIO - 1.0) * (state[4] - kinetic)
    return [u, v, w, p, jnp.sqrt(HEAT_RATIO * p * inverse)]


def flux(state, q, p, component):
    rows = [state[0] * q, state[1] * q, state[2] * q, state[3] * q, (state[4] + p) * q]
    rows[component] = rows[component] + p
    return rows


def kernel(
    density_in,
    velocity_in,
    pressure_in,
    palette_ref,
    index_ref,
    fluid_out,
    picture_out,
    raw,
    u_first,
    u_second,
    u_third,
    prim_a,
    prim_b,
    tend,
    x_send,
    x_recv,
    y_send,
    y_recv,
    y_part,
    max_own,
    max_line,
    max_mid,
    max_plane,
    fluid,
    shade,
    shade_index,
    tables,
    sheet,
    pair_recv,
    joined,
    chip_recv,
    picture,
    load_sem,
    store_sem,
    halo_send,
    halo_recv,
    line_send,
    line_recv,
    plane_send,
    plane_recv,
    pair_send_sem,
    pair_recv_sem,
    chip_send_sem,
    chip_recv_sem,
):
    g, d, i = lax.axis_index("group"), lax.axis_index("depth"), lax.axis_index("image")
    states = [u_first, u_second, u_third]
    prims = [prim_a, prim_b, prim_a]

    loads = [
        pltpu.make_async_copy(density_in, raw.at[0], load_sem.at[0]),
        pltpu.make_async_copy(velocity_in, raw.at[pl.ds(1, 3)], load_sem.at[1]),
        pltpu.make_async_copy(pressure_in, raw.at[4], load_sem.at[2]),
    ]
    for load in loads:
        load.start()

    barrier = pltpu.get_barrier_semaphore()
    for o in range(1, ND):
        pl.semaphore_signal(
            barrier, inc=1, device_id={"depth": lax.rem(d + o, ND)}, device_id_type=MESH
        )
    for og, oi in PAIRS:
        pl.semaphore_signal(
            barrier,
            inc=1,
            device_id={"group": lax.rem(g + og, NG), "image": lax.rem(i + oi, NI)},
            device_id_type=MESH,
        )

    lane = lax.broadcasted_iota(jnp.int32, (8, PY), 1)
    even = lax.rem(lane, 2) == 0
    at_first = lane == 0
    at_last = lane == PY - 1

    def pack_edges(s, z, r, new):
        rows = pl.ds(8 * r, 8)
        for c in range(5):
            shift = 16 * c + 2 * z
            turned = pltpu.roll(new[c], shift, 1)
            low = lax.rem(shift + PY - 1, PY)
            pltpu.store(
                y_send.at[s, rows, :], turned, mask=(lane == shift) | (lane == low)
            )
            if r == 0:
                x_send[s, 0, c, pl.ds(z, 1), :] = new[c][0:1]
            if r == NB - 1:
                x_send[s, 1, c, pl.ds(z, 1), :] = new[c][7:8]

    def put(s, z, r, new, derived):
        rows = pl.ds(TOP + 8 * r, 8)
        for c in range(5):
            states[s][c, z + 1, rows, :] = new[c]
            prims[s][c, z + 1, rows, :] = derived[c]
        pack_edges(s, z, r, new)

    def halo(s):
        up_d, down_d = lax.rem(d + 1, ND), lax.rem(d + ND - 1, ND)
        up_g, down_g = lax.rem(g + 1, NG), lax.rem(g + NG - 1, NG)
        up_i, down_i = lax.rem(i + 1, NI), lax.rem(i + NI - 1, NI)
        rows = pl.ds(TOP, PX)
        state = states[s]
        plan = [
            (state.at[:, 1, rows, :], state.at[:, PZ + 1, rows, :], {"depth": down_d}),
            (state.at[:, PZ, rows, :], state.at[:, 0, rows, :], {"depth": up_d}),
            (y_send.at[s], y_recv.at[s, 1], {"image": down_i}),
            (y_send.at[s], y_recv.at[s, 0], {"image": up_i}),
            (x_send.at[s, 0], x_recv.at[s, 1], {"group": down_g}),
            (x_send.at[s, 1], x_recv.at[s, 0], {"group": up_g}),
        ]
        return [
            pltpu.make_async_remote_copy(
                src_ref=src,
                dst_ref=dst,
                send_sem=halo_send.at[s, k],
                recv_sem=halo_recv.at[s, k],
                device_id=device,
                device_id_type=MESH,
            )
            for k, (src, dst, device) in enumerate(plan)
        ]

    def receive(s, copies):
        state, derived = states[s], prims[s]
        copies[4].wait_recv()
        copies[5].wait_recv()
        for side, wall, row in ((0, g == 0, TOP - 1), (1, g == NG - 1, TOP + PX)):
            cells = []
            for c in range(5):
                own = x_send[s, side, c]
                cells.append(jnp.where(wall, -own if c == 1 else own, x_recv[s, side, c]))
            values = primitives(cells)
            for c in range(5):
                for z in range(PZ):
                    state[c, z + 1, row : row + 1, :] = cells[c][z : z + 1]
                    derived[c, z + 1, row : row + 1, :] = values[c][z : z + 1]
        copies[2].wait_recv()
        copies[3].wait_recv()

        def edge(r, carry):
            rows = pl.ds(pl.multiple_of(8 * r, 8), 8)
            own, left, right = y_send[s, rows, :], y_recv[s, 0, rows, :], y_recv[s, 1, rows, :]
            inner, outer = [], []
            for c in range(5):
                inner.append(pltpu.roll(own, (PY - 16 * c) % PY, 1))
                outer.append(
                    jnp.where(
                        even,
                        pltpu.roll(left, (PY + 1 - 16 * c) % PY, 1),
                        pltpu.roll(right, (PY - 1 - 16 * c) % PY, 1),
                    )
                )
            prim_in, prim_out = primitives(inner), primitives(outer)
            fastest = jnp.maximum(
                jnp.abs(prim_in[1]) + prim_in[4], jnp.abs(prim_out[1]) + prim_out[4]
            )
            flows = flux(outer, prim_out[1], prim_out[3], 2)
            for c in range(5):
                y_part[c, rows, :] = jnp.where(even, flows[c], -flows[c]) + fastest * (
                    outer[c] - inner[c]
                )
            return carry

        lax.fori_loop(0, NB, edge, 0)
        copies[0].wait_recv()
        copies[1].wait_recv()

        def plane(r, carry):
            rows = pl.ds(pl.multiple_of(TOP + 8 * r, 8), 8)
            for z in (0, PZ + 1):
                values = primitives([state[c, z, rows, :] for c in range(5)])
                for c in range(5):
                    derived[c, z, rows, :] = values[c]
            return carry

        lax.fori_loop(0, NB, plane, 0)

    def twice_tendency(s, z, r):
        state, derived = states[s], prims[s]
        row = TOP + 8 * r
        cell = [state[c, z + 1, row : row + 8, :] for c in range(5)]
        prim = [derived[c, z + 1, row : row + 8, :] for c in range(5)]
        total = [None] * 5
        for axis, component in ((0, 3), (1, 1)):
            here = jnp.abs(prim[component - 1]) + prim[4]
            for side in (-1, 1):
                zz = z + 1 + (side if axis == 0 else 0)
                rr = row + (side if axis == 1 else 0)
                near = [state[c, zz, rr : rr + 8, :] for c in range(5)]
                q = derived[component - 1, zz, rr : rr + 8, :]
                p = derived[3, zz, rr : rr + 8, :]
                fastest = jnp.maximum(here, jnp.abs(q) + derived[4, zz, rr : rr + 8, :])
                flows = flux(near, q, p, component)
                for c in range(5):
                    part = fastest * (near[c] - cell[c])
                    part = part + flows[c] if side < 0 else part - flows[c]
                    total[c] = part if total[c] is None else total[c] + part
        here = jnp.abs(prim[1]) + prim[4]
        turn = lax.rem(PY - 2 * z, PY)
        edges = [pltpu.roll(y_part[c, 8 * r : 8 * r + 8, :], turn, 1) for c in range(5)]
        for side in (-1, 1):
            shift = 1 if side < 0 else PY - 1
            near = [pltpu.roll(cell[c], shift, 1) for c in range(5)]
            q, p = pltpu.roll(prim[1], shift, 1), pltpu.roll(prim[3], shift, 1)
            fastest = jnp.maximum(here, pltpu.roll(here, shift, 1))
            flows = flux(near, q, p, 2)
            for c in range(5):
                part = fastest * (near[c] - cell[c])
                part = part + flows[c] if side < 0 else part - flows[c]
                total[c] = total[c] + jnp.where(at_first if side < 0 else at_last, edges[c], part)
        return total

    for load in loads:
        load.wait()

    def first(z, most):
        for r in range(NB):
            rho, u, v, w, p = [raw[c, z, 8 * r : 8 * r + 8, :] for c in range(5)]
            energy = p / (HEAT_RATIO - 1.0) + 0.5 * rho * (u * u + v * v + w * w)
            sound = jnp.sqrt(HEAT_RATIO * p / rho)
            put(0, z, r, [rho, rho * u, rho * v, rho * w, energy], [u, v, w, p, sound])
            most = jnp.maximum(most, jnp.abs(u) + jnp.abs(v) + jnp.abs(w) + 3.0 * sound)
        return most

    max_own[...] = lax.fori_loop(0, PZ, first, jnp.zeros((8, PY), jnp.float32))
    pl.semaphore_wait(barrier, ND - 1 + len(PAIRS))

    lines = [
        pltpu.make_async_remote_copy(
            src_ref=max_own,
            dst_ref=max_line.at[o - 1],
            send_sem=line_send.at[o - 1],
            recv_sem=line_recv.at[o - 1],
            device_id={"depth": lax.rem(d + o, ND)},
            device_id_type=MESH,
        )
        for o in range(1, ND)
    ]
    for copy in lines:
        copy.start()
    halos = [halo(0)]
    for copy in halos[0]:
        copy.start()
    for copy in lines:
        copy.wait_recv()
    most = max_own[...]
    for o in range(ND - 1):
        most = jnp.maximum(most, max_line[o])
    max_mid[...] = most
    planes = [
        pltpu.make_async_remote_copy(
            src_ref=max_mid,
            dst_ref=max_plane.at[k],
            send_sem=plane_send.at[k],
            recv_sem=plane_recv.at[k],
            device_id={"group": lax.rem(g + og, NG), "image": lax.rem(i + oi, NI)},
            device_id_type=MESH,
        )
        for k, (og, oi) in enumerate(PAIRS)
    ]
    for copy in planes:
        copy.start()

    pick = lax.rem(2 * lane, PY)
    low, high = index_ref[:, 0:PY], index_ref[:, PY : 2 * PY]
    half = lane < PY // 2
    bins = [
        jnp.where(half, take(low, pick + k), take(high, pick + k)) for k in range(2)
    ]
    for c in range(4):
        pal_low = jnp.broadcast_to(palette_ref[c : c + 1, 0:PY], (8, PY))
        pal_high = jnp.broadcast_to(palette_ref[c : c + 1, PY : 2 * PY], (8, PY))
        colours = []
        for b in bins:
            within = b & (PY - 1)
            colours.append(jnp.where(b < PY, take(pal_low, within), take(pal_high, within)))
        after = pltpu.roll(colours[0], PY - 1, 1)
        tables[3 * c] = colours[0]
        tables[3 * c + 1] = colours[1] - colours[0]
        tables[3 * c + 2] = after - colours[1]

    receive(0, halos[0])

    def tend_plane(z, carry):
        for r in range(NB):
            total = twice_tendency(0, z, r)
            for c in range(5):
                tend[c, z, 8 * r : 8 * r + 8, :] = total[c]
        return carry

    lax.fori_loop(0, PZ, tend_plane, 0)

    for copy in planes:
        copy.wait_recv()
    most = max_mid[...]
    for k in range(len(PAIRS)):
        most = jnp.maximum(most, max_plane[k])
    half_step = (0.5 * COURANT) / jnp.broadcast_to(
        jnp.max(most, axis=(0, 1), keepdims=True), (8, PY)
    )

    def section_one(z, carry):
        for r in range(NB):
            new = [
                u_first[c, z + 1, TOP + 8 * r : TOP + 8 * r + 8, :]
                + half_step * tend[c, z, 8 * r : 8 * r + 8, :]
                for c in range(5)
            ]
            put(1, z, r, new, primitives(new))
        return carry

    lax.fori_loop(0, PZ, section_one, 0)
    halos.append(halo(1))
    for copy in halos[1]:
        copy.start()
    receive(1, halos[1])

    def section_two(z, carry):
        for r in range(NB):
            total = twice_tendency(1, z, r)
            row = TOP + 8 * r
            new = [
                0.75 * u_first[c, z + 1, row : row + 8, :]
                + 0.25 * (u_second[c, z + 1, row : row + 8, :] + half_step * total[c])
                for c in range(5)
            ]
            put(2, z, r, new, primitives(new))
        return carry

    lax.fori_loop(0, PZ, section_two, 0)
    halos.append(halo(2))
    for copy in halos[2]:
        copy.start()
    receive(2, halos[2])

    def section_three(z, carry):
        for r in range(NB):
            total = twice_tendency(2, z, r)
            row = TOP + 8 * r
            rows = slice(8 * r, 8 * r + 8)
            new = [
                u_first[c, z + 1, row : row + 8, :] * (1.0 / 3.0)
                + (2.0 / 3.0) * (u_third[c, z + 1, row : row + 8, :] + half_step * total[c])
                for c in range(5)
            ]
            for c in range(5):
                fluid[c, z, rows, :] = new[c]
            inverse = 1.0 / new[0]
            kinetic = 0.5 * inverse * (new[1] * new[1] + new[2] * new[2] + new[3] * new[3])
            position = jnp.clip(new[0] - 0.5, 0.0, 1.0) * 255.0
            index = (position * 0.5).astype(jnp.int32)
            past = position - 2.0 * index.astype(jnp.float32)
            shade_index[z, rows, :] = index
            shade[0, z, rows, :] = jnp.minimum(past, 1.0)
            shade[1, z, rows, :] = jnp.maximum(past - 1.0, 0.0)
            shade[2, z, rows, :] = new[0] * (-2.0 / (PZ * ND))
            shade[3, z, rows, :] = (HEAT_RATIO - 1.0) * (new[4] - kinetic) * inverse
        return carry

    lax.fori_loop(0, PZ, section_three, 0)
    fluid_store = pltpu.make_async_copy(fluid, fluid_out, store_sem.at[0])
    fluid_store.start()

    chip, core = d // 2, lax.rem(d, 2)

    def render(t):
        rows_of = [
            jnp.broadcast_to(tables[k, pl.ds(t, 1), :], (8, PY)) for k in range(12)
        ]

        def block(r, carry):
            rows = pl.ds(pl.multiple_of(8 * r, 8), 8)
            clear = jnp.ones((8, PY), jnp.float32)
            light = [jnp.zeros((8, PY), jnp.float32) for _ in range(3)]
            for z in range(PZ):
                index = shade_index[z, rows, :]
                one, two = shade[0, z, rows, :], shade[1, z, rows, :]
                looked = [
                    take(rows_of[3 * c], index)
                    + one * take(rows_of[3 * c + 1], index)
                    + two * take(rows_of[3 * c + 2], index)
                    for c in range(4)
                ]
                through = jnp.exp(looked[3] * shade[2, z, rows, :])
                weight = clear * (1.0 - through) * shade[3, z, rows, :]
                light = [light[c] + weight * looked[c] for c in range(3)]
                clear = clear * through
            sheet[t, 0, rows, :] = clear
            for c in range(3):
                sheet[t, c + 1, rows, :] = light[c]
            return carry

        lax.fori_loop(0, NB, block, 0)

    pair_copies, chip_copies = [], []
    for k in range(4):
        t = 2 * lax.rem(chip + 2 + k, 4) + (1 - core)
        slot = lax.rem(chip + 2 + k, 4)
        render(t)
        copy = pltpu.make_async_remote_copy(
            src_ref=sheet.at[t],
            dst_ref=pair_recv.at[slot],
            send_sem=pair_send_sem.at[slot],
            recv_sem=pair_recv_sem.at[slot],
            device_id={"depth": 2 * chip + 1 - core},
            device_id_type=MESH,
        )
        copy.start()
        pair_copies.append(copy)
    front = core == 0
    for k, offset in enumerate((2, 3, 1, 0)):
        owner = lax.rem(chip + offset, 4)
        t = 2 * owner + core
        render(t)
        pltpu.make_async_remote_copy(
            src_ref=sheet.at[t],
            dst_ref=pair_recv.at[owner],
            send_sem=pair_send_sem.at[owner],
            recv_sem=pair_recv_sem.at[owner],
            device_id={"depth": 2 * chip + 1 - core},
            device_id_type=MESH,
        ).wait_recv()
        own_clear, other_clear = sheet[t, 0], pair_recv[owner, 0]
        own_scale = jnp.where(front, 1.0, other_clear)
        other_scale = jnp.where(front, own_clear, 1.0)
        target = chip_recv.at[chip] if offset == 0 else joined.at[owner]
        target[0] = own_clear * other_clear
        for c in range(1, 4):
            target[c] = own_scale * sheet[t, c] + other_scale * pair_recv[owner, c]
        if offset != 0:
            copy = pltpu.make_async_remote_copy(
                src_ref=joined.at[owner],
                dst_ref=chip_recv.at[chip],
                send_sem=chip_send_sem.at[owner],
                recv_sem=chip_recv_sem.at[chip],
                device_id={"depth": t},
                device_id_type=MESH,
            )
            copy.start()
            chip_copies.append(copy)
    for offset in (1, 3, 2):
        source = lax.rem(chip + offset, 4)
        pltpu.make_async_remote_copy(
            src_ref=joined.at[source],
            dst_ref=chip_recv.at[source],
            send_sem=chip_send_sem.at[source],
            recv_sem=chip_recv_sem.at[source],
            device_id={"depth": 2 * source + core},
            device_id_type=MESH,
        ).wait_recv()
    ahead = chip_recv[0, 0]
    light = [chip_recv[0, c] for c in range(1, 4)]
    for k in range(1, 4):
        for c in range(3):
            light[c] = light[c] + ahead * chip_recv[k, c + 1]
        if k < 3:
            ahead = ahead * chip_recv[k, 0]
    for c in range(3):
        picture[c] = light[c]
    picture_store = pltpu.make_async_copy(picture, picture_out, store_sem.at[1])
    picture_store.start()

    for copy in lines + planes + halos[0] + halos[1] + halos[2] + pair_copies + chip_copies:
        copy.wait_send()
    fluid_store.wait()
    picture_store.wait()


def shards(density, velocity, pressure, palette, palette_index):
    f32 = jnp.float32
    any_space = pl.BlockSpec(memory_space=pl.ANY)
    vmem = pl.BlockSpec(memory_space=pltpu.VMEM)
    padded = (5, PZ + 2, PX + 16, PY)
    dma = pltpu.SemaphoreType.DMA
    fluid_state, picture = pl.pallas_call(
        kernel,
        out_shape=(
            jax.ShapeDtypeStruct((5, PZ, PX, PY), f32),
            jax.ShapeDtypeStruct((3, PX, PY), f32),
        ),
        in_specs=[any_space, any_space, any_space, vmem, vmem],
        out_specs=(any_space, any_space),
        scratch_shapes=[
            pltpu.VMEM((5, PZ, PX, PY), f32),
            pltpu.VMEM(padded, f32),
            pltpu.VMEM(padded, f32),
            pltpu.VMEM(padded, f32),
            pltpu.VMEM(padded, f32),
            pltpu.VMEM(padded, f32),
            pltpu.VMEM((5, PZ, PX, PY), f32),
            pltpu.VMEM((3, 2, 5, PZ, PY), f32),
            pltpu.VMEM((3, 2, 5, PZ, PY), f32),
            pltpu.VMEM((3, PX, PY), f32),
            pltpu.VMEM((3, 2, PX, PY), f32),
            pltpu.VMEM((5, PX, PY), f32),
            pltpu.VMEM((8, PY), f32),
            pltpu.VMEM((ND - 1, 8, PY), f32),
            pltpu.VMEM((8, PY), f32),
            pltpu.VMEM((len(PAIRS), 8, PY), f32),
            pltpu.VMEM((5, PZ, PX, PY), f32),
            pltpu.VMEM((4, PZ, PX, PY), f32),
            pltpu.VMEM((PZ, PX, PY), jnp.int32),
            pltpu.VMEM((12, 8, PY), f32),
            pltpu.VMEM((8, 4, PX, PY), f32),
            pltpu.VMEM((4, 4, PX, PY), f32),
            pltpu.VMEM((4, 4, PX, PY), f32),
            pltpu.VMEM((4, 4, PX, PY), f32),
            pltpu.VMEM((3, PX, PY), f32),
            dma((3,)),
            dma((2,)),
            dma((3, 6)),
            dma((3, 6)),
            dma((ND - 1,)),
            dma((ND - 1,)),
            dma((len(PAIRS),)),
            dma((len(PAIRS),)),
            dma((4,)),
            dma((4,)),
            dma((4,)),
            dma((4,)),
        ],
        compiler_params=pltpu.CompilerParams(
            collective_id=0, has_side_effects=True, vmem_limit_bytes=40 * 1024 * 1024
        ),
    )(density, velocity, pressure, palette, palette_index)
    return fluid_state, picture[None]


def solution(mesh):
    return jax.shard_map(
        shards,
        mesh=mesh,
        in_specs=(
            P("depth", "group", "image"),
            P(None, "depth", "group", "image"),
            P("depth", "group", "image"),
            P(),
            P(),
        ),
        out_specs=(P(None, "depth", "group", "image"), P("depth", None, "group", "image")),
        check_vma=False,
    )
```

```python
import jax
import jax.numpy as jnp
from jax import lax
from jax.experimental import pallas as pl
from jax.experimental.pallas import tpu as pltpu
from jax.sharding import PartitionSpec as P

MESH = pl.DeviceIdType.MESH
HEAT_RATIO = 1.4
COURANT = 0.8
NG, ND, NI = 4, 8, 4
PZ, PX, PY = 8, 48, 128
NB = PX // 8
TOP = 8
STEP = 2.0 / 65535.0
PAIRS = [(g, i) for g in range(NG) for i in range(NI) if (g, i) != (0, 0)]


def take(table, index):
    return jnp.take_along_axis(table, index, axis=1, mode="promise_in_bounds")


def primitives(state):
    inverse = 1.0 / state[0]
    u, v, w = state[1] * inverse, state[2] * inverse, state[3] * inverse
    kinetic = 0.5 * (state[1] * u + state[2] * v + state[3] * w)
    p = (HEAT_RATIO - 1.0) * (state[4] - kinetic)
    return [u, v, w, p, jnp.sqrt(HEAT_RATIO * p * inverse)]


def flux(state, q, p, component):
    rows = [state[0] * q, state[1] * q, state[2] * q, state[3] * q, (state[4] + p) * q]
    rows[component] = rows[component] + p
    return rows


def kernel(
    density_in,
    velocity_in,
    pressure_in,
    palette_in,
    index_in,
    fluid_out,
    picture_out,
    raw,
    palette_ref,
    index_ref,
    u_first,
    u_second,
    u_third,
    prim_a,
    prim_b,
    tend,
    x_send,
    x_recv,
    y_send,
    y_recv,
    y_part,
    max_own,
    max_line,
    max_mid,
    max_plane,
    fluid,
    shade,
    shade_index,
    tables,
    sheet,
    pair_recv,
    joined,
    chip_recv,
    picture,
    load_sem,
    store_sem,
    halo_send,
    halo_recv,
    line_send,
    line_recv,
    plane_send,
    plane_recv,
    token,
    pair_send_sem,
    pair_recv_sem,
    chip_send_sem,
    chip_recv_sem,
):
    g, d, i = lax.axis_index("group"), lax.axis_index("depth"), lax.axis_index("image")
    states = [u_first, u_second, u_third]
    prims = [prim_a, prim_b, prim_a]

    loads = [
        pltpu.make_async_copy(density_in, raw.at[0], load_sem.at[0]),
        pltpu.make_async_copy(velocity_in, raw.at[pl.ds(1, 3)], load_sem.at[1]),
        pltpu.make_async_copy(pressure_in, raw.at[4], load_sem.at[2]),
        pltpu.make_async_copy(palette_in, palette_ref, load_sem.at[3]),
        pltpu.make_async_copy(index_in, index_ref, load_sem.at[4]),
    ]
    for load in loads:
        load.start()

    barrier = pltpu.get_barrier_semaphore()
    for o in range(1, ND):
        pl.semaphore_signal(
            barrier, inc=1, device_id={"depth": lax.rem(d + o, ND)}, device_id_type=MESH
        )
    for o in range(1, NG):
        pl.semaphore_signal(
            barrier, inc=1, device_id={"group": lax.rem(g + o, NG)}, device_id_type=MESH
        )
    for o in range(1, NI):
        pl.semaphore_signal(
            barrier, inc=1, device_id={"image": lax.rem(i + o, NI)}, device_id_type=MESH
        )

    lane = lax.broadcasted_iota(jnp.int32, (8, PY), 1)
    even = lax.rem(lane, 2) == 0
    at_first = lane == 0
    at_last = lane == PY - 1

    def pack_edges(s, z, r, new):
        rows = pl.ds(8 * r, 8)
        for c in range(5):
            shift = 16 * c + 2 * z
            turned = pltpu.roll(new[c], shift, 1)
            low = lax.rem(shift + PY - 1, PY)
            pltpu.store(
                y_send.at[s, rows, :], turned, mask=(lane == shift) | (lane == low)
            )
            if r == 0:
                x_send[s, 0, c, pl.ds(z, 1), :] = new[c][0:1]
            if r == NB - 1:
                x_send[s, 1, c, pl.ds(z, 1), :] = new[c][7:8]

    def put(s, z, r, new, derived):
        rows = pl.ds(TOP + 8 * r, 8)
        for c in range(5):
            states[s][c, z + 1, rows, :] = new[c]
            prims[s][c, z + 1, rows, :] = derived[c]
        pack_edges(s, z, r, new)

    def halo(s):
        up_d, down_d = lax.rem(d + 1, ND), lax.rem(d + ND - 1, ND)
        up_g, down_g = lax.rem(g + 1, NG), lax.rem(g + NG - 1, NG)
        up_i, down_i = lax.rem(i + 1, NI), lax.rem(i + NI - 1, NI)
        rows = pl.ds(TOP, PX)
        state = states[s]
        plan = [
            (state.at[:, 1, rows, :], state.at[:, PZ + 1, rows, :], {"depth": down_d}),
            (state.at[:, PZ, rows, :], state.at[:, 0, rows, :], {"depth": up_d}),
            (y_send.at[s], y_recv.at[s, 1], {"image": down_i}),
            (y_send.at[s], y_recv.at[s, 0], {"image": up_i}),
            (x_send.at[s, 0], x_recv.at[s, 1], {"group": down_g}),
            (x_send.at[s, 1], x_recv.at[s, 0], {"group": up_g}),
        ]
        return [
            pltpu.make_async_remote_copy(
                src_ref=src,
                dst_ref=dst,
                send_sem=halo_send.at[s, k],
                recv_sem=halo_recv.at[s, k],
                device_id=device,
                device_id_type=MESH,
            )
            for k, (src, dst, device) in enumerate(plan)
        ]

    def receive(s, copies):
        state, derived = states[s], prims[s]
        copies[4].wait_recv()
        copies[5].wait_recv()
        for side, wall, row in ((0, g == 0, TOP - 1), (1, g == NG - 1, TOP + PX)):
            cells = []
            for c in range(5):
                own = x_send[s, side, c]
                cells.append(jnp.where(wall, -own if c == 1 else own, x_recv[s, side, c]))
            values = primitives(cells)
            for c in range(5):
                for z in range(PZ):
                    state[c, z + 1, row : row + 1, :] = cells[c][z : z + 1]
                    derived[c, z + 1, row : row + 1, :] = values[c][z : z + 1]
        copies[2].wait_recv()
        copies[3].wait_recv()

        def edge(r, carry):
            rows = pl.ds(pl.multiple_of(8 * r, 8), 8)
            own, left, right = y_send[s, rows, :], y_recv[s, 0, rows, :], y_recv[s, 1, rows, :]
            inner, outer = [], []
            for c in range(5):
                inner.append(pltpu.roll(own, (PY - 16 * c) % PY, 1))
                outer.append(
                    jnp.where(
                        even,
                        pltpu.roll(left, (PY + 1 - 16 * c) % PY, 1),
                        pltpu.roll(right, (PY - 1 - 16 * c) % PY, 1),
                    )
                )
            prim_in, prim_out = primitives(inner), primitives(outer)
            fastest = jnp.maximum(
                jnp.abs(prim_in[1]) + prim_in[4], jnp.abs(prim_out[1]) + prim_out[4]
            )
            flows = flux(outer, prim_out[1], prim_out[3], 2)
            for c in range(5):
                y_part[c, rows, :] = jnp.where(even, flows[c], -flows[c]) + fastest * (
                    outer[c] - inner[c]
                )
            return carry

        lax.fori_loop(0, NB, edge, 0)
        copies[0].wait_recv()
        copies[1].wait_recv()

        def plane(r, carry):
            rows = pl.ds(pl.multiple_of(TOP + 8 * r, 8), 8)
            for z in (0, PZ + 1):
                values = primitives([state[c, z, rows, :] for c in range(5)])
                for c in range(5):
                    derived[c, z, rows, :] = values[c]
            return carry

        lax.fori_loop(0, NB, plane, 0)

    def twice_tendency(s, z, r):
        state, derived = states[s], prims[s]
        row = TOP + 8 * r
        cell = [state[c, z + 1, row : row + 8, :] for c in range(5)]
        prim = [derived[c, z + 1, row : row + 8, :] for c in range(5)]
        total = [None] * 5
        for axis, component in ((0, 3), (1, 1)):
            here = jnp.abs(prim[component - 1]) + prim[4]
            for side in (-1, 1):
                zz = z + 1 + (side if axis == 0 else 0)
                rr = row + (side if axis == 1 else 0)
                near = [state[c, zz, rr : rr + 8, :] for c in range(5)]
                q = derived[component - 1, zz, rr : rr + 8, :]
                p = derived[3, zz, rr : rr + 8, :]
                fastest = jnp.maximum(here, jnp.abs(q) + derived[4, zz, rr : rr + 8, :])
                flows = flux(near, q, p, component)
                for c in range(5):
                    part = fastest * (near[c] - cell[c])
                    part = part + flows[c] if side < 0 else part - flows[c]
                    total[c] = part if total[c] is None else total[c] + part
        here = jnp.abs(prim[1]) + prim[4]
        turn = lax.rem(PY - 2 * z, PY)
        edges = [pltpu.roll(y_part[c, 8 * r : 8 * r + 8, :], turn, 1) for c in range(5)]
        for side in (-1, 1):
            shift = 1 if side < 0 else PY - 1
            near = [pltpu.roll(cell[c], shift, 1) for c in range(5)]
            q, p = pltpu.roll(prim[1], shift, 1), pltpu.roll(prim[3], shift, 1)
            fastest = jnp.maximum(here, pltpu.roll(here, shift, 1))
            flows = flux(near, q, p, 2)
            for c in range(5):
                part = fastest * (near[c] - cell[c])
                part = part + flows[c] if side < 0 else part - flows[c]
                total[c] = total[c] + jnp.where(at_first if side < 0 else at_last, edges[c], part)
        return total

    for load in loads[:3]:
        load.wait()

    def first(z, most):
        for r in range(NB):
            rho, u, v, w, p = [raw[c, z, 8 * r : 8 * r + 8, :] for c in range(5)]
            energy = p / (HEAT_RATIO - 1.0) + 0.5 * rho * (u * u + v * v + w * w)
            sound = jnp.sqrt(HEAT_RATIO * p / rho)
            put(0, z, r, [rho, rho * u, rho * v, rho * w, energy], [u, v, w, p, sound])
            most = jnp.maximum(most, jnp.abs(u) + jnp.abs(v) + jnp.abs(w) + 3.0 * sound)
        return most

    max_own[...] = lax.fori_loop(0, PZ, first, jnp.zeros((8, PY), jnp.float32))
    pl.semaphore_wait(barrier, ND + NG + NI - 3)

    for o in range(1, NI):
        pl.semaphore_signal(
            token, inc=1, device_id={"image": lax.rem(i + o, NI)}, device_id_type=MESH
        )
    lines = [
        pltpu.make_async_remote_copy(
            src_ref=max_own,
            dst_ref=max_line.at[o - 1],
            send_sem=line_send.at[o - 1],
            recv_sem=line_recv.at[o - 1],
            device_id={"depth": lax.rem(d + o, ND)},
            device_id_type=MESH,
        )
        for o in range(1, ND)
    ]
    for copy in lines:
        copy.start()
    halos = [halo(0)]
    for copy in halos[0]:
        copy.start()
    for copy in lines:
        copy.wait_recv()
    most = max_own[...]
    for o in range(ND - 1):
        most = jnp.maximum(most, max_line[o])
    max_mid[...] = most
    planes = [
        pltpu.make_async_remote_copy(
            src_ref=max_mid,
            dst_ref=max_plane.at[k],
            send_sem=plane_send.at[k],
            recv_sem=plane_recv.at[k],
            device_id={"group": lax.rem(g + og, NG), "image": lax.rem(i + oi, NI)},
            device_id_type=MESH,
        )
        for k, (og, oi) in enumerate(PAIRS)
    ]
    pl.semaphore_wait(token, NI - 1)
    for copy in planes:
        copy.start()

    for load in loads[3:]:
        load.wait()
    pick = lax.rem(2 * lane, PY)
    low, high = index_ref[:, 0:PY], index_ref[:, PY : 2 * PY]
    half = lane < PY // 2
    bins = [
        jnp.where(half, take(low, pick + k), take(high, pick + k)) for k in range(2)
    ]
    words = []
    for c in range(4):
        pal_low = jnp.broadcast_to(palette_ref[c : c + 1, 0:PY], (8, PY))
        pal_high = jnp.broadcast_to(palette_ref[c : c + 1, PY : 2 * PY], (8, PY))
        levels = []
        for b in bins:
            within = b & (PY - 1)
            colour = jnp.where(b < PY, take(pal_low, within), take(pal_high, within))
            levels.append((colour * (1.0 / STEP) + 0.5).astype(jnp.int32))
        levels.append(pltpu.roll(levels[0], PY - 1, 1))
        words.append(levels)
    for k in range(3):
        for c in range(2):
            tables[2 * k + c] = (words[c][k] - 32768) * 65536 + words[c + 2][k]

    receive(0, halos[0])

    def tend_plane(z, carry):
        for r in range(NB):
            total = twice_tendency(0, z, r)
            for c in range(5):
                tend[c, z, 8 * r : 8 * r + 8, :] = total[c]
        return carry

    lax.fori_loop(0, PZ, tend_plane, 0)

    for copy in planes:
        copy.wait_recv()
    most = max_mid[...]
    for k in range(len(PAIRS)):
        most = jnp.maximum(most, max_plane[k])
    half_step = (0.5 * COURANT) / jnp.broadcast_to(
        jnp.max(most, axis=(0, 1), keepdims=True), (8, PY)
    )

    def section_one(z, carry):
        for r in range(NB):
            new = [
                u_first[c, z + 1, TOP + 8 * r : TOP + 8 * r + 8, :]
                + half_step * tend[c, z, 8 * r : 8 * r + 8, :]
                for c in range(5)
            ]
            put(1, z, r, new, primitives(new))
        return carry

    lax.fori_loop(0, PZ, section_one, 0)
    halos.append(halo(1))
    for copy in halos[1]:
        copy.start()
    receive(1, halos[1])

    def section_two(z, carry):
        for r in range(NB):
            total = twice_tendency(1, z, r)
            row = TOP + 8 * r
            new = [
                0.75 * u_first[c, z + 1, row : row + 8, :]
                + 0.25 * (u_second[c, z + 1, row : row + 8, :] + half_step * total[c])
                for c in range(5)
            ]
            put(2, z, r, new, primitives(new))
        return carry

    lax.fori_loop(0, PZ, section_two, 0)
    halos.append(halo(2))
    for copy in halos[2]:
        copy.start()
    receive(2, halos[2])

    def section_three(z, carry):
        for r in range(NB):
            total = twice_tendency(2, z, r)
            row = TOP + 8 * r
            rows = slice(8 * r, 8 * r + 8)
            new = [
                u_first[c, z + 1, row : row + 8, :] * (1.0 / 3.0)
                + (2.0 / 3.0) * (u_third[c, z + 1, row : row + 8, :] + half_step * total[c])
                for c in range(5)
            ]
            for c in range(5):
                fluid[c, z, rows, :] = new[c]
            inverse = 1.0 / new[0]
            kinetic = 0.5 * inverse * (new[1] * new[1] + new[2] * new[2] + new[3] * new[3])
            position = jnp.clip(new[0] - 0.5, 0.0, 1.0) * 255.0
            index = (position * 0.5).astype(jnp.int32)
            past = position - 2.0 * index.astype(jnp.float32)
            shade_index[z, rows, :] = index
            shade[0, z, rows, :] = 1.0 - jnp.minimum(past, 1.0)
            shade[1, z, rows, :] = jnp.maximum(past - 1.0, 0.0)
            shade[2, z, rows, :] = new[0] * (-2.0 * STEP / (PZ * ND))
            shade[3, z, rows, :] = (STEP * (HEAT_RATIO - 1.0)) * (new[4] - kinetic) * inverse
        return carry

    lax.fori_loop(0, PZ, section_three, 0)
    fluid_store = pltpu.make_async_copy(fluid, fluid_out, store_sem.at[0])
    fluid_store.start()

    chip, core = d // 2, lax.rem(d, 2)

    def render(t):
        rows_of = [
            jnp.broadcast_to(tables[k, pl.ds(t, 1), :], (8, PY)) for k in range(6)
        ]
        for r in range(NB):
            rows = slice(8 * r, 8 * r + 8)
            clear, light = None, None
            for z in range(PZ):
                index = shade_index[z, rows, :]
                scale = [shade[0, z, rows, :], None, shade[1, z, rows, :]]
                scale[1] = 1.0 - scale[0] - scale[2]
                looked = [None] * 4
                for k in range(3):
                    for c in range(2):
                        word = take(rows_of[2 * k + c], index)
                        upper = (word >> 16).astype(jnp.float32) * scale[k]
                        lower = (word & 65535).astype(jnp.float32) * scale[k]
                        looked[c] = upper if k == 0 else looked[c] + upper
                        looked[c + 2] = lower if k == 0 else looked[c + 2] + lower
                looked[0] = looked[0] + 32768.0
                looked[1] = looked[1] + 32768.0
                through = jnp.exp(looked[3] * shade[2, z, rows, :])
                weight = (1.0 - through) * shade[3, z, rows, :]
                if z == 0:
                    light = [weight * looked[c] for c in range(3)]
                    clear = through
                else:
                    weight = weight * clear
                    light = [light[c] + weight * looked[c] for c in range(3)]
                    clear = clear * through
            sheet[t, 0, rows, :] = clear
            for c in range(3):
                sheet[t, c + 1, rows, :] = light[c]

    def pair_copy(slot):
        return pltpu.make_async_remote_copy(
            src_ref=sheet.at[2 * slot + 1 - core],
            dst_ref=pair_recv.at[slot],
            send_sem=pair_send_sem.at[slot],
            recv_sem=pair_recv_sem.at[slot],
            device_id={"depth": 2 * chip + 1 - core},
            device_id_type=MESH,
        )

    def chip_copy(owner, source):
        return pltpu.make_async_remote_copy(
            src_ref=joined.at[owner],
            dst_ref=chip_recv.at[source],
            send_sem=chip_send_sem.at[owner],
            recv_sem=chip_recv_sem.at[source],
            device_id={"depth": 2 * owner + core},
            device_id_type=MESH,
        )

    def turn(k, carry):
        mine = (k == 3) | (k == 4) | (k == 5) | (k == 7)
        offset = jnp.where(k < 6, 1 + lax.rem(k + 1, 3), 0)
        owner = lax.rem(chip + offset, 4)
        t = 2 * owner + jnp.where(mine, core, 1 - core)
        render(t)

        @pl.when(jnp.logical_not(mine))
        def _():
            pair_copy(owner).start()

        @pl.when(mine)
        def _():
            pair_copy(owner).wait_recv()
            for r in range(NB):
                rows = slice(8 * r, 8 * r + 8)
                own_clear, other_clear = sheet[t, 0, rows, :], pair_recv[owner, 0, rows, :]
                own_scale = jnp.where(core == 0, 1.0, other_clear)
                other_scale = jnp.where(core == 0, own_clear, 1.0)
                joined[owner, 0, rows, :] = own_clear * other_clear
                for c in range(1, 4):
                    joined[owner, c, rows, :] = (
                        own_scale * sheet[t, c, rows, :]
                        + other_scale * pair_recv[owner, c, rows, :]
                    )

        @pl.when(mine & (k < 6))
        def _():
            chip_copy(owner, chip).start()

        return carry

    lax.fori_loop(0, 8, turn, 0)
    for o in (1, 3, 2):
        source = lax.rem(chip + o, 4)
        chip_copy(source, source).wait_recv()
    chip_recv[chip] = joined[chip]
    ahead = chip_recv[0, 0]
    light = [chip_recv[0, c] for c in range(1, 4)]
    for k in range(1, 4):
        for c in range(3):
            light[c] = light[c] + ahead * chip_recv[k, c + 1]
        if k < 3:
            ahead = ahead * chip_recv[k, 0]
    for c in range(3):
        picture[c] = light[c]
    picture_store = pltpu.make_async_copy(picture, picture_out, store_sem.at[1])
    picture_store.start()

    for copy in lines + planes + halos[0] + halos[1] + halos[2]:
        copy.wait_send()
    for k in range(4):
        pair_copy(k).wait_send()
    for o in range(1, 4):
        source = lax.rem(chip + o, 4)
        chip_copy(source, source).wait_send()
    fluid_store.wait()
    picture_store.wait()


def shards(density, velocity, pressure, palette, palette_index):
    f32 = jnp.float32
    any_space = pl.BlockSpec(memory_space=pl.ANY)
    padded = (5, PZ + 2, PX + 16, PY)
    dma = pltpu.SemaphoreType.DMA
    fluid_state, picture = pl.pallas_call(
        kernel,
        out_shape=(
            jax.ShapeDtypeStruct((5, PZ, PX, PY), f32),
            jax.ShapeDtypeStruct((3, PX, PY), f32),
        ),
        in_specs=[any_space] * 5,
        out_specs=(any_space, any_space),
        scratch_shapes=[
            pltpu.VMEM((5, PZ, PX, PY), f32),
            pltpu.VMEM((4, 2 * PY), f32),
            pltpu.VMEM((8, 2 * PY), jnp.int32),
            pltpu.VMEM(padded, f32),
            pltpu.VMEM(padded, f32),
            pltpu.VMEM(padded, f32),
            pltpu.VMEM(padded, f32),
            pltpu.VMEM(padded, f32),
            pltpu.VMEM((5, PZ, PX, PY), f32),
            pltpu.VMEM((3, 2, 5, PZ, PY), f32),
            pltpu.VMEM((3, 2, 5, PZ, PY), f32),
            pltpu.VMEM((3, PX, PY), f32),
            pltpu.VMEM((3, 2, PX, PY), f32),
            pltpu.VMEM((5, PX, PY), f32),
            pltpu.VMEM((8, PY), f32),
            pltpu.VMEM((ND - 1, 8, PY), f32),
            pltpu.VMEM((8, PY), f32),
            pltpu.VMEM((len(PAIRS), 8, PY), f32),
            pltpu.VMEM((5, PZ, PX, PY), f32),
            pltpu.VMEM((4, PZ, PX, PY), f32),
            pltpu.VMEM((PZ, PX, PY), jnp.int32),
            pltpu.VMEM((6, 8, PY), jnp.int32),
            pltpu.VMEM((8, 4, PX, PY), f32),
            pltpu.VMEM((4, 4, PX, PY), f32),
            pltpu.VMEM((4, 4, PX, PY), f32),
            pltpu.VMEM((4, 4, PX, PY), f32),
            pltpu.VMEM((3, PX, PY), f32),
            dma((5,)),
            dma((2,)),
            dma((3, 6)),
            dma((3, 6)),
            dma((ND - 1,)),
            dma((ND - 1,)),
            dma((len(PAIRS),)),
            dma((len(PAIRS),)),
            pltpu.SemaphoreType.REGULAR,
            dma((4,)),
            dma((4,)),
            dma((4,)),
            dma((4,)),
        ],
        compiler_params=pltpu.CompilerParams(
            collective_id=0, has_side_effects=True, vmem_limit_bytes=60 * 1024 * 1024
        ),
    )(density, velocity, pressure, palette, palette_index)
    return fluid_state, picture[None]


def solution(mesh):
    return jax.shard_map(
        shards,
        mesh=mesh,
        in_specs=(
            P("depth", "group", "image"),
            P(None, "depth", "group", "image"),
            P("depth", "group", "image"),
            P(),
            P(),
        ),
        out_specs=(P(None, "depth", "group", "image"), P("depth", None, "group", "image")),
        check_vma=False,
    )
```

```python
import jax
import jax.numpy as jnp
from jax import lax
from jax.experimental import pallas as pl
from jax.experimental.pallas import tpu as pltpu
from jax.sharding import PartitionSpec as P

MESH = pl.DeviceIdType.MESH
HEAT_RATIO = 1.4
COURANT = 0.8
NG, ND, NI = 4, 8, 4
PZ, PX, PY = 8, 48, 128
NB = PX // 8
TOP = 8
STEP = 2.0 / 65535.0
PAIRS = [(g, i) for g in range(NG) for i in range(NI) if (g, i) != (0, 0)]


def take(table, index):
    return jnp.take_along_axis(table, index, axis=1, mode="promise_in_bounds")


def primitives(state):
    inverse = 1.0 / state[0]
    u, v, w = state[1] * inverse, state[2] * inverse, state[3] * inverse
    kinetic = 0.5 * (state[1] * u + state[2] * v + state[3] * w)
    p = (HEAT_RATIO - 1.0) * (state[4] - kinetic)
    return [u, v, w, p, jnp.sqrt(HEAT_RATIO * p * inverse)]


def flux(state, q, p, component):
    rows = [state[0] * q, state[1] * q, state[2] * q, state[3] * q, (state[4] + p) * q]
    rows[component] = rows[component] + p
    return rows


def kernel(
    density_in,
    velocity_in,
    pressure_in,
    palette_in,
    index_in,
    fluid_out,
    picture_out,
    raw,
    palette_ref,
    index_ref,
    u_first,
    u_second,
    u_third,
    prim_a,
    prim_b,
    tend,
    x_send,
    x_recv,
    y_send,
    y_recv,
    x_part,
    y_part,
    max_own,
    max_line,
    max_mid,
    max_plane,
    fluid,
    shade,
    shade_index,
    tables,
    sheet,
    pair_recv,
    joined,
    chip_recv,
    picture,
    load_sem,
    store_sem,
    halo_send,
    halo_recv,
    line_send,
    line_recv,
    plane_send,
    plane_recv,
    token,
    pair_send_sem,
    pair_recv_sem,
    chip_send_sem,
    chip_recv_sem,
):
    g, d, i = lax.axis_index("group"), lax.axis_index("depth"), lax.axis_index("image")
    states = [u_first, u_second, u_third]
    prims = [prim_a, prim_b, prim_a]

    loads = [
        pltpu.make_async_copy(density_in, raw.at[0], load_sem.at[0]),
        pltpu.make_async_copy(velocity_in, raw.at[pl.ds(1, 3)], load_sem.at[1]),
        pltpu.make_async_copy(pressure_in, raw.at[4], load_sem.at[2]),
        pltpu.make_async_copy(palette_in, palette_ref, load_sem.at[3]),
        pltpu.make_async_copy(index_in, index_ref, load_sem.at[4]),
    ]
    for load in loads:
        load.start()

    barrier = pltpu.get_barrier_semaphore()
    for o in range(1, ND):
        pl.semaphore_signal(
            barrier, inc=1, device_id={"depth": lax.rem(d + o, ND)}, device_id_type=MESH
        )
    for o in range(1, NG):
        pl.semaphore_signal(
            barrier, inc=1, device_id={"group": lax.rem(g + o, NG)}, device_id_type=MESH
        )
    for o in range(1, NI):
        pl.semaphore_signal(
            barrier, inc=1, device_id={"image": lax.rem(i + o, NI)}, device_id_type=MESH
        )

    lane = lax.broadcasted_iota(jnp.int32, (8, PY), 1)
    even = lax.rem(lane, 2) == 0
    at_first = lane == 0
    at_last = lane == PY - 1

    def pack_edges(s, z, r, new):
        rows = pl.ds(8 * r, 8)
        for c in range(5):
            shift = 16 * c + 2 * z
            turned = pltpu.roll(new[c], shift, 1)
            low = lax.rem(shift + PY - 1, PY)
            pltpu.store(
                y_send.at[s, rows, :], turned, mask=(lane == shift) | (lane == low)
            )
            if r == 0:
                x_send[s, 0, c, pl.ds(z, 1), :] = new[c][0:1]
            if r == NB - 1:
                x_send[s, 1, c, pl.ds(z, 1), :] = new[c][7:8]

    def put(s, z, r, new, derived):
        rows = pl.ds(TOP + 8 * r, 8)
        for c in range(5):
            states[s][c, z + 1, rows, :] = new[c]
            prims[s][c, z + 1, rows, :] = derived[c]
        pack_edges(s, z, r, new)

    def halo(s):
        up_d, down_d = lax.rem(d + 1, ND), lax.rem(d + ND - 1, ND)
        up_g, down_g = lax.rem(g + 1, NG), lax.rem(g + NG - 1, NG)
        up_i, down_i = lax.rem(i + 1, NI), lax.rem(i + NI - 1, NI)
        rows = pl.ds(TOP, PX)
        state = states[s]
        plan = [
            (state.at[:, 1, rows, :], state.at[:, PZ + 1, rows, :], {"depth": down_d}),
            (state.at[:, PZ, rows, :], state.at[:, 0, rows, :], {"depth": up_d}),
            (y_send.at[s], y_recv.at[s, 1], {"image": down_i}),
            (y_send.at[s], y_recv.at[s, 0], {"image": up_i}),
            (x_send.at[s, 0], x_recv.at[s, 1], {"group": down_g}),
            (x_send.at[s, 1], x_recv.at[s, 0], {"group": up_g}),
        ]
        return [
            pltpu.make_async_remote_copy(
                src_ref=src,
                dst_ref=dst,
                send_sem=halo_send.at[s, k],
                recv_sem=halo_recv.at[s, k],
                device_id=device,
                device_id_type=MESH,
            )
            for k, (src, dst, device) in enumerate(plan)
        ]

    row_of = lax.broadcasted_iota(jnp.int32, (8, PY), 0)
    at_top, at_bottom = row_of == 0, row_of == 7

    def from_outside(inner, outer, component, sign):
        prim_in, prim_out = primitives(inner), primitives(outer)
        fastest = jnp.maximum(
            jnp.abs(prim_in[component - 1]) + prim_in[4],
            jnp.abs(prim_out[component - 1]) + prim_out[4],
        )
        flows = flux(outer, prim_out[component - 1], prim_out[3], component)
        return [sign(flows[c]) + fastest * (outer[c] - inner[c]) for c in range(5)]

    def receive_sides(s, copies):
        copies[4].wait_recv()
        copies[5].wait_recv()
        for side, wall in ((0, g == 0), (1, g == NG - 1)):
            own = [x_send[s, side, c] for c in range(5)]
            near = [
                jnp.where(wall, -own[c] if c == 1 else own[c], x_recv[s, side, c])
                for c in range(5)
            ]
            parts = from_outside(own, near, 1, (lambda f: f) if side == 0 else (lambda f: -f))
            for c in range(5):
                x_part[side, c] = parts[c]
        copies[2].wait_recv()
        copies[3].wait_recv()

        def edge(r, carry):
            rows = pl.ds(pl.multiple_of(8 * r, 8), 8)
            own, left, right = y_send[s, rows, :], y_recv[s, 0, rows, :], y_recv[s, 1, rows, :]
            inner, outer = [], []
            for c in range(5):
                inner.append(pltpu.roll(own, (PY - 16 * c) % PY, 1))
                outer.append(
                    jnp.where(
                        even,
                        pltpu.roll(left, (PY + 1 - 16 * c) % PY, 1),
                        pltpu.roll(right, (PY - 1 - 16 * c) % PY, 1),
                    )
                )
            parts = from_outside(inner, outer, 2, lambda f: jnp.where(even, f, -f))
            for c in range(5):
                y_part[c, rows, :] = parts[c]
            return carry

        lax.fori_loop(0, NB, edge, 0, unroll=2)

    def receive_planes(s, copies):
        state, derived = states[s], prims[s]
        copies[0].wait_recv()
        copies[1].wait_recv()

        def plane(r, carry):
            rows = pl.ds(pl.multiple_of(TOP + 8 * r, 8), 8)
            for z in (0, PZ + 1):
                values = primitives([state[c, z, rows, :] for c in range(5)])
                for c in range(5):
                    derived[c, z, rows, :] = values[c]
            return carry

        lax.fori_loop(0, NB, plane, 0, unroll=2)

    def add(total, parts):
        return parts if total is None else [t + p for t, p in zip(total, parts)]

    def along_z(s, z, row, cell, prim, total):
        state, derived = states[s], prims[s]
        here = jnp.abs(prim[2]) + prim[4]
        for side in (-1, 1):
            zz = z + 1 + side
            near = [state[c, zz, row : row + 8, :] for c in range(5)]
            q, p = derived[2, zz, row : row + 8, :], derived[3, zz, row : row + 8, :]
            fastest = jnp.maximum(here, jnp.abs(q) + derived[4, zz, row : row + 8, :])
            flows = flux(near, q, p, 3)
            parts = [fastest * (near[c] - cell[c]) for c in range(5)]
            parts = [a + f if side < 0 else a - f for a, f in zip(parts, flows)]
            total = add(total, parts)
        return total

    def centre(s, z, row):
        cell = [states[s][c, z + 1, row : row + 8, :] for c in range(5)]
        return cell, [prims[s][c, z + 1, row : row + 8, :] for c in range(5)]

    def within(s, z, r, with_z):
        state, derived = states[s], prims[s]
        row = TOP + 8 * r
        cell, prim = centre(s, z, row)
        total = along_z(s, z, row, cell, prim, None) if with_z else None
        here = jnp.abs(prim[0]) + prim[4]
        for side in (-1, 1):
            rr = row + side
            near = [state[c, z + 1, rr : rr + 8, :] for c in range(5)]
            q, p = derived[0, z + 1, rr : rr + 8, :], derived[3, z + 1, rr : rr + 8, :]
            fastest = jnp.maximum(here, jnp.abs(q) + derived[4, z + 1, rr : rr + 8, :])
            flows = flux(near, q, p, 1)
            parts = [fastest * (near[c] - cell[c]) for c in range(5)]
            parts = [a + f if side < 0 else a - f for a, f in zip(parts, flows)]
            if side < 0 and r == 0:
                parts = [jnp.where(at_top, 0.0, a) for a in parts]
            if side > 0 and r == NB - 1:
                parts = [jnp.where(at_bottom, 0.0, a) for a in parts]
            total = add(total, parts)
        here = jnp.abs(prim[1]) + prim[4]
        for side in (-1, 1):
            shift = 1 if side < 0 else PY - 1
            near = [pltpu.roll(cell[c], shift, 1) for c in range(5)]
            q, p = pltpu.roll(prim[1], shift, 1), pltpu.roll(prim[3], shift, 1)
            fastest = jnp.maximum(here, pltpu.roll(here, shift, 1))
            flows = flux(near, q, p, 2)
            parts = [fastest * (near[c] - cell[c]) for c in range(5)]
            parts = [a + f if side < 0 else a - f for a, f in zip(parts, flows)]
            outside = at_first if side < 0 else at_last
            total = add(total, [jnp.where(outside, 0.0, a) for a in parts])
        return total

    def completed(s, z, r, with_z):
        rows = slice(8 * r, 8 * r + 8)
        total = [tend[c, z, rows, :] for c in range(5)]
        turn = lax.rem(PY - 2 * z, PY)
        for c in range(5):
            edges = pltpu.roll(y_part[c, rows, :], turn, 1)
            total[c] = total[c] + jnp.where(at_first | at_last, edges, 0.0)
        for side, block, place in ((0, 0, at_top), (1, NB - 1, at_bottom)):
            if r == block:
                for c in range(5):
                    line = jnp.broadcast_to(x_part[side, c, pl.ds(z, 1), :], (8, PY))
                    total[c] = total[c] + jnp.where(place, line, 0.0)
        if with_z:
            row = TOP + 8 * r
            cell, prim = centre(s, z, row)
            total = along_z(s, z, row, cell, prim, total)
        return total

    def middle_planes(visit):
        def one(z, carry):
            for r in range(NB):
                visit(z, r, False)
            return carry

        lax.fori_loop(1, PZ - 1, one, 0)

    def end_planes(visit):
        def one(k, carry):
            for r in range(NB):
                visit((PZ - 1) * k, r, True)
            return carry

        lax.fori_loop(0, 2, one, 0)

    def inside(s):
        def visit(z, r, at_end):
            total = within(s, z, r, not at_end)
            for c in range(5):
                tend[c, z, 8 * r : 8 * r + 8, :] = total[c]

        middle_planes(visit)
        end_planes(visit)

    for load in loads[:3]:
        load.wait()

    def first(z, most):
        for r in range(NB):
            rho, u, v, w, p = [raw[c, z, 8 * r : 8 * r + 8, :] for c in range(5)]
            energy = p / (HEAT_RATIO - 1.0) + 0.5 * rho * (u * u + v * v + w * w)
            sound = jnp.sqrt(HEAT_RATIO * p / rho)
            put(0, z, r, [rho, rho * u, rho * v, rho * w, energy], [u, v, w, p, sound])
            most = jnp.maximum(most, jnp.abs(u) + jnp.abs(v) + jnp.abs(w) + 3.0 * sound)
        return most

    max_own[...] = lax.fori_loop(0, PZ, first, jnp.zeros((8, PY), jnp.float32))
    pl.semaphore_wait(barrier, ND + NG + NI - 3)

    for o in range(1, NI):
        pl.semaphore_signal(
            token, inc=1, device_id={"image": lax.rem(i + o, NI)}, device_id_type=MESH
        )
    lines = [
        pltpu.make_async_remote_copy(
            src_ref=max_own,
            dst_ref=max_line.at[o - 1],
            send_sem=line_send.at[o - 1],
            recv_sem=line_recv.at[o - 1],
            device_id={"depth": lax.rem(d + o, ND)},
            device_id_type=MESH,
        )
        for o in range(1, ND)
    ]
    for copy in lines:
        copy.start()
    halos = [halo(0)]
    for copy in halos[0]:
        copy.start()
    for copy in lines:
        copy.wait_recv()
    most = max_own[...]
    for o in range(ND - 1):
        most = jnp.maximum(most, max_line[o])
    max_mid[...] = most
    planes = [
        pltpu.make_async_remote_copy(
            src_ref=max_mid,
            dst_ref=max_plane.at[k],
            send_sem=plane_send.at[k],
            recv_sem=plane_recv.at[k],
            device_id={"group": lax.rem(g + og, NG), "image": lax.rem(i + oi, NI)},
            device_id_type=MESH,
        )
        for k, (og, oi) in enumerate(PAIRS)
    ]
    pl.semaphore_wait(token, NI - 1)
    for copy in planes:
        copy.start()

    for load in loads[3:]:
        load.wait()
    pick = lax.rem(2 * lane, PY)
    low, high = index_ref[:, 0:PY], index_ref[:, PY : 2 * PY]
    half = lane < PY // 2
    bins = [
        jnp.where(half, take(low, pick + k), take(high, pick + k)) for k in range(2)
    ]
    words = []
    for c in range(4):
        pal_low = jnp.broadcast_to(palette_ref[c : c + 1, 0:PY], (8, PY))
        pal_high = jnp.broadcast_to(palette_ref[c : c + 1, PY : 2 * PY], (8, PY))
        levels = []
        for b in bins:
            spot = b & (PY - 1)
            colour = jnp.where(b < PY, take(pal_low, spot), take(pal_high, spot))
            levels.append((colour * (1.0 / STEP) + 0.5).astype(jnp.int32))
        levels.append(pltpu.roll(levels[0], PY - 1, 1))
        words.append(levels)
    for k in range(3):
        for c in range(2):
            tables[2 * k + c] = (words[c][k] - 32768) * 65536 + words[c + 2][k]

    inside(0)
    receive_sides(0, halos[0])
    receive_planes(0, halos[0])

    def complete(z, r, at_end):
        total = completed(0, z, r, at_end)
        for c in range(5):
            tend[c, z, 8 * r : 8 * r + 8, :] = total[c]

    middle_planes(complete)
    end_planes(complete)
    for copy in planes:
        copy.wait_recv()
    most = max_mid[...]
    for k in range(len(PAIRS)):
        most = jnp.maximum(most, max_plane[k])
    half_step = (0.5 * COURANT) / jnp.broadcast_to(
        jnp.max(most, axis=(0, 1), keepdims=True), (8, PY)
    )

    def section_one(z, r, at_end):
        row = TOP + 8 * r
        new = [
            u_first[c, z + 1, row : row + 8, :]
            + half_step * tend[c, z, 8 * r : 8 * r + 8, :]
            for c in range(5)
        ]
        put(1, z, r, new, primitives(new))

    def section_two(z, r, at_end):
        total = completed(1, z, r, at_end)
        row = TOP + 8 * r
        new = [
            0.75 * u_first[c, z + 1, row : row + 8, :]
            + 0.25 * (u_second[c, z + 1, row : row + 8, :] + half_step * total[c])
            for c in range(5)
        ]
        put(2, z, r, new, primitives(new))

    def section_three(z, r, at_end):
        total = completed(2, z, r, at_end)
        row = TOP + 8 * r
        rows = slice(8 * r, 8 * r + 8)
        new = [
            u_first[c, z + 1, row : row + 8, :] * (1.0 / 3.0)
            + (2.0 / 3.0) * (u_third[c, z + 1, row : row + 8, :] + half_step * total[c])
            for c in range(5)
        ]
        for c in range(5):
            fluid[c, z, rows, :] = new[c]
        inverse = 1.0 / new[0]
        kinetic = 0.5 * inverse * (new[1] * new[1] + new[2] * new[2] + new[3] * new[3])
        position = jnp.clip(new[0] - 0.5, 0.0, 1.0) * 255.0
        index = (position * 0.5).astype(jnp.int32)
        past = position - 2.0 * index.astype(jnp.float32)
        shade_index[z, rows, :] = index
        shade[0, z, rows, :] = 1.0 - jnp.minimum(past, 1.0)
        shade[1, z, rows, :] = jnp.maximum(past - 1.0, 0.0)
        shade[2, z, rows, :] = new[0] * (-2.0 * STEP / (PZ * ND))
        shade[3, z, rows, :] = (STEP * (HEAT_RATIO - 1.0)) * (new[4] - kinetic) * inverse

    halos.append(halo(1))
    end_planes(section_one)
    for copy in halos[1][:2]:
        copy.start()
    middle_planes(section_one)
    for copy in halos[1][2:]:
        copy.start()
    inside(1)
    receive_sides(1, halos[1])
    middle_planes(section_two)
    receive_planes(1, halos[1])
    halos.append(halo(2))
    end_planes(section_two)
    for copy in halos[2]:
        copy.start()
    inside(2)
    receive_sides(2, halos[2])
    middle_planes(section_three)
    receive_planes(2, halos[2])
    end_planes(section_three)
    fluid_store = pltpu.make_async_copy(fluid, fluid_out, store_sem.at[0])
    fluid_store.start()

    chip, core = d // 2, lax.rem(d, 2)

    def render(t):
        rows_of = [
            jnp.broadcast_to(tables[k, pl.ds(t, 1), :], (8, PY)) for k in range(6)
        ]
        for r in range(NB):
            rows = slice(8 * r, 8 * r + 8)
            clear, light = None, None
            for z in range(PZ):
                index = shade_index[z, rows, :]
                scale = [shade[0, z, rows, :], None, shade[1, z, rows, :]]
                scale[1] = 1.0 - scale[0] - scale[2]
                looked = [None] * 4
                for k in range(3):
                    for c in range(2):
                        word = take(rows_of[2 * k + c], index)
                        upper = (word >> 16).astype(jnp.float32) * scale[k]
                        lower = (word & 65535).astype(jnp.float32) * scale[k]
                        looked[c] = upper if k == 0 else looked[c] + upper
                        looked[c + 2] = lower if k == 0 else looked[c + 2] + lower
                looked[0] = looked[0] + 32768.0
                looked[1] = looked[1] + 32768.0
                through = jnp.exp(looked[3] * shade[2, z, rows, :])
                weight = (1.0 - through) * shade[3, z, rows, :]
                if z == 0:
                    light = [weight * looked[c] for c in range(3)]
                    clear = through
                else:
                    weight = weight * clear
                    light = [light[c] + weight * looked[c] for c in range(3)]
                    clear = clear * through
            sheet[t, 0, rows, :] = clear
            for c in range(3):
                sheet[t, c + 1, rows, :] = light[c]

    def pair_copy(slot):
        return pltpu.make_async_remote_copy(
            src_ref=sheet.at[2 * slot + 1 - core],
            dst_ref=pair_recv.at[slot],
            send_sem=pair_send_sem.at[slot],
            recv_sem=pair_recv_sem.at[slot],
            device_id={"depth": 2 * chip + 1 - core},
            device_id_type=MESH,
        )

    def chip_copy(owner, source):
        return pltpu.make_async_remote_copy(
            src_ref=joined.at[owner],
            dst_ref=chip_recv.at[source],
            send_sem=chip_send_sem.at[owner],
            recv_sem=chip_recv_sem.at[source],
            device_id={"depth": 2 * owner + core},
            device_id_type=MESH,
        )

    def turn(k, carry):
        mine = (k == 3) | (k == 4) | (k == 5) | (k == 7)
        offset = jnp.where(k < 6, 1 + lax.rem(k + 1, 3), 0)
        owner = lax.rem(chip + offset, 4)
        t = 2 * owner + jnp.where(mine, core, 1 - core)
        render(t)

        @pl.when(jnp.logical_not(mine))
        def _():
            pair_copy(owner).start()

        @pl.when(mine)
        def _():
            pair_copy(owner).wait_recv()
            for r in range(NB):
                rows = slice(8 * r, 8 * r + 8)
                own_clear, other_clear = sheet[t, 0, rows, :], pair_recv[owner, 0, rows, :]
                own_scale = jnp.where(core == 0, 1.0, other_clear)
                other_scale = jnp.where(core == 0, own_clear, 1.0)
                joined[owner, 0, rows, :] = own_clear * other_clear
                for c in range(1, 4):
                    joined[owner, c, rows, :] = (
                        own_scale * sheet[t, c, rows, :]
                        + other_scale * pair_recv[owner, c, rows, :]
                    )

        @pl.when(mine & (k < 6))
        def _():
            chip_copy(owner, chip).start()

        return carry

    lax.fori_loop(0, 8, turn, 0)
    for o in (1, 3, 2):
        source = lax.rem(chip + o, 4)
        chip_copy(source, source).wait_recv()
    chip_recv[chip] = joined[chip]
    ahead = chip_recv[0, 0]
    light = [chip_recv[0, c] for c in range(1, 4)]
    for k in range(1, 4):
        for c in range(3):
            light[c] = light[c] + ahead * chip_recv[k, c + 1]
        if k < 3:
            ahead = ahead * chip_recv[k, 0]
    for c in range(3):
        picture[c] = light[c]
    picture_store = pltpu.make_async_copy(picture, picture_out, store_sem.at[1])
    picture_store.start()

    for copy in lines + planes + halos[0] + halos[1] + halos[2]:
        copy.wait_send()
    for k in range(4):
        pair_copy(k).wait_send()
    for o in range(1, 4):
        source = lax.rem(chip + o, 4)
        chip_copy(source, source).wait_send()
    fluid_store.wait()
    picture_store.wait()


def shards(density, velocity, pressure, palette, palette_index):
    f32 = jnp.float32
    any_space = pl.BlockSpec(memory_space=pl.ANY)
    padded = (5, PZ + 2, PX + 16, PY)
    dma = pltpu.SemaphoreType.DMA
    fluid_state, picture = pl.pallas_call(
        kernel,
        out_shape=(
            jax.ShapeDtypeStruct((5, PZ, PX, PY), f32),
            jax.ShapeDtypeStruct((3, PX, PY), f32),
        ),
        in_specs=[any_space] * 5,
        out_specs=(any_space, any_space),
        scratch_shapes=[
            pltpu.VMEM((5, PZ, PX, PY), f32),
            pltpu.VMEM((4, 2 * PY), f32),
            pltpu.VMEM((8, 2 * PY), jnp.int32),
            pltpu.VMEM(padded, f32),
            pltpu.VMEM(padded, f32),
            pltpu.VMEM(padded, f32),
            pltpu.VMEM(padded, f32),
            pltpu.VMEM(padded, f32),
            pltpu.VMEM((5, PZ, PX, PY), f32),
            pltpu.VMEM((3, 2, 5, PZ, PY), f32),
            pltpu.VMEM((3, 2, 5, PZ, PY), f32),
            pltpu.VMEM((3, PX, PY), f32),
            pltpu.VMEM((3, 2, PX, PY), f32),
            pltpu.VMEM((2, 5, PZ, PY), f32),
            pltpu.VMEM((5, PX, PY), f32),
            pltpu.VMEM((8, PY), f32),
            pltpu.VMEM((ND - 1, 8, PY), f32),
            pltpu.VMEM((8, PY), f32),
            pltpu.VMEM((len(PAIRS), 8, PY), f32),
            pltpu.VMEM((5, PZ, PX, PY), f32),
            pltpu.VMEM((4, PZ, PX, PY), f32),
            pltpu.VMEM((PZ, PX, PY), jnp.int32),
            pltpu.VMEM((6, 8, PY), jnp.int32),
            pltpu.VMEM((8, 4, PX, PY), f32),
            pltpu.VMEM((4, 4, PX, PY), f32),
            pltpu.VMEM((4, 4, PX, PY), f32),
            pltpu.VMEM((4, 4, PX, PY), f32),
            pltpu.VMEM((3, PX, PY), f32),
            dma((5,)),
            dma((2,)),
            dma((3, 6)),
            dma((3, 6)),
            dma((ND - 1,)),
            dma((ND - 1,)),
            dma((len(PAIRS),)),
            dma((len(PAIRS),)),
            pltpu.SemaphoreType.REGULAR,
            dma((4,)),
            dma((4,)),
            dma((4,)),
            dma((4,)),
        ],
        compiler_params=pltpu.CompilerParams(
            collective_id=0, has_side_effects=True, vmem_limit_bytes=60 * 1024 * 1024
        ),
    )(density, velocity, pressure, palette, palette_index)
    return fluid_state, picture[None]


def solution(mesh):
    return jax.shard_map(
        shards,
        mesh=mesh,
        in_specs=(
            P("depth", "group", "image"),
            P(None, "depth", "group", "image"),
            P("depth", "group", "image"),
            P(),
            P(),
        ),
        out_specs=(P(None, "depth", "group", "image"), P("depth", None, "group", "image")),
        check_vma=False,
    )
```

```python
import jax
import jax.numpy as jnp
from jax import lax
from jax.experimental import pallas as pl
from jax.experimental.pallas import tpu as pltpu
from jax.sharding import PartitionSpec as P

MESH = pl.DeviceIdType.MESH
HEAT_RATIO = 1.4
COURANT = 0.8
NG, ND, NI = 4, 8, 4
PZ, PX, PY = 8, 48, 128
NB = PX // 8
TOP = 8
STEP = 2.0 / 65535.0
PAIRS = [(g, i) for g in range(NG) for i in range(NI) if (g, i) != (0, 0)]


def take(table, index):
    return jnp.take_along_axis(table, index, axis=1, mode="promise_in_bounds")


def primitives(state):
    inverse = 1.0 / state[0]
    u, v, w = state[1] * inverse, state[2] * inverse, state[3] * inverse
    kinetic = 0.5 * (state[1] * u + state[2] * v + state[3] * w)
    p = (HEAT_RATIO - 1.0) * (state[4] - kinetic)
    return [u, v, w, p, jnp.sqrt(HEAT_RATIO * p * inverse)]


def flux(state, q, p, component):
    rows = [state[0] * q, state[1] * q, state[2] * q, state[3] * q, (state[4] + p) * q]
    rows[component] = rows[component] + p
    return rows


def kernel(
    density_in,
    velocity_in,
    pressure_in,
    palette_in,
    index_in,
    fluid_out,
    picture_out,
    raw,
    palette_ref,
    index_ref,
    u_first,
    u_second,
    u_third,
    prim_a,
    prim_b,
    tend,
    tend_recv,
    x_send,
    x_recv,
    y_send,
    y_recv,
    x_part,
    y_part,
    max_own,
    max_line,
    max_mid,
    max_plane,
    fluid,
    shade,
    shade_index,
    tables,
    sheet,
    pair_recv,
    joined,
    chip_recv,
    picture,
    load_sem,
    store_sem,
    halo_send,
    halo_recv,
    line_send,
    line_recv,
    plane_send,
    plane_recv,
    token,
    pair_send_sem,
    pair_recv_sem,
    chip_send_sem,
    chip_recv_sem,
):
    g, d, i = lax.axis_index("group"), lax.axis_index("depth"), lax.axis_index("image")
    states = [u_first, u_second, u_third]
    prims = [prim_a, prim_b, prim_a]

    loads = [
        pltpu.make_async_copy(density_in, raw.at[0], load_sem.at[0]),
        pltpu.make_async_copy(velocity_in, raw.at[pl.ds(1, 3)], load_sem.at[1]),
        pltpu.make_async_copy(pressure_in, raw.at[4], load_sem.at[2]),
        pltpu.make_async_copy(palette_in, palette_ref, load_sem.at[3]),
        pltpu.make_async_copy(index_in, index_ref, load_sem.at[4]),
    ]
    for load in loads:
        load.start()

    barrier = pltpu.get_barrier_semaphore()
    for o in range(1, ND):
        pl.semaphore_signal(
            barrier, inc=1, device_id={"depth": lax.rem(d + o, ND)}, device_id_type=MESH
        )
    for o in range(1, NG):
        pl.semaphore_signal(
            barrier, inc=1, device_id={"group": lax.rem(g + o, NG)}, device_id_type=MESH
        )
    for o in range(1, NI):
        pl.semaphore_signal(
            barrier, inc=1, device_id={"image": lax.rem(i + o, NI)}, device_id_type=MESH
        )

    lane = lax.broadcasted_iota(jnp.int32, (8, PY), 1)
    even = lax.rem(lane, 2) == 0
    at_first = lane == 0
    at_last = lane == PY - 1

    def pack_edges(s, z, r, new):
        rows = pl.ds(8 * r, 8)
        for c in range(5):
            shift = 16 * c + 2 * z
            turned = pltpu.roll(new[c], shift, 1)
            low = lax.rem(shift + PY - 1, PY)
            pltpu.store(
                y_send.at[s, rows, :], turned, mask=(lane == shift) | (lane == low)
            )
            if r == 0:
                x_send[s, 0, c, pl.ds(z, 1), :] = new[c][0:1]
            if r == NB - 1:
                x_send[s, 1, c, pl.ds(z, 1), :] = new[c][7:8]

    def put(s, z, r, new, derived):
        rows = pl.ds(TOP + 8 * r, 8)
        for c in range(5):
            states[s][c, z + 1, rows, :] = new[c]
            prims[s][c, z + 1, rows, :] = derived[c]
        pack_edges(3 if s == 1 else s, z, r, new)

    def halo(s):
        up_d, down_d = lax.rem(d + 1, ND), lax.rem(d + ND - 1, ND)
        up_g, down_g = lax.rem(g + 1, NG), lax.rem(g + NG - 1, NG)
        up_i, down_i = lax.rem(i + 1, NI), lax.rem(i + NI - 1, NI)
        rows = pl.ds(TOP, PX)
        if s == 1:
            below, above = tend.at[:, 0], tend.at[:, PZ - 1]
            to_above, to_below = tend_recv.at[1], tend_recv.at[0]
        else:
            state = states[s]
            below, above = state.at[:, 1, rows, :], state.at[:, PZ, rows, :]
            to_above, to_below = state.at[:, PZ + 1, rows, :], state.at[:, 0, rows, :]
        plan = [
            (below, to_above, {"depth": down_d}),
            (above, to_below, {"depth": up_d}),
            (y_send.at[s], y_recv.at[s, 1], {"image": down_i}),
            (y_send.at[s], y_recv.at[s, 0], {"image": up_i}),
            (x_send.at[s, 0], x_recv.at[s, 1], {"group": down_g}),
            (x_send.at[s, 1], x_recv.at[s, 0], {"group": up_g}),
        ]
        return [
            pltpu.make_async_remote_copy(
                src_ref=src,
                dst_ref=dst,
                send_sem=halo_send.at[s, k],
                recv_sem=halo_recv.at[s, k],
                device_id=device,
                device_id_type=MESH,
            )
            for k, (src, dst, device) in enumerate(plan)
        ]

    row_of = lax.broadcasted_iota(jnp.int32, (8, PY), 0)
    at_top, at_bottom = row_of == 0, row_of == 7

    def from_outside(inner, outer, component, sign):
        prim_in, prim_out = primitives(inner), primitives(outer)
        fastest = jnp.maximum(
            jnp.abs(prim_in[component - 1]) + prim_in[4],
            jnp.abs(prim_out[component - 1]) + prim_out[4],
        )
        flows = flux(outer, prim_out[component - 1], prim_out[3], component)
        return [sign(flows[c]) + fastest * (outer[c] - inner[c]) for c in range(5)]

    def receive_sides(s, copies):
        s = 3 if s == 1 else s
        if copies is not None:
            copies[4].wait_recv()
            copies[5].wait_recv()
        for side, wall in ((0, g == 0), (1, g == NG - 1)):
            own = [x_send[s, side, c] for c in range(5)]
            near = [
                jnp.where(wall, -own[c] if c == 1 else own[c], x_recv[s, side, c])
                for c in range(5)
            ]
            parts = from_outside(own, near, 1, (lambda f: f) if side == 0 else (lambda f: -f))
            for c in range(5):
                x_part[side, c] = parts[c]
        if copies is not None:
            copies[2].wait_recv()
            copies[3].wait_recv()

        def edge(r, carry):
            rows = pl.ds(pl.multiple_of(8 * r, 8), 8)
            own, left, right = y_send[s, rows, :], y_recv[s, 0, rows, :], y_recv[s, 1, rows, :]
            inner, outer = [], []
            for c in range(5):
                inner.append(pltpu.roll(own, (PY - 16 * c) % PY, 1))
                outer.append(
                    jnp.where(
                        even,
                        pltpu.roll(left, (PY + 1 - 16 * c) % PY, 1),
                        pltpu.roll(right, (PY - 1 - 16 * c) % PY, 1),
                    )
                )
            parts = from_outside(inner, outer, 2, lambda f: jnp.where(even, f, -f))
            for c in range(5):
                y_part[c, rows, :] = parts[c]
            return carry

        lax.fori_loop(0, NB, edge, 0, unroll=2)

    def receive_planes(s, copies):
        state, derived = states[s], prims[s]
        if copies is not None:
            copies[0].wait_recv()
            copies[1].wait_recv()

        def plane(r, carry):
            rows = pl.ds(pl.multiple_of(TOP + 8 * r, 8), 8)
            for z in (0, PZ + 1):
                values = primitives([state[c, z, rows, :] for c in range(5)])
                for c in range(5):
                    derived[c, z, rows, :] = values[c]
            return carry

        lax.fori_loop(0, NB, plane, 0, unroll=2)

    def add(total, parts):
        return parts if total is None else [t + p for t, p in zip(total, parts)]

    def along_z(s, z, row, cell, prim, total):
        state, derived = states[s], prims[s]
        here = jnp.abs(prim[2]) + prim[4]
        for side in (-1, 1):
            zz = z + 1 + side
            near = [state[c, zz, row : row + 8, :] for c in range(5)]
            q, p = derived[2, zz, row : row + 8, :], derived[3, zz, row : row + 8, :]
            fastest = jnp.maximum(here, jnp.abs(q) + derived[4, zz, row : row + 8, :])
            flows = flux(near, q, p, 3)
            parts = [fastest * (near[c] - cell[c]) for c in range(5)]
            parts = [a + f if side < 0 else a - f for a, f in zip(parts, flows)]
            total = add(total, parts)
        return total

    def centre(s, z, row):
        cell = [states[s][c, z + 1, row : row + 8, :] for c in range(5)]
        return cell, [prims[s][c, z + 1, row : row + 8, :] for c in range(5)]

    def within(s, z, r, with_z):
        state, derived = states[s], prims[s]
        row = TOP + 8 * r
        cell, prim = centre(s, z, row)
        total = along_z(s, z, row, cell, prim, None) if with_z else None
        here = jnp.abs(prim[0]) + prim[4]
        for side in (-1, 1):
            rr = row + side
            near = [state[c, z + 1, rr : rr + 8, :] for c in range(5)]
            q, p = derived[0, z + 1, rr : rr + 8, :], derived[3, z + 1, rr : rr + 8, :]
            fastest = jnp.maximum(here, jnp.abs(q) + derived[4, z + 1, rr : rr + 8, :])
            flows = flux(near, q, p, 1)
            parts = [fastest * (near[c] - cell[c]) for c in range(5)]
            parts = [a + f if side < 0 else a - f for a, f in zip(parts, flows)]
            if side < 0 and r == 0:
                parts = [jnp.where(at_top, 0.0, a) for a in parts]
            if side > 0 and r == NB - 1:
                parts = [jnp.where(at_bottom, 0.0, a) for a in parts]
            total = add(total, parts)
        here = jnp.abs(prim[1]) + prim[4]
        for side in (-1, 1):
            shift = 1 if side < 0 else PY - 1
            near = [pltpu.roll(cell[c], shift, 1) for c in range(5)]
            q, p = pltpu.roll(prim[1], shift, 1), pltpu.roll(prim[3], shift, 1)
            fastest = jnp.maximum(here, pltpu.roll(here, shift, 1))
            flows = flux(near, q, p, 2)
            parts = [fastest * (near[c] - cell[c]) for c in range(5)]
            parts = [a + f if side < 0 else a - f for a, f in zip(parts, flows)]
            outside = at_first if side < 0 else at_last
            total = add(total, [jnp.where(outside, 0.0, a) for a in parts])
        return total

    def completed(s, z, r, with_z, total=None):
        rows = slice(8 * r, 8 * r + 8)
        if total is None:
            total = [tend[c, z, rows, :] for c in range(5)]
        turn = lax.rem(PY - 2 * z, PY)
        for c in range(5):
            edges = pltpu.roll(y_part[c, rows, :], turn, 1)
            total[c] = total[c] + jnp.where(at_first | at_last, edges, 0.0)
        for side, block, place in ((0, 0, at_top), (1, NB - 1, at_bottom)):
            if r == block:
                for c in range(5):
                    line = jnp.broadcast_to(x_part[side, c, pl.ds(z, 1), :], (8, PY))
                    total[c] = total[c] + jnp.where(place, line, 0.0)
        if with_z:
            row = TOP + 8 * r
            cell, prim = centre(s, z, row)
            total = along_z(s, z, row, cell, prim, total)
        return total

    def middle_planes(visit):
        def one(z, carry):
            for r in range(NB):
                visit(z, r, False)
            return carry

        lax.fori_loop(1, PZ - 1, one, 0)

    def end_planes(visit):
        def one(k, carry):
            for r in range(NB):
                visit((PZ - 1) * k, r, True)
            return carry

        lax.fori_loop(0, 2, one, 0)

    def inside(s):
        def visit(z, r, at_end):
            total = within(s, z, r, not at_end)
            for c in range(5):
                tend[c, z, 8 * r : 8 * r + 8, :] = total[c]

        middle_planes(visit)
        end_planes(visit)

    for load in loads[:3]:
        load.wait()

    def signals(z, most):
        for r in range(NB):
            rho, u, v, w, p = [raw[c, z, 8 * r : 8 * r + 8, :] for c in range(5)]
            sound = jnp.sqrt(HEAT_RATIO * p / rho)
            prims[0][4, z + 1, TOP + 8 * r : TOP + 8 * r + 8, :] = sound
            most = jnp.maximum(most, jnp.abs(u) + jnp.abs(v) + jnp.abs(w) + 3.0 * sound)
        return most

    max_own[...] = lax.fori_loop(0, PZ, signals, jnp.zeros((8, PY), jnp.float32), unroll=2)

    def first(z, carry):
        for r in range(NB):
            rho, u, v, w, p = [raw[c, z, 8 * r : 8 * r + 8, :] for c in range(5)]
            energy = p / (HEAT_RATIO - 1.0) + 0.5 * rho * (u * u + v * v + w * w)
            sound = prims[0][4, z + 1, TOP + 8 * r : TOP + 8 * r + 8, :]
            put(0, z, r, [rho, rho * u, rho * v, rho * w, energy], [u, v, w, p, sound])
        return carry

    pl.semaphore_wait(barrier, ND + NG + NI - 3)

    for o in range(1, NI):
        pl.semaphore_signal(
            token, inc=1, device_id={"image": lax.rem(i + o, NI)}, device_id_type=MESH
        )
    lines = [
        pltpu.make_async_remote_copy(
            src_ref=max_own,
            dst_ref=max_line.at[o - 1],
            send_sem=line_send.at[o - 1],
            recv_sem=line_recv.at[o - 1],
            device_id={"depth": lax.rem(d + o, ND)},
            device_id_type=MESH,
        )
        for o in range(1, ND)
    ]
    for copy in lines:
        copy.start()
    lax.fori_loop(0, PZ, first, 0)
    halos = [halo(0)]
    for copy in halos[0]:
        copy.start()
    inside(0)
    for copy in lines:
        copy.wait_recv()
    most = max_own[...]
    for o in range(ND - 1):
        most = jnp.maximum(most, max_line[o])
    max_mid[...] = most
    planes = [
        pltpu.make_async_remote_copy(
            src_ref=max_mid,
            dst_ref=max_plane.at[k],
            send_sem=plane_send.at[k],
            recv_sem=plane_recv.at[k],
            device_id={"group": lax.rem(g + og, NG), "image": lax.rem(i + oi, NI)},
            device_id_type=MESH,
        )
        for k, (og, oi) in enumerate(PAIRS)
    ]
    pl.semaphore_wait(token, NI - 1)
    for copy in planes:
        copy.start()

    for load in loads[3:]:
        load.wait()
    pick = lax.rem(2 * lane, PY)
    low, high = index_ref[:, 0:PY], index_ref[:, PY : 2 * PY]
    half = lane < PY // 2
    bins = [
        jnp.where(half, take(low, pick + k), take(high, pick + k)) for k in range(2)
    ]
    words = []
    for c in range(4):
        pal_low = jnp.broadcast_to(palette_ref[c : c + 1, 0:PY], (8, PY))
        pal_high = jnp.broadcast_to(palette_ref[c : c + 1, PY : 2 * PY], (8, PY))
        levels = []
        for b in bins:
            spot = b & (PY - 1)
            colour = jnp.where(b < PY, take(pal_low, spot), take(pal_high, spot))
            levels.append((colour * (1.0 / STEP) + 0.5).astype(jnp.int32))
        levels.append(pltpu.roll(levels[0], PY - 1, 1))
        words.append(levels)
    for k in range(3):
        for c in range(2):
            tables[2 * k + c] = (words[c][k] - 32768) * 65536 + words[c + 2][k]

    receive_sides(0, halos[0])
    receive_planes(0, halos[0])

    def complete(z, r, at_end):
        total = completed(0, z, r, at_end)
        for c in range(5):
            tend[c, z, 8 * r : 8 * r + 8, :] = total[c]
        pack_edges(1, z, r, total)

    middle_planes(complete)
    end_planes(complete)
    halos.append(halo(1))
    for copy in halos[1]:
        copy.start()
    for copy in planes:
        copy.wait_recv()
    most = max_mid[...]
    for k in range(len(PAIRS)):
        most = jnp.maximum(most, max_plane[k])
    half_step = (0.5 * COURANT) / jnp.broadcast_to(
        jnp.max(most, axis=(0, 1), keepdims=True), (8, PY)
    )

    def section_one(z, r, at_end):
        row = TOP + 8 * r
        new = [
            u_first[c, z + 1, row : row + 8, :]
            + half_step * tend[c, z, 8 * r : 8 * r + 8, :]
            for c in range(5)
        ]
        put(1, z, r, new, primitives(new))

    def section_two(z, r, at_end):
        total = completed(1, z, r, False, within(1, z, r, True))
        row = TOP + 8 * r
        new = [
            0.75 * u_first[c, z + 1, row : row + 8, :]
            + 0.25 * (u_second[c, z + 1, row : row + 8, :] + half_step * total[c])
            for c in range(5)
        ]
        put(2, z, r, new, primitives(new))

    def section_three(z, r, at_end):
        total = completed(2, z, r, at_end)
        row = TOP + 8 * r
        rows = slice(8 * r, 8 * r + 8)
        new = [
            u_first[c, z + 1, row : row + 8, :] * (1.0 / 3.0)
            + (2.0 / 3.0) * (u_third[c, z + 1, row : row + 8, :] + half_step * total[c])
            for c in range(5)
        ]
        for c in range(5):
            fluid[c, z, rows, :] = new[c]
        inverse = 1.0 / new[0]
        kinetic = 0.5 * inverse * (new[1] * new[1] + new[2] * new[2] + new[3] * new[3])
        position = jnp.clip(new[0] - 0.5, 0.0, 1.0) * 255.0
        index = (position * 0.5).astype(jnp.int32)
        past = position - 2.0 * index.astype(jnp.float32)
        shade_index[z, rows, :] = index
        shade[0, z, rows, :] = 1.0 - jnp.minimum(past, 1.0)
        shade[1, z, rows, :] = jnp.maximum(past - 1.0, 0.0)
        shade[2, z, rows, :] = new[0] * (-2.0 * STEP / (PZ * ND))
        shade[3, z, rows, :] = (STEP * (HEAT_RATIO - 1.0)) * (new[4] - kinetic) * inverse

    middle_planes(section_one)
    end_planes(section_one)
    for copy in halos[1]:
        copy.wait_recv()
    for side in range(2):
        for c in range(5):
            x_recv[3, side, c] = x_recv[0, side, c] + half_step * x_recv[1, side, c]
        for r in range(NB):
            rows = slice(8 * r, 8 * r + 8)
            y_recv[3, side, rows, :] = (
                y_recv[0, side, rows, :] + half_step * y_recv[1, side, rows, :]
            )

    def outer_planes(r, carry):
        rows = pl.ds(pl.multiple_of(8 * r, 8), 8)
        padded = pl.ds(pl.multiple_of(TOP + 8 * r, 8), 8)
        for side, z in ((0, 0), (1, PZ + 1)):
            for c in range(5):
                u_second[c, z, padded, :] = (
                    u_first[c, z, padded, :] + half_step * tend_recv[side, c, rows, :]
                )
        return carry

    lax.fori_loop(0, NB, outer_planes, 0, unroll=2)
    receive_sides(1, None)
    receive_planes(1, None)
    halos.append(halo(2))
    end_planes(section_two)
    for copy in halos[2][:2]:
        copy.start()
    middle_planes(section_two)
    for copy in halos[2][2:]:
        copy.start()
    for copy in halos[1]:
        copy.wait_send()
    inside(2)
    receive_sides(2, halos[2])
    middle_planes(section_three)
    receive_planes(2, halos[2])
    end_planes(section_three)
    fluid_store = pltpu.make_async_copy(fluid, fluid_out, store_sem.at[0])
    fluid_store.start()

    chip, core = d // 2, lax.rem(d, 2)

    def render(t):
        rows_of = [
            jnp.broadcast_to(tables[k, pl.ds(t, 1), :], (8, PY)) for k in range(6)
        ]
        for r in range(NB):
            rows = slice(8 * r, 8 * r + 8)
            clear, light = None, None
            for z in range(PZ):
                index = shade_index[z, rows, :]
                scale = [shade[0, z, rows, :], None, shade[1, z, rows, :]]
                scale[1] = 1.0 - scale[0] - scale[2]
                looked = [None] * 4
                for k in range(3):
                    for c in range(2):
                        word = take(rows_of[2 * k + c], index)
                        upper = (word >> 16).astype(jnp.float32) * scale[k]
                        lower = (word & 65535).astype(jnp.float32) * scale[k]
                        looked[c] = upper if k == 0 else looked[c] + upper
                        looked[c + 2] = lower if k == 0 else looked[c + 2] + lower
                looked[0] = looked[0] + 32768.0
                looked[1] = looked[1] + 32768.0
                through = jnp.exp(looked[3] * shade[2, z, rows, :])
                weight = (1.0 - through) * shade[3, z, rows, :]
                if z == 0:
                    light = [weight * looked[c] for c in range(3)]
                    clear = through
                else:
                    weight = weight * clear
                    light = [light[c] + weight * looked[c] for c in range(3)]
                    clear = clear * through
            sheet[t, 0, rows, :] = clear
            for c in range(3):
                sheet[t, c + 1, rows, :] = light[c]

    def pair_copy(slot):
        return pltpu.make_async_remote_copy(
            src_ref=sheet.at[2 * slot + 1 - core],
            dst_ref=pair_recv.at[slot],
            send_sem=pair_send_sem.at[slot],
            recv_sem=pair_recv_sem.at[slot],
            device_id={"depth": 2 * chip + 1 - core},
            device_id_type=MESH,
        )

    def chip_copy(owner, source):
        return pltpu.make_async_remote_copy(
            src_ref=joined.at[owner],
            dst_ref=chip_recv.at[source],
            send_sem=chip_send_sem.at[owner],
            recv_sem=chip_recv_sem.at[source],
            device_id={"depth": 2 * owner + core},
            device_id_type=MESH,
        )

    def turn(k, carry):
        mine = (k == 3) | (k == 4) | (k == 5) | (k == 7)
        offset = jnp.where(k < 6, 1 + lax.rem(k + 1, 3), 0)
        owner = lax.rem(chip + offset, 4)
        t = 2 * owner + jnp.where(mine, core, 1 - core)
        render(t)

        @pl.when(jnp.logical_not(mine))
        def _():
            pair_copy(owner).start()

        @pl.when(mine)
        def _():
            pair_copy(owner).wait_recv()
            for r in range(NB):
                rows = slice(8 * r, 8 * r + 8)
                own_clear, other_clear = sheet[t, 0, rows, :], pair_recv[owner, 0, rows, :]
                own_scale = jnp.where(core == 0, 1.0, other_clear)
                other_scale = jnp.where(core == 0, own_clear, 1.0)
                joined[owner, 0, rows, :] = own_clear * other_clear
                for c in range(1, 4):
                    joined[owner, c, rows, :] = (
                        own_scale * sheet[t, c, rows, :]
                        + other_scale * pair_recv[owner, c, rows, :]
                    )

        @pl.when(mine & (k < 6))
        def _():
            chip_copy(owner, chip).start()

        return carry

    lax.fori_loop(0, 8, turn, 0)
    for o in (1, 3, 2):
        source = lax.rem(chip + o, 4)
        chip_copy(source, source).wait_recv()
    chip_recv[chip] = joined[chip]
    ahead = chip_recv[0, 0]
    light = [chip_recv[0, c] for c in range(1, 4)]
    for k in range(1, 4):
        for c in range(3):
            light[c] = light[c] + ahead * chip_recv[k, c + 1]
        if k < 3:
            ahead = ahead * chip_recv[k, 0]
    for c in range(3):
        picture[c] = light[c]
    picture_store = pltpu.make_async_copy(picture, picture_out, store_sem.at[1])
    picture_store.start()

    for copy in lines + planes + halos[0] + halos[2]:
        copy.wait_send()
    for k in range(4):
        pair_copy(k).wait_send()
    for o in range(1, 4):
        source = lax.rem(chip + o, 4)
        chip_copy(source, source).wait_send()
    fluid_store.wait()
    picture_store.wait()


def shards(density, velocity, pressure, palette, palette_index):
    f32 = jnp.float32
    any_space = pl.BlockSpec(memory_space=pl.ANY)
    padded = (5, PZ + 2, PX + 16, PY)
    dma = pltpu.SemaphoreType.DMA
    fluid_state, picture = pl.pallas_call(
        kernel,
        out_shape=(
            jax.ShapeDtypeStruct((5, PZ, PX, PY), f32),
            jax.ShapeDtypeStruct((3, PX, PY), f32),
        ),
        in_specs=[any_space] * 5,
        out_specs=(any_space, any_space),
        scratch_shapes=[
            pltpu.VMEM((5, PZ, PX, PY), f32),
            pltpu.VMEM((4, 2 * PY), f32),
            pltpu.VMEM((8, 2 * PY), jnp.int32),
            pltpu.VMEM(padded, f32),
            pltpu.VMEM(padded, f32),
            pltpu.VMEM(padded, f32),
            pltpu.VMEM(padded, f32),
            pltpu.VMEM(padded, f32),
            pltpu.VMEM((5, PZ, PX, PY), f32),
            pltpu.VMEM((2, 5, PX, PY), f32),
            pltpu.VMEM((4, 2, 5, PZ, PY), f32),
            pltpu.VMEM((4, 2, 5, PZ, PY), f32),
            pltpu.VMEM((4, PX, PY), f32),
            pltpu.VMEM((4, 2, PX, PY), f32),
            pltpu.VMEM((2, 5, PZ, PY), f32),
            pltpu.VMEM((5, PX, PY), f32),
            pltpu.VMEM((8, PY), f32),
            pltpu.VMEM((ND - 1, 8, PY), f32),
            pltpu.VMEM((8, PY), f32),
            pltpu.VMEM((len(PAIRS), 8, PY), f32),
            pltpu.VMEM((5, PZ, PX, PY), f32),
            pltpu.VMEM((4, PZ, PX, PY), f32),
            pltpu.VMEM((PZ, PX, PY), jnp.int32),
            pltpu.VMEM((6, 8, PY), jnp.int32),
            pltpu.VMEM((8, 4, PX, PY), f32),
            pltpu.VMEM((4, 4, PX, PY), f32),
            pltpu.VMEM((4, 4, PX, PY), f32),
            pltpu.VMEM((4, 4, PX, PY), f32),
            pltpu.VMEM((3, PX, PY), f32),
            dma((5,)),
            dma((2,)),
            dma((3, 6)),
            dma((3, 6)),
            dma((ND - 1,)),
            dma((ND - 1,)),
            dma((len(PAIRS),)),
            dma((len(PAIRS),)),
            pltpu.SemaphoreType.REGULAR,
            dma((4,)),
            dma((4,)),
            dma((4,)),
            dma((4,)),
        ],
        compiler_params=pltpu.CompilerParams(
            collective_id=0, has_side_effects=True, vmem_limit_bytes=60 * 1024 * 1024
        ),
    )(density, velocity, pressure, palette, palette_index)
    return fluid_state, picture[None]


def solution(mesh):
    return jax.shard_map(
        shards,
        mesh=mesh,
        in_specs=(
            P("depth", "group", "image"),
            P(None, "depth", "group", "image"),
            P("depth", "group", "image"),
            P(),
            P(),
        ),
        out_specs=(P(None, "depth", "group", "image"), P("depth", None, "group", "image")),
        check_vma=False,
    )
```

```python
import jax
import jax.numpy as jnp
from jax import lax
from jax.experimental import pallas as pl
from jax.experimental.pallas import tpu as pltpu
from jax.sharding import PartitionSpec as P

MESH = pl.DeviceIdType.MESH
HEAT_RATIO = 1.4
COURANT = 0.8
NG, ND, NI = 4, 8, 4
PZ, PX, PY = 8, 48, 128
NB = PX // 8
TOP = 8
STEP = 2.0 / 65535.0
PAIRS = [(g, i) for g in range(NG) for i in range(NI) if (g, i) != (0, 0)]


def take(table, index):
    return jnp.take_along_axis(table, index, axis=1, mode="promise_in_bounds")


def primitives(state):
    inverse = 1.0 / state[0]
    u, v, w = state[1] * inverse, state[2] * inverse, state[3] * inverse
    kinetic = 0.5 * (state[1] * u + state[2] * v + state[3] * w)
    p = (HEAT_RATIO - 1.0) * (state[4] - kinetic)
    return [u, v, w, p, jnp.sqrt(HEAT_RATIO * p * inverse)]


def flux(state, q, p, component):
    rows = [state[0] * q, state[1] * q, state[2] * q, state[3] * q, (state[4] + p) * q]
    rows[component] = rows[component] + p
    return rows


def kernel(
    density_in,
    velocity_in,
    pressure_in,
    palette_in,
    index_in,
    fluid_out,
    picture_out,
    raw,
    palette_ref,
    index_ref,
    u_first,
    u_second,
    u_third,
    prim_a,
    prim_b,
    tend,
    tend_recv,
    x_send,
    x_recv,
    y_send,
    y_recv,
    x_part,
    y_part,
    max_own,
    max_line,
    max_mid,
    max_plane,
    fluid,
    shade,
    shade_index,
    tables,
    sheet,
    pair_recv,
    joined,
    chip_recv,
    picture,
    load_sem,
    store_sem,
    halo_send,
    halo_recv,
    line_send,
    line_recv,
    plane_send,
    plane_recv,
    token,
    pair_send_sem,
    pair_recv_sem,
    chip_send_sem,
    chip_recv_sem,
):
    g, d, i = lax.axis_index("group"), lax.axis_index("depth"), lax.axis_index("image")
    states = [u_first, u_second, u_third]
    prims = [prim_a, prim_b, prim_a]

    loads = [
        pltpu.make_async_copy(density_in, raw.at[0], load_sem.at[0]),
        pltpu.make_async_copy(velocity_in, raw.at[pl.ds(1, 3)], load_sem.at[1]),
        pltpu.make_async_copy(pressure_in, raw.at[4], load_sem.at[2]),
        pltpu.make_async_copy(palette_in, palette_ref, load_sem.at[3]),
        pltpu.make_async_copy(index_in, index_ref, load_sem.at[4]),
    ]
    for load in loads:
        load.start()

    barrier = pltpu.get_barrier_semaphore()
    for o in range(1, ND):
        pl.semaphore_signal(
            barrier, inc=1, device_id={"depth": lax.rem(d + o, ND)}, device_id_type=MESH
        )
    for o in range(1, NG):
        pl.semaphore_signal(
            barrier, inc=1, device_id={"group": lax.rem(g + o, NG)}, device_id_type=MESH
        )
    for o in range(1, NI):
        pl.semaphore_signal(
            barrier, inc=1, device_id={"image": lax.rem(i + o, NI)}, device_id_type=MESH
        )

    lane = lax.broadcasted_iota(jnp.int32, (8, PY), 1)
    even = lax.rem(lane, 2) == 0
    at_first = lane == 0
    at_last = lane == PY - 1

    def pack_edges(s, z, r, new):
        rows = pl.ds(8 * r, 8)
        for c in range(5):
            shift = 16 * c + 2 * z
            turned = pltpu.roll(new[c], shift, 1)
            low = lax.rem(shift + PY - 1, PY)
            pltpu.store(
                y_send.at[s, rows, :], turned, mask=(lane == shift) | (lane == low)
            )
            if r == 0:
                x_send[s, 0, c, pl.ds(z, 1), :] = new[c][0:1]
            if r == NB - 1:
                x_send[s, 1, c, pl.ds(z, 1), :] = new[c][7:8]

    def put(s, z, r, new, derived):
        rows = pl.ds(TOP + 8 * r, 8)
        for c in range(5):
            states[s][c, z + 1, rows, :] = new[c]
            prims[s][c, z + 1, rows, :] = derived[c]
        pack_edges(3 if s == 1 else s, z, r, new)

    def halo(s):
        up_d, down_d = lax.rem(d + 1, ND), lax.rem(d + ND - 1, ND)
        up_g, down_g = lax.rem(g + 1, NG), lax.rem(g + NG - 1, NG)
        up_i, down_i = lax.rem(i + 1, NI), lax.rem(i + NI - 1, NI)
        rows = pl.ds(TOP, PX)
        if s == 1:
            below, above = tend.at[:, 0], tend.at[:, PZ - 1]
            to_above, to_below = tend_recv.at[1], tend_recv.at[0]
        else:
            state = states[s]
            below, above = state.at[:, 1, rows, :], state.at[:, PZ, rows, :]
            to_above, to_below = state.at[:, PZ + 1, rows, :], state.at[:, 0, rows, :]
        plan = [
            (below, to_above, {"depth": down_d}),
            (above, to_below, {"depth": up_d}),
            (y_send.at[s], y_recv.at[s, 1], {"image": down_i}),
            (y_send.at[s], y_recv.at[s, 0], {"image": up_i}),
            (x_send.at[s, 0], x_recv.at[s, 1], {"group": down_g}),
            (x_send.at[s, 1], x_recv.at[s, 0], {"group": up_g}),
        ]
        return [
            pltpu.make_async_remote_copy(
                src_ref=src,
                dst_ref=dst,
                send_sem=halo_send.at[s, k],
                recv_sem=halo_recv.at[s, k],
                device_id=device,
                device_id_type=MESH,
            )
            for k, (src, dst, device) in enumerate(plan)
        ]

    row_of = lax.broadcasted_iota(jnp.int32, (8, PY), 0)
    at_top, at_bottom = row_of == 0, row_of == 7

    def from_outside(inner, outer, component, sign):
        prim_in, prim_out = primitives(inner), primitives(outer)
        fastest = jnp.maximum(
            jnp.abs(prim_in[component - 1]) + prim_in[4],
            jnp.abs(prim_out[component - 1]) + prim_out[4],
        )
        flows = flux(outer, prim_out[component - 1], prim_out[3], component)
        return [sign(flows[c]) + fastest * (outer[c] - inner[c]) for c in range(5)]

    def receive_sides(s, copies):
        s = 3 if s == 1 else s
        if copies is not None:
            copies[4].wait_recv()
            copies[5].wait_recv()
        for side, wall in ((0, g == 0), (1, g == NG - 1)):
            own = [x_send[s, side, c] for c in range(5)]
            near = [
                jnp.where(wall, -own[c] if c == 1 else own[c], x_recv[s, side, c])
                for c in range(5)
            ]
            parts = from_outside(own, near, 1, (lambda f: f) if side == 0 else (lambda f: -f))
            for c in range(5):
                x_part[side, c] = parts[c]
        if copies is not None:
            copies[2].wait_recv()
            copies[3].wait_recv()

        def edge(r, carry):
            rows = pl.ds(pl.multiple_of(8 * r, 8), 8)
            own, left, right = y_send[s, rows, :], y_recv[s, 0, rows, :], y_recv[s, 1, rows, :]
            inner, outer = [], []
            for c in range(5):
                inner.append(pltpu.roll(own, (PY - 16 * c) % PY, 1))
                outer.append(
                    jnp.where(
                        even,
                        pltpu.roll(left, (PY + 1 - 16 * c) % PY, 1),
                        pltpu.roll(right, (PY - 1 - 16 * c) % PY, 1),
                    )
                )
            parts = from_outside(inner, outer, 2, lambda f: jnp.where(even, f, -f))
            for c in range(5):
                y_part[c, rows, :] = parts[c]
            return carry

        lax.fori_loop(0, NB, edge, 0, unroll=2)

    def receive_planes(s, copies):
        state, derived = states[s], prims[s]
        if copies is not None:
            copies[0].wait_recv()
            copies[1].wait_recv()

        def plane(r, carry):
            rows = pl.ds(pl.multiple_of(TOP + 8 * r, 8), 8)
            for z in (0, PZ + 1):
                values = primitives([state[c, z, rows, :] for c in range(5)])
                for c in range(5):
                    derived[c, z, rows, :] = values[c]
            return carry

        lax.fori_loop(0, NB, plane, 0, unroll=2)

    def add(total, parts):
        return parts if total is None else [t + p for t, p in zip(total, parts)]

    def along_z(s, z, row, cell, prim, total):
        state, derived = states[s], prims[s]
        here = jnp.abs(prim[2]) + prim[4]
        for side in (-1, 1):
            zz = z + 1 + side
            near = [state[c, zz, row : row + 8, :] for c in range(5)]
            q, p = derived[2, zz, row : row + 8, :], derived[3, zz, row : row + 8, :]
            fastest = jnp.maximum(here, jnp.abs(q) + derived[4, zz, row : row + 8, :])
            flows = flux(near, q, p, 3)
            parts = [fastest * (near[c] - cell[c]) for c in range(5)]
            parts = [a + f if side < 0 else a - f for a, f in zip(parts, flows)]
            total = add(total, parts)
        return total

    def centre(s, z, row):
        cell = [states[s][c, z + 1, row : row + 8, :] for c in range(5)]
        return cell, [prims[s][c, z + 1, row : row + 8, :] for c in range(5)]

    def within(s, z, r, with_z):
        state, derived = states[s], prims[s]
        row = TOP + 8 * r
        cell, prim = centre(s, z, row)
        total = along_z(s, z, row, cell, prim, None) if with_z else None
        here = jnp.abs(prim[0]) + prim[4]
        for side in (-1, 1):
            rr = row + side
            near = [state[c, z + 1, rr : rr + 8, :] for c in range(5)]
            q, p = derived[0, z + 1, rr : rr + 8, :], derived[3, z + 1, rr : rr + 8, :]
            fastest = jnp.maximum(here, jnp.abs(q) + derived[4, z + 1, rr : rr + 8, :])
            flows = flux(near, q, p, 1)
            parts = [fastest * (near[c] - cell[c]) for c in range(5)]
            parts = [a + f if side < 0 else a - f for a, f in zip(parts, flows)]
            if side < 0 and r == 0:
                parts = [jnp.where(at_top, 0.0, a) for a in parts]
            if side > 0 and r == NB - 1:
                parts = [jnp.where(at_bottom, 0.0, a) for a in parts]
            total = add(total, parts)
        here = jnp.abs(prim[1]) + prim[4]
        for side in (-1, 1):
            shift = 1 if side < 0 else PY - 1
            near = [pltpu.roll(cell[c], shift, 1) for c in range(5)]
            q, p = pltpu.roll(prim[1], shift, 1), pltpu.roll(prim[3], shift, 1)
            fastest = jnp.maximum(here, pltpu.roll(here, shift, 1))
            flows = flux(near, q, p, 2)
            parts = [fastest * (near[c] - cell[c]) for c in range(5)]
            parts = [a + f if side < 0 else a - f for a, f in zip(parts, flows)]
            outside = at_first if side < 0 else at_last
            total = add(total, [jnp.where(outside, 0.0, a) for a in parts])
        return total

    def completed(s, z, r, with_z, total=None):
        rows = slice(8 * r, 8 * r + 8)
        if total is None:
            total = [tend[c, z, rows, :] for c in range(5)]
        turn = lax.rem(PY - 2 * z, PY)
        for c in range(5):
            edges = pltpu.roll(y_part[c, rows, :], turn, 1)
            total[c] = total[c] + jnp.where(at_first | at_last, edges, 0.0)
        for side, block, place in ((0, 0, at_top), (1, NB - 1, at_bottom)):
            if r == block:
                for c in range(5):
                    line = jnp.broadcast_to(x_part[side, c, pl.ds(z, 1), :], (8, PY))
                    total[c] = total[c] + jnp.where(place, line, 0.0)
        if with_z:
            row = TOP + 8 * r
            cell, prim = centre(s, z, row)
            total = along_z(s, z, row, cell, prim, total)
        return total

    def middle_planes(visit):
        def one(z, carry):
            for r in range(NB):
                visit(z, r, False)
            return carry

        lax.fori_loop(1, PZ - 1, one, 0)

    def all_planes(visit):
        def one(z, carry):
            for r in range(NB):
                visit(z, r, False)
            return carry

        lax.fori_loop(0, PZ, one, 0, unroll=2)

    def end_planes(visit):
        def one(k, carry):
            for r in range(NB):
                visit((PZ - 1) * k, r, True)
            return carry

        lax.fori_loop(0, 2, one, 0)

    def inside(s):
        def visit(z, r, at_end):
            total = within(s, z, r, not at_end)
            for c in range(5):
                tend[c, z, 8 * r : 8 * r + 8, :] = total[c]

        middle_planes(visit)
        end_planes(visit)

    for load in loads[:3]:
        load.wait()

    def signals(z, most):
        for r in range(NB):
            rho, u, v, w, p = [raw[c, z, 8 * r : 8 * r + 8, :] for c in range(5)]
            sound = jnp.sqrt(HEAT_RATIO * p / rho)
            prims[0][4, z + 1, TOP + 8 * r : TOP + 8 * r + 8, :] = sound
            most = jnp.maximum(most, jnp.abs(u) + jnp.abs(v) + jnp.abs(w) + 3.0 * sound)
        return most

    max_own[...] = lax.fori_loop(0, PZ, signals, jnp.zeros((8, PY), jnp.float32), unroll=2)

    def first(z, carry):
        for r in range(NB):
            rho, u, v, w, p = [raw[c, z, 8 * r : 8 * r + 8, :] for c in range(5)]
            energy = p / (HEAT_RATIO - 1.0) + 0.5 * rho * (u * u + v * v + w * w)
            sound = prims[0][4, z + 1, TOP + 8 * r : TOP + 8 * r + 8, :]
            put(0, z, r, [rho, rho * u, rho * v, rho * w, energy], [u, v, w, p, sound])
        return carry

    pl.semaphore_wait(barrier, ND + NG + NI - 3)

    for o in range(1, NI):
        pl.semaphore_signal(
            token, inc=1, device_id={"image": lax.rem(i + o, NI)}, device_id_type=MESH
        )
    lines = [
        pltpu.make_async_remote_copy(
            src_ref=max_own,
            dst_ref=max_line.at[o - 1],
            send_sem=line_send.at[o - 1],
            recv_sem=line_recv.at[o - 1],
            device_id={"depth": lax.rem(d + o, ND)},
            device_id_type=MESH,
        )
        for o in range(1, ND)
    ]
    for copy in lines:
        copy.start()
    lax.fori_loop(0, PZ, first, 0)
    halos = [halo(0)]
    for copy in halos[0]:
        copy.start()
    inside(0)
    for copy in lines:
        copy.wait_recv()
    most = max_own[...]
    for o in range(ND - 1):
        most = jnp.maximum(most, max_line[o])
    max_mid[...] = most
    planes = [
        pltpu.make_async_remote_copy(
            src_ref=max_mid,
            dst_ref=max_plane.at[k],
            send_sem=plane_send.at[k],
            recv_sem=plane_recv.at[k],
            device_id={"group": lax.rem(g + og, NG), "image": lax.rem(i + oi, NI)},
            device_id_type=MESH,
        )
        for k, (og, oi) in enumerate(PAIRS)
    ]
    pl.semaphore_wait(token, NI - 1)
    for copy in planes:
        copy.start()

    receive_sides(0, halos[0])
    receive_planes(0, halos[0])

    def complete(z, r, at_end):
        total = completed(0, z, r, at_end)
        for c in range(5):
            tend[c, z, 8 * r : 8 * r + 8, :] = total[c]
        pack_edges(1, z, r, total)

    halos.append(halo(1))
    end_planes(complete)
    for copy in halos[1][:2]:
        copy.start()
    middle_planes(complete)
    for copy in halos[1][2:]:
        copy.start()

    for load in loads[3:]:
        load.wait()
    pick = lax.rem(2 * lane, PY)
    low, high = index_ref[:, 0:PY], index_ref[:, PY : 2 * PY]
    half = lane < PY // 2
    bins = [
        jnp.where(half, take(low, pick + k), take(high, pick + k)) for k in range(2)
    ]
    words = []
    for c in range(4):
        pal_low = jnp.broadcast_to(palette_ref[c : c + 1, 0:PY], (8, PY))
        pal_high = jnp.broadcast_to(palette_ref[c : c + 1, PY : 2 * PY], (8, PY))
        levels = []
        for b in bins:
            spot = b & (PY - 1)
            colour = jnp.where(b < PY, take(pal_low, spot), take(pal_high, spot))
            levels.append((colour * (1.0 / STEP) + 0.5).astype(jnp.int32))
        levels.append(pltpu.roll(levels[0], PY - 1, 1))
        words.append(levels)
    for k in range(3):
        for c in range(2):
            tables[2 * k + c] = (words[c][k] - 32768) * 65536 + words[c + 2][k]
    for copy in planes:
        copy.wait_recv()
    most = max_mid[...]
    for k in range(len(PAIRS)):
        most = jnp.maximum(most, max_plane[k])
    half_step = (0.5 * COURANT) / jnp.broadcast_to(
        jnp.max(most, axis=(0, 1), keepdims=True), (8, PY)
    )

    def section_one(z, r, at_end):
        row = TOP + 8 * r
        new = [
            u_first[c, z + 1, row : row + 8, :]
            + half_step * tend[c, z, 8 * r : 8 * r + 8, :]
            for c in range(5)
        ]
        put(1, z, r, new, primitives(new))

    def section_two(z, r, at_end):
        total = completed(1, z, r, False, within(1, z, r, True))
        row = TOP + 8 * r
        new = [
            0.75 * u_first[c, z + 1, row : row + 8, :]
            + 0.25 * (u_second[c, z + 1, row : row + 8, :] + half_step * total[c])
            for c in range(5)
        ]
        put(2, z, r, new, primitives(new))

    def section_three(z, r, at_end):
        total = completed(2, z, r, False)
        row = TOP + 8 * r
        rows = slice(8 * r, 8 * r + 8)
        new = [
            u_first[c, z + 1, row : row + 8, :] * (1.0 / 3.0)
            + (2.0 / 3.0) * (u_third[c, z + 1, row : row + 8, :] + half_step * total[c])
            for c in range(5)
        ]
        for c in range(5):
            fluid[c, z, rows, :] = new[c]
        inverse = 1.0 / new[0]
        kinetic = 0.5 * inverse * (new[1] * new[1] + new[2] * new[2] + new[3] * new[3])
        position = jnp.clip(new[0] - 0.5, 0.0, 1.0) * 255.0
        index = (position * 0.5).astype(jnp.int32)
        past = position - 2.0 * index.astype(jnp.float32)
        shade_index[z, rows, :] = index
        shade[0, z, rows, :] = 1.0 - jnp.minimum(past, 1.0)
        shade[1, z, rows, :] = jnp.maximum(past - 1.0, 0.0)
        shade[2, z, rows, :] = new[0] * (-2.0 * STEP / (PZ * ND))
        shade[3, z, rows, :] = (STEP * (HEAT_RATIO - 1.0)) * (new[4] - kinetic) * inverse

    all_planes(section_one)
    for copy in halos[1]:
        copy.wait_recv()
    for side in range(2):
        for c in range(5):
            x_recv[3, side, c] = x_recv[0, side, c] + half_step * x_recv[1, side, c]
        for r in range(NB):
            rows = slice(8 * r, 8 * r + 8)
            y_recv[3, side, rows, :] = (
                y_recv[0, side, rows, :] + half_step * y_recv[1, side, rows, :]
            )

    def outer_planes(r, carry):
        rows = pl.ds(pl.multiple_of(8 * r, 8), 8)
        padded = pl.ds(pl.multiple_of(TOP + 8 * r, 8), 8)
        for side, z in ((0, 0), (1, PZ + 1)):
            for c in range(5):
                u_second[c, z, padded, :] = (
                    u_first[c, z, padded, :] + half_step * tend_recv[side, c, rows, :]
                )
        return carry

    lax.fori_loop(0, NB, outer_planes, 0, unroll=2)
    receive_sides(1, None)
    receive_planes(1, None)
    halos.append(halo(2))
    end_planes(section_two)
    for copy in halos[2][:2]:
        copy.start()
    middle_planes(section_two)
    for copy in halos[2][2:]:
        copy.start()
    for copy in halos[1]:
        copy.wait_send()
    inside(2)
    receive_planes(2, halos[2])

    def with_planes(z, r, at_end):
        row = TOP + 8 * r
        total = along_z(2, z, row, *centre(2, z, row), [tend[c, z, 8 * r : 8 * r + 8, :] for c in range(5)])
        for c in range(5):
            tend[c, z, 8 * r : 8 * r + 8, :] = total[c]

    end_planes(with_planes)
    receive_sides(2, halos[2])
    all_planes(section_three)
    fluid_store = pltpu.make_async_copy(fluid, fluid_out, store_sem.at[0])
    fluid_store.start()

    chip, core = d // 2, lax.rem(d, 2)

    def render(t):
        rows_of = [
            jnp.broadcast_to(tables[k, pl.ds(t, 1), :], (8, PY)) for k in range(6)
        ]
        for r in range(NB):
            rows = slice(8 * r, 8 * r + 8)
            clear, light = None, None
            for z in range(PZ):
                index = shade_index[z, rows, :]
                scale = [shade[0, z, rows, :], None, shade[1, z, rows, :]]
                scale[1] = 1.0 - scale[0] - scale[2]
                looked = [None] * 4
                for k in range(3):
                    for c in range(2):
                        word = take(rows_of[2 * k + c], index)
                        upper = (word >> 16).astype(jnp.float32) * scale[k]
                        lower = (word & 65535).astype(jnp.float32) * scale[k]
                        looked[c] = upper if k == 0 else looked[c] + upper
                        looked[c + 2] = lower if k == 0 else looked[c + 2] + lower
                looked[0] = looked[0] + 32768.0
                looked[1] = looked[1] + 32768.0
                through = jnp.exp(looked[3] * shade[2, z, rows, :])
                weight = (1.0 - through) * shade[3, z, rows, :]
                if z == 0:
                    light = [weight * looked[c] for c in range(3)]
                    clear = through
                else:
                    weight = weight * clear
                    light = [light[c] + weight * looked[c] for c in range(3)]
                    clear = clear * through
            sheet[t, 0, rows, :] = clear
            for c in range(3):
                sheet[t, c + 1, rows, :] = light[c]

    def pair_copy(slot):
        return pltpu.make_async_remote_copy(
            src_ref=sheet.at[2 * slot + 1 - core],
            dst_ref=pair_recv.at[slot],
            send_sem=pair_send_sem.at[slot],
            recv_sem=pair_recv_sem.at[slot],
            device_id={"depth": 2 * chip + 1 - core},
            device_id_type=MESH,
        )

    def chip_copy(owner, source):
        return pltpu.make_async_remote_copy(
            src_ref=joined.at[owner],
            dst_ref=chip_recv.at[source],
            send_sem=chip_send_sem.at[owner],
            recv_sem=chip_recv_sem.at[source],
            device_id={"depth": 2 * owner + core},
            device_id_type=MESH,
        )

    def turn(k, carry):
        mine = (k == 3) | (k == 4) | (k == 5) | (k == 7)
        offset = jnp.where(k < 6, 1 + lax.rem(k + 1, 3), 0)
        owner = lax.rem(chip + offset, 4)
        t = 2 * owner + jnp.where(mine, core, 1 - core)
        render(t)

        @pl.when(jnp.logical_not(mine))
        def _():
            pair_copy(owner).start()

        @pl.when(mine)
        def _():
            pair_copy(owner).wait_recv()
            for r in range(NB):
                rows = slice(8 * r, 8 * r + 8)
                own_clear, other_clear = sheet[t, 0, rows, :], pair_recv[owner, 0, rows, :]
                own_scale = jnp.where(core == 0, 1.0, other_clear)
                other_scale = jnp.where(core == 0, own_clear, 1.0)
                joined[owner, 0, rows, :] = own_clear * other_clear
                for c in range(1, 4):
                    joined[owner, c, rows, :] = (
                        own_scale * sheet[t, c, rows, :]
                        + other_scale * pair_recv[owner, c, rows, :]
                    )

        @pl.when(mine & (k < 6))
        def _():
            chip_copy(owner, chip).start()

        return carry

    lax.fori_loop(0, 8, turn, 0)
    for o in (1, 3, 2):
        source = lax.rem(chip + o, 4)
        chip_copy(source, source).wait_recv()
    chip_recv[chip] = joined[chip]
    ahead = chip_recv[0, 0]
    light = [chip_recv[0, c] for c in range(1, 4)]
    for k in range(1, 4):
        for c in range(3):
            light[c] = light[c] + ahead * chip_recv[k, c + 1]
        if k < 3:
            ahead = ahead * chip_recv[k, 0]
    for c in range(3):
        picture[c] = light[c]
    picture_store = pltpu.make_async_copy(picture, picture_out, store_sem.at[1])
    picture_store.start()

    for copy in lines + planes + halos[0] + halos[2]:
        copy.wait_send()
    for k in range(4):
        pair_copy(k).wait_send()
    for o in range(1, 4):
        source = lax.rem(chip + o, 4)
        chip_copy(source, source).wait_send()
    fluid_store.wait()
    picture_store.wait()


def shards(density, velocity, pressure, palette, palette_index):
    f32 = jnp.float32
    any_space = pl.BlockSpec(memory_space=pl.ANY)
    padded = (5, PZ + 2, PX + 16, PY)
    dma = pltpu.SemaphoreType.DMA
    fluid_state, picture = pl.pallas_call(
        kernel,
        out_shape=(
            jax.ShapeDtypeStruct((5, PZ, PX, PY), f32),
            jax.ShapeDtypeStruct((3, PX, PY), f32),
        ),
        in_specs=[any_space] * 5,
        out_specs=(any_space, any_space),
        scratch_shapes=[
            pltpu.VMEM((5, PZ, PX, PY), f32),
            pltpu.VMEM((4, 2 * PY), f32),
            pltpu.VMEM((8, 2 * PY), jnp.int32),
            pltpu.VMEM(padded, f32),
            pltpu.VMEM(padded, f32),
            pltpu.VMEM(padded, f32),
            pltpu.VMEM(padded, f32),
            pltpu.VMEM(padded, f32),
            pltpu.VMEM((5, PZ, PX, PY), f32),
            pltpu.VMEM((2, 5, PX, PY), f32),
            pltpu.VMEM((4, 2, 5, PZ, PY), f32),
            pltpu.VMEM((4, 2, 5, PZ, PY), f32),
            pltpu.VMEM((4, PX, PY), f32),
            pltpu.VMEM((4, 2, PX, PY), f32),
            pltpu.VMEM((2, 5, PZ, PY), f32),
            pltpu.VMEM((5, PX, PY), f32),
            pltpu.VMEM((8, PY), f32),
            pltpu.VMEM((ND - 1, 8, PY), f32),
            pltpu.VMEM((8, PY), f32),
            pltpu.VMEM((len(PAIRS), 8, PY), f32),
            pltpu.VMEM((5, PZ, PX, PY), f32),
            pltpu.VMEM((4, PZ, PX, PY), f32),
            pltpu.VMEM((PZ, PX, PY), jnp.int32),
            pltpu.VMEM((6, 8, PY), jnp.int32),
            pltpu.VMEM((8, 4, PX, PY), f32),
            pltpu.VMEM((4, 4, PX, PY), f32),
            pltpu.VMEM((4, 4, PX, PY), f32),
            pltpu.VMEM((4, 4, PX, PY), f32),
            pltpu.VMEM((3, PX, PY), f32),
            dma((5,)),
            dma((2,)),
            dma((3, 6)),
            dma((3, 6)),
            dma((ND - 1,)),
            dma((ND - 1,)),
            dma((len(PAIRS),)),
            dma((len(PAIRS),)),
            pltpu.SemaphoreType.REGULAR,
            dma((4,)),
            dma((4,)),
            dma((4,)),
            dma((4,)),
        ],
        compiler_params=pltpu.CompilerParams(
            collective_id=0, has_side_effects=True, vmem_limit_bytes=60 * 1024 * 1024
        ),
    )(density, velocity, pressure, palette, palette_index)
    return fluid_state, picture[None]


def solution(mesh):
    return jax.shard_map(
        shards,
        mesh=mesh,
        in_specs=(
            P("depth", "group", "image"),
            P(None, "depth", "group", "image"),
            P("depth", "group", "image"),
            P(),
            P(),
        ),
        out_specs=(P(None, "depth", "group", "image"), P("depth", None, "group", "image")),
        check_vma=False,
    )
```

```python
import jax
import jax.numpy as jnp
from jax import lax
from jax.experimental import pallas as pl
from jax.experimental.pallas import tpu as pltpu
from jax.sharding import PartitionSpec as P

MESH = pl.DeviceIdType.MESH
HEAT_RATIO = 1.4
COURANT = 0.8
NG, ND, NI = 4, 8, 4
PZ, PX, PY = 8, 48, 128
NB = PX // 8
TOP = 8
STEP = 2.0 / 65535.0
PAIRS = [(g, i) for g in range(NG) for i in range(NI) if (g, i) != (0, 0)]


def take(table, index):
    return jnp.take_along_axis(table, index, axis=1, mode="promise_in_bounds")


def primitives(state):
    inverse = 1.0 / state[0]
    u, v, w = state[1] * inverse, state[2] * inverse, state[3] * inverse
    kinetic = 0.5 * (state[1] * u + state[2] * v + state[3] * w)
    p = (HEAT_RATIO - 1.0) * (state[4] - kinetic)
    return [u, v, w, p, jnp.sqrt(HEAT_RATIO * p * inverse)]


def flux(state, q, p, component):
    rows = [state[0] * q, state[1] * q, state[2] * q, state[3] * q, (state[4] + p) * q]
    rows[component] = rows[component] + p
    return rows


def kernel(
    density_in,
    velocity_in,
    pressure_in,
    palette_in,
    index_in,
    fluid_out,
    picture_out,
    raw,
    palette_ref,
    index_ref,
    u_first,
    u_second,
    u_third,
    prim_a,
    prim_b,
    tend,
    tend_recv,
    x_send,
    x_recv,
    y_send,
    y_recv,
    x_part,
    y_part,
    max_own,
    max_line,
    max_mid,
    max_plane,
    fluid,
    shade,
    shade_index,
    tables,
    sheet,
    pair_recv,
    joined,
    chip_recv,
    picture,
    load_sem,
    store_sem,
    halo_send,
    halo_recv,
    line_send,
    line_recv,
    plane_send,
    plane_recv,
    token,
    pair_send_sem,
    pair_recv_sem,
    chip_send_sem,
    chip_recv_sem,
):
    g, d, i = lax.axis_index("group"), lax.axis_index("depth"), lax.axis_index("image")
    states = [u_first, u_second, u_third]
    prims = [prim_a, prim_b, prim_a]

    loads = [
        pltpu.make_async_copy(density_in, raw.at[0], load_sem.at[0]),
        pltpu.make_async_copy(velocity_in, raw.at[pl.ds(1, 3)], load_sem.at[1]),
        pltpu.make_async_copy(pressure_in, raw.at[4], load_sem.at[2]),
        pltpu.make_async_copy(palette_in, palette_ref, load_sem.at[3]),
        pltpu.make_async_copy(index_in, index_ref, load_sem.at[4]),
    ]
    for load in loads:
        load.start()

    barrier = pltpu.get_barrier_semaphore()
    for o in range(1, ND):
        pl.semaphore_signal(
            barrier, inc=1, device_id={"depth": lax.rem(d + o, ND)}, device_id_type=MESH
        )
    for o in range(1, NG):
        pl.semaphore_signal(
            barrier, inc=1, device_id={"group": lax.rem(g + o, NG)}, device_id_type=MESH
        )
    for o in range(1, NI):
        pl.semaphore_signal(
            barrier, inc=1, device_id={"image": lax.rem(i + o, NI)}, device_id_type=MESH
        )

    lane = lax.broadcasted_iota(jnp.int32, (8, PY), 1)
    even = lax.rem(lane, 2) == 0
    at_first = lane == 0
    at_last = lane == PY - 1

    def pack_edges(s, z, r, new):
        rows = pl.ds(8 * r, 8)
        for c in range(5):
            shift = 16 * c + 2 * z
            turned = pltpu.roll(new[c], shift, 1)
            low = lax.rem(shift + PY - 1, PY)
            pltpu.store(
                y_send.at[s, rows, :], turned, mask=(lane == shift) | (lane == low)
            )
            if r == 0:
                x_send[s, 0, c, pl.ds(z, 1), :] = new[c][0:1]
            if r == NB - 1:
                x_send[s, 1, c, pl.ds(z, 1), :] = new[c][7:8]

    def put(s, z, r, new, derived):
        rows = pl.ds(TOP + 8 * r, 8)
        for c in range(5):
            states[s][c, z + 1, rows, :] = new[c]
            prims[s][c, z + 1, rows, :] = derived[c]
        pack_edges(3 if s == 1 else s, z, r, new)

    def halo(s):
        up_d, down_d = lax.rem(d + 1, ND), lax.rem(d + ND - 1, ND)
        up_g, down_g = lax.rem(g + 1, NG), lax.rem(g + NG - 1, NG)
        up_i, down_i = lax.rem(i + 1, NI), lax.rem(i + NI - 1, NI)
        rows = pl.ds(TOP, PX)
        if s == 1:
            below, above = tend.at[:, 0], tend.at[:, PZ - 1]
            to_above, to_below = tend_recv.at[1], tend_recv.at[0]
        else:
            state = states[s]
            below, above = state.at[:, 1, rows, :], state.at[:, PZ, rows, :]
            to_above, to_below = state.at[:, PZ + 1, rows, :], state.at[:, 0, rows, :]
        plan = [
            (below, to_above, {"depth": down_d}),
            (above, to_below, {"depth": up_d}),
            (y_send.at[s], y_recv.at[s, 1], {"image": down_i}),
            (y_send.at[s], y_recv.at[s, 0], {"image": up_i}),
            (x_send.at[s, 0], x_recv.at[s, 1], {"group": down_g}),
            (x_send.at[s, 1], x_recv.at[s, 0], {"group": up_g}),
        ]
        return [
            pltpu.make_async_remote_copy(
                src_ref=src,
                dst_ref=dst,
                send_sem=halo_send.at[s, k],
                recv_sem=halo_recv.at[s, k],
                device_id=device,
                device_id_type=MESH,
            )
            for k, (src, dst, device) in enumerate(plan)
        ]

    row_of = lax.broadcasted_iota(jnp.int32, (8, PY), 0)
    at_top, at_bottom = row_of == 0, row_of == 7

    def from_outside(inner, outer, component, sign):
        prim_in, prim_out = primitives(inner), primitives(outer)
        fastest = jnp.maximum(
            jnp.abs(prim_in[component - 1]) + prim_in[4],
            jnp.abs(prim_out[component - 1]) + prim_out[4],
        )
        flows = flux(outer, prim_out[component - 1], prim_out[3], component)
        return [sign(flows[c]) + fastest * (outer[c] - inner[c]) for c in range(5)]

    def receive_sides(s, copies):
        s = 3 if s == 1 else s
        if copies is not None:
            copies[4].wait_recv()
            copies[5].wait_recv()
        for side, wall in ((0, g == 0), (1, g == NG - 1)):
            own = [x_send[s, side, c] for c in range(5)]
            near = [
                jnp.where(wall, -own[c] if c == 1 else own[c], x_recv[s, side, c])
                for c in range(5)
            ]
            parts = from_outside(own, near, 1, (lambda f: f) if side == 0 else (lambda f: -f))
            for c in range(5):
                x_part[side, c] = parts[c]
        if copies is not None:
            copies[2].wait_recv()
            copies[3].wait_recv()

        def edge(r, carry):
            rows = pl.ds(pl.multiple_of(8 * r, 8), 8)
            own, left, right = y_send[s, rows, :], y_recv[s, 0, rows, :], y_recv[s, 1, rows, :]
            inner, outer = [], []
            for c in range(5):
                inner.append(pltpu.roll(own, (PY - 16 * c) % PY, 1))
                outer.append(
                    jnp.where(
                        even,
                        pltpu.roll(left, (PY + 1 - 16 * c) % PY, 1),
                        pltpu.roll(right, (PY - 1 - 16 * c) % PY, 1),
                    )
                )
            parts = from_outside(inner, outer, 2, lambda f: jnp.where(even, f, -f))
            for c in range(5):
                y_part[c, rows, :] = parts[c]
            return carry

        lax.fori_loop(0, NB, edge, 0, unroll=NB)

    def receive_planes(s, copies):
        state, derived = states[s], prims[s]
        if copies is not None:
            copies[0].wait_recv()
            copies[1].wait_recv()

        def plane(r, carry):
            rows = pl.ds(pl.multiple_of(TOP + 8 * r, 8), 8)
            for z in (0, PZ + 1):
                values = primitives([state[c, z, rows, :] for c in range(5)])
                for c in range(5):
                    derived[c, z, rows, :] = values[c]
            return carry

        lax.fori_loop(0, NB, plane, 0, unroll=NB // 2)

    def add(total, parts):
        return parts if total is None else [t + p for t, p in zip(total, parts)]

    def along_z(s, z, row, cell, prim, total):
        state, derived = states[s], prims[s]
        here = jnp.abs(prim[2]) + prim[4]
        for side in (-1, 1):
            zz = z + 1 + side
            near = [state[c, zz, row : row + 8, :] for c in range(5)]
            q, p = derived[2, zz, row : row + 8, :], derived[3, zz, row : row + 8, :]
            fastest = jnp.maximum(here, jnp.abs(q) + derived[4, zz, row : row + 8, :])
            flows = flux(near, q, p, 3)
            parts = [fastest * (near[c] - cell[c]) for c in range(5)]
            parts = [a + f if side < 0 else a - f for a, f in zip(parts, flows)]
            total = add(total, parts)
        return total

    def centre(s, z, row):
        cell = [states[s][c, z + 1, row : row + 8, :] for c in range(5)]
        return cell, [prims[s][c, z + 1, row : row + 8, :] for c in range(5)]

    def within(s, z, r, with_z):
        state, derived = states[s], prims[s]
        row = TOP + 8 * r
        cell, prim = centre(s, z, row)
        total = along_z(s, z, row, cell, prim, None) if with_z else None
        here = jnp.abs(prim[0]) + prim[4]
        for side in (-1, 1):
            rr = row + side
            near = [state[c, z + 1, rr : rr + 8, :] for c in range(5)]
            q, p = derived[0, z + 1, rr : rr + 8, :], derived[3, z + 1, rr : rr + 8, :]
            fastest = jnp.maximum(here, jnp.abs(q) + derived[4, z + 1, rr : rr + 8, :])
            flows = flux(near, q, p, 1)
            parts = [fastest * (near[c] - cell[c]) for c in range(5)]
            parts = [a + f if side < 0 else a - f for a, f in zip(parts, flows)]
            if side < 0 and r == 0:
                parts = [jnp.where(at_top, 0.0, a) for a in parts]
            if side > 0 and r == NB - 1:
                parts = [jnp.where(at_bottom, 0.0, a) for a in parts]
            total = add(total, parts)
        here = jnp.abs(prim[1]) + prim[4]
        for side in (-1, 1):
            shift = 1 if side < 0 else PY - 1
            near = [pltpu.roll(cell[c], shift, 1) for c in range(5)]
            q, p = pltpu.roll(prim[1], shift, 1), pltpu.roll(prim[3], shift, 1)
            fastest = jnp.maximum(here, pltpu.roll(here, shift, 1))
            flows = flux(near, q, p, 2)
            parts = [fastest * (near[c] - cell[c]) for c in range(5)]
            parts = [a + f if side < 0 else a - f for a, f in zip(parts, flows)]
            outside = at_first if side < 0 else at_last
            total = add(total, [jnp.where(outside, 0.0, a) for a in parts])
        return total

    def completed(s, z, r, with_z, total=None):
        rows = slice(8 * r, 8 * r + 8)
        if total is None:
            total = [tend[c, z, rows, :] for c in range(5)]
        turn = lax.rem(PY - 2 * z, PY)
        for c in range(5):
            edges = pltpu.roll(y_part[c, rows, :], turn, 1)
            total[c] = total[c] + jnp.where(at_first | at_last, edges, 0.0)
        for side, block, place in ((0, 0, at_top), (1, NB - 1, at_bottom)):
            if r == block:
                for c in range(5):
                    line = jnp.broadcast_to(x_part[side, c, pl.ds(z, 1), :], (8, PY))
                    total[c] = total[c] + jnp.where(place, line, 0.0)
        if with_z:
            row = TOP + 8 * r
            cell, prim = centre(s, z, row)
            total = along_z(s, z, row, cell, prim, total)
        return total

    def middle_planes(visit):
        def one(z, carry):
            for r in range(NB):
                visit(z, r, False)
            return carry

        lax.fori_loop(1, PZ - 1, one, 0)

    def all_planes(visit):
        def one(z, carry):
            for r in range(NB):
                visit(z, r, False)
            return carry

        lax.fori_loop(0, PZ, one, 0, unroll=2)

    def end_planes(visit):
        def one(k, carry):
            for r in range(NB):
                visit((PZ - 1) * k, r, True)
            return carry

        lax.fori_loop(0, 2, one, 0)

    def inside(s):
        def visit(z, r, at_end):
            total = within(s, z, r, not at_end)
            for c in range(5):
                tend[c, z, 8 * r : 8 * r + 8, :] = total[c]

        middle_planes(visit)
        end_planes(visit)

    for load in loads[:3]:
        load.wait()

    def signals(z, most):
        for r in range(NB):
            rho, u, v, w, p = [raw[c, z, 8 * r : 8 * r + 8, :] for c in range(5)]
            sound = jnp.sqrt(HEAT_RATIO * p / rho)
            prims[0][4, z + 1, TOP + 8 * r : TOP + 8 * r + 8, :] = sound
            most = jnp.maximum(most, jnp.abs(u) + jnp.abs(v) + jnp.abs(w) + 3.0 * sound)
        return most

    max_own[...] = lax.fori_loop(0, PZ, signals, jnp.zeros((8, PY), jnp.float32), unroll=2)

    def first(z, carry):
        for r in range(NB):
            rho, u, v, w, p = [raw[c, z, 8 * r : 8 * r + 8, :] for c in range(5)]
            energy = p / (HEAT_RATIO - 1.0) + 0.5 * rho * (u * u + v * v + w * w)
            sound = prims[0][4, z + 1, TOP + 8 * r : TOP + 8 * r + 8, :]
            put(0, z, r, [rho, rho * u, rho * v, rho * w, energy], [u, v, w, p, sound])
        return carry

    pl.semaphore_wait(barrier, ND + NG + NI - 3)

    for o in range(1, NI):
        pl.semaphore_signal(
            token, inc=1, device_id={"image": lax.rem(i + o, NI)}, device_id_type=MESH
        )
    lines = [
        pltpu.make_async_remote_copy(
            src_ref=max_own,
            dst_ref=max_line.at[o - 1],
            send_sem=line_send.at[o - 1],
            recv_sem=line_recv.at[o - 1],
            device_id={"depth": lax.rem(d + o, ND)},
            device_id_type=MESH,
        )
        for o in range(1, ND)
    ]
    for copy in lines:
        copy.start()
    lax.fori_loop(0, PZ, first, 0)
    halos = [halo(0)]
    for copy in halos[0]:
        copy.start()
    inside(0)
    for copy in lines:
        copy.wait_recv()
    most = max_own[...]
    for o in range(ND - 1):
        most = jnp.maximum(most, max_line[o])
    max_mid[...] = most
    planes = [
        pltpu.make_async_remote_copy(
            src_ref=max_mid,
            dst_ref=max_plane.at[k],
            send_sem=plane_send.at[k],
            recv_sem=plane_recv.at[k],
            device_id={"group": lax.rem(g + og, NG), "image": lax.rem(i + oi, NI)},
            device_id_type=MESH,
        )
        for k, (og, oi) in enumerate(PAIRS)
    ]
    pl.semaphore_wait(token, NI - 1)
    for copy in planes:
        copy.start()

    receive_sides(0, halos[0])
    receive_planes(0, halos[0])

    def complete(z, r, at_end):
        total = completed(0, z, r, at_end)
        for c in range(5):
            tend[c, z, 8 * r : 8 * r + 8, :] = total[c]
        pack_edges(1, z, r, total)

    halos.append(halo(1))
    end_planes(complete)
    for copy in halos[1][:2]:
        copy.start()
    middle_planes(complete)
    for copy in halos[1][2:]:
        copy.start()

    for load in loads[3:]:
        load.wait()
    pick = lax.rem(2 * lane, PY)
    low, high = index_ref[:, 0:PY], index_ref[:, PY : 2 * PY]
    half = lane < PY // 2
    bins = [
        jnp.where(half, take(low, pick + k), take(high, pick + k)) for k in range(2)
    ]
    words = []
    for c in range(4):
        pal_low = jnp.broadcast_to(palette_ref[c : c + 1, 0:PY], (8, PY))
        pal_high = jnp.broadcast_to(palette_ref[c : c + 1, PY : 2 * PY], (8, PY))
        levels = []
        for b in bins:
            spot = b & (PY - 1)
            colour = jnp.where(b < PY, take(pal_low, spot), take(pal_high, spot))
            levels.append((colour * (1.0 / STEP) + 0.5).astype(jnp.int32))
        levels.append(pltpu.roll(levels[0], PY - 1, 1))
        words.append(levels)
    for k in range(3):
        for c in range(2):
            tables[2 * k + c] = (words[c][k] - 32768) * 65536 + words[c + 2][k]
    for copy in planes:
        copy.wait_recv()
    most = max_mid[...]
    for k in range(len(PAIRS)):
        most = jnp.maximum(most, max_plane[k])
    half_step = (0.5 * COURANT) / jnp.broadcast_to(
        jnp.max(most, axis=(0, 1), keepdims=True), (8, PY)
    )

    def section_one(z, r, at_end):
        row = TOP + 8 * r
        new = [
            u_first[c, z + 1, row : row + 8, :]
            + half_step * tend[c, z, 8 * r : 8 * r + 8, :]
            for c in range(5)
        ]
        put(1, z, r, new, primitives(new))

    def section_two(z, r, at_end):
        total = completed(1, z, r, False, within(1, z, r, True))
        row = TOP + 8 * r
        new = [
            0.75 * u_first[c, z + 1, row : row + 8, :]
            + 0.25 * (u_second[c, z + 1, row : row + 8, :] + half_step * total[c])
            for c in range(5)
        ]
        put(2, z, r, new, primitives(new))

    def section_three(z, r, at_end):
        total = completed(2, z, r, False)
        row = TOP + 8 * r
        rows = slice(8 * r, 8 * r + 8)
        new = [
            u_first[c, z + 1, row : row + 8, :] * (1.0 / 3.0)
            + (2.0 / 3.0) * (u_third[c, z + 1, row : row + 8, :] + half_step * total[c])
            for c in range(5)
        ]
        for c in range(5):
            fluid[c, z, rows, :] = new[c]
        inverse = 1.0 / new[0]
        kinetic = 0.5 * inverse * (new[1] * new[1] + new[2] * new[2] + new[3] * new[3])
        position = jnp.clip(new[0] - 0.5, 0.0, 1.0) * 255.0
        index = (position * 0.5).astype(jnp.int32)
        past = position - 2.0 * index.astype(jnp.float32)
        shade_index[z, rows, :] = index
        shade[0, z, rows, :] = 1.0 - jnp.minimum(past, 1.0)
        shade[1, z, rows, :] = jnp.maximum(past - 1.0, 0.0)
        shade[2, z, rows, :] = new[0] * (-2.0 * STEP / (PZ * ND))
        shade[3, z, rows, :] = (STEP * (HEAT_RATIO - 1.0)) * (new[4] - kinetic) * inverse

    all_planes(section_one)
    for copy in halos[1]:
        copy.wait_recv()
    for side in range(2):
        for c in range(5):
            x_recv[3, side, c] = x_recv[0, side, c] + half_step * x_recv[1, side, c]
        for r in range(NB):
            rows = slice(8 * r, 8 * r + 8)
            y_recv[3, side, rows, :] = (
                y_recv[0, side, rows, :] + half_step * y_recv[1, side, rows, :]
            )

    def outer_planes(r, carry):
        rows = pl.ds(pl.multiple_of(8 * r, 8), 8)
        padded = pl.ds(pl.multiple_of(TOP + 8 * r, 8), 8)
        for side, z in ((0, 0), (1, PZ + 1)):
            for c in range(5):
                u_second[c, z, padded, :] = (
                    u_first[c, z, padded, :] + half_step * tend_recv[side, c, rows, :]
                )
        return carry

    lax.fori_loop(0, NB, outer_planes, 0, unroll=2)
    receive_sides(1, None)
    receive_planes(1, None)
    halos.append(halo(2))
    end_planes(section_two)
    for copy in halos[2][:2]:
        copy.start()
    middle_planes(section_two)
    for copy in halos[2][2:]:
        copy.start()
    for copy in halos[1]:
        copy.wait_send()
    inside(2)
    receive_planes(2, halos[2])

    def with_planes(z, r, at_end):
        row = TOP + 8 * r
        total = along_z(2, z, row, *centre(2, z, row), [tend[c, z, 8 * r : 8 * r + 8, :] for c in range(5)])
        for c in range(5):
            tend[c, z, 8 * r : 8 * r + 8, :] = total[c]

    end_planes(with_planes)
    receive_sides(2, halos[2])
    all_planes(section_three)
    fluid_store = pltpu.make_async_copy(fluid, fluid_out, store_sem.at[0])
    fluid_store.start()

    chip, core = d // 2, lax.rem(d, 2)

    def render(t):
        rows_of = [
            jnp.broadcast_to(tables[k, pl.ds(t, 1), :], (8, PY)) for k in range(6)
        ]
        for r in range(NB):
            rows = slice(8 * r, 8 * r + 8)
            clear, light = None, None
            for z in range(PZ):
                index = shade_index[z, rows, :]
                scale = [shade[0, z, rows, :], None, shade[1, z, rows, :]]
                scale[1] = 1.0 - scale[0] - scale[2]
                looked = [None] * 4
                for k in range(3):
                    for c in range(2):
                        word = take(rows_of[2 * k + c], index)
                        upper = (word >> 16).astype(jnp.float32) * scale[k]
                        lower = (word & 65535).astype(jnp.float32) * scale[k]
                        looked[c] = upper if k == 0 else looked[c] + upper
                        looked[c + 2] = lower if k == 0 else looked[c + 2] + lower
                looked[0] = looked[0] + 32768.0
                looked[1] = looked[1] + 32768.0
                through = jnp.exp(looked[3] * shade[2, z, rows, :])
                weight = (1.0 - through) * shade[3, z, rows, :]
                if z == 0:
                    light = [weight * looked[c] for c in range(3)]
                    clear = through
                else:
                    weight = weight * clear
                    light = [light[c] + weight * looked[c] for c in range(3)]
                    clear = clear * through
            sheet[t, 0, rows, :] = clear
            for c in range(3):
                sheet[t, c + 1, rows, :] = light[c]

    def pair_copy(slot):
        return pltpu.make_async_remote_copy(
            src_ref=sheet.at[2 * slot + 1 - core],
            dst_ref=pair_recv.at[slot],
            send_sem=pair_send_sem.at[slot],
            recv_sem=pair_recv_sem.at[slot],
            device_id={"depth": 2 * chip + 1 - core},
            device_id_type=MESH,
        )

    def chip_copy(owner, source):
        return pltpu.make_async_remote_copy(
            src_ref=joined.at[owner],
            dst_ref=chip_recv.at[source],
            send_sem=chip_send_sem.at[owner],
            recv_sem=chip_recv_sem.at[source],
            device_id={"depth": 2 * owner + core},
            device_id_type=MESH,
        )

    def turn(k, carry):
        mine = (k == 3) | (k == 4) | (k == 5) | (k == 7)
        offset = jnp.where(k < 6, 1 + lax.rem(k, 3), 0)
        owner = lax.rem(chip + offset, 4)
        t = 2 * owner + jnp.where(mine, core, 1 - core)
        render(t)

        @pl.when(jnp.logical_not(mine))
        def _():
            pair_copy(owner).start()

        @pl.when(mine)
        def _():
            pair_copy(owner).wait_recv()
            for r in range(NB):
                rows = slice(8 * r, 8 * r + 8)
                own_clear, other_clear = sheet[t, 0, rows, :], pair_recv[owner, 0, rows, :]
                own_scale = jnp.where(core == 0, 1.0, other_clear)
                other_scale = jnp.where(core == 0, own_clear, 1.0)
                joined[owner, 0, rows, :] = own_clear * other_clear
                for c in range(1, 4):
                    joined[owner, c, rows, :] = (
                        own_scale * sheet[t, c, rows, :]
                        + other_scale * pair_recv[owner, c, rows, :]
                    )

        @pl.when(mine & (k < 6))
        def _():
            chip_copy(owner, chip).start()

        return carry

    lax.fori_loop(0, 8, turn, 0)
    for o in (1, 3, 2):
        source = lax.rem(chip + o, 4)
        chip_copy(source, source).wait_recv()
    chip_recv[chip] = joined[chip]
    ahead = chip_recv[0, 0]
    light = [chip_recv[0, c] for c in range(1, 4)]
    for k in range(1, 4):
        for c in range(3):
            light[c] = light[c] + ahead * chip_recv[k, c + 1]
        if k < 3:
            ahead = ahead * chip_recv[k, 0]
    for c in range(3):
        picture[c] = light[c]
    picture_store = pltpu.make_async_copy(picture, picture_out, store_sem.at[1])
    picture_store.start()

    for copy in lines + planes + halos[0] + halos[2]:
        copy.wait_send()
    for k in range(4):
        pair_copy(k).wait_send()
    for o in range(1, 4):
        source = lax.rem(chip + o, 4)
        chip_copy(source, source).wait_send()
    fluid_store.wait()
    picture_store.wait()


def shards(density, velocity, pressure, palette, palette_index):
    f32 = jnp.float32
    any_space = pl.BlockSpec(memory_space=pl.ANY)
    padded = (5, PZ + 2, PX + 16, PY)
    dma = pltpu.SemaphoreType.DMA
    fluid_state, picture = pl.pallas_call(
        kernel,
        out_shape=(
            jax.ShapeDtypeStruct((5, PZ, PX, PY), f32),
            jax.ShapeDtypeStruct((3, PX, PY), f32),
        ),
        in_specs=[any_space] * 5,
        out_specs=(any_space, any_space),
        scratch_shapes=[
            pltpu.VMEM((5, PZ, PX, PY), f32),
            pltpu.VMEM((4, 2 * PY), f32),
            pltpu.VMEM((8, 2 * PY), jnp.int32),
            pltpu.VMEM(padded, f32),
            pltpu.VMEM(padded, f32),
            pltpu.VMEM(padded, f32),
            pltpu.VMEM(padded, f32),
            pltpu.VMEM(padded, f32),
            pltpu.VMEM((5, PZ, PX, PY), f32),
            pltpu.VMEM((2, 5, PX, PY), f32),
            pltpu.VMEM((4, 2, 5, PZ, PY), f32),
            pltpu.VMEM((4, 2, 5, PZ, PY), f32),
            pltpu.VMEM((4, PX, PY), f32),
            pltpu.VMEM((4, 2, PX, PY), f32),
            pltpu.VMEM((2, 5, PZ, PY), f32),
            pltpu.VMEM((5, PX, PY), f32),
            pltpu.VMEM((8, PY), f32),
            pltpu.VMEM((ND - 1, 8, PY), f32),
            pltpu.VMEM((8, PY), f32),
            pltpu.VMEM((len(PAIRS), 8, PY), f32),
            pltpu.VMEM((5, PZ, PX, PY), f32),
            pltpu.VMEM((4, PZ, PX, PY), f32),
            pltpu.VMEM((PZ, PX, PY), jnp.int32),
            pltpu.VMEM((6, 8, PY), jnp.int32),
            pltpu.VMEM((8, 4, PX, PY), f32),
            pltpu.VMEM((4, 4, PX, PY), f32),
            pltpu.VMEM((4, 4, PX, PY), f32),
            pltpu.VMEM((4, 4, PX, PY), f32),
            pltpu.VMEM((3, PX, PY), f32),
            dma((5,)),
            dma((2,)),
            dma((3, 6)),
            dma((3, 6)),
            dma((ND - 1,)),
            dma((ND - 1,)),
            dma((len(PAIRS),)),
            dma((len(PAIRS),)),
            pltpu.SemaphoreType.REGULAR,
            dma((4,)),
            dma((4,)),
            dma((4,)),
            dma((4,)),
        ],
        compiler_params=pltpu.CompilerParams(
            collective_id=0, has_side_effects=True, vmem_limit_bytes=60 * 1024 * 1024
        ),
    )(density, velocity, pressure, palette, palette_index)
    return fluid_state, picture[None]


def solution(mesh):
    return jax.shard_map(
        shards,
        mesh=mesh,
        in_specs=(
            P("depth", "group", "image"),
            P(None, "depth", "group", "image"),
            P("depth", "group", "image"),
            P(),
            P(),
        ),
        out_specs=(P(None, "depth", "group", "image"), P("depth", None, "group", "image")),
        check_vma=False,
    )
```

```python
import jax
import jax.numpy as jnp
from jax import lax
from jax.experimental import pallas as pl
from jax.experimental.pallas import tpu as pltpu
from jax.sharding import PartitionSpec as P

MESH = pl.DeviceIdType.MESH
HEAT_RATIO = 1.4
COURANT = 0.8
NG, ND, NI = 4, 8, 4
PZ, PX, PY = 8, 48, 128
NB = PX // 8
TOP = 8
STEP = 2.0 / 65535.0
PAIRS = [(g, i) for g in range(NG) for i in range(NI) if (g, i) != (0, 0)]


def take(table, index):
    return jnp.take_along_axis(table, index, axis=1, mode="promise_in_bounds")


def primitives(state):
    inverse = 1.0 / state[0]
    u, v, w = state[1] * inverse, state[2] * inverse, state[3] * inverse
    kinetic = 0.5 * (state[1] * u + state[2] * v + state[3] * w)
    p = (HEAT_RATIO - 1.0) * (state[4] - kinetic)
    return [u, v, w, p, jnp.sqrt(HEAT_RATIO * p * inverse)]


def flux(state, q, p, component):
    rows = [state[0] * q, state[1] * q, state[2] * q, state[3] * q, (state[4] + p) * q]
    rows[component] = rows[component] + p
    return rows


def kernel(
    density_in,
    velocity_in,
    pressure_in,
    palette_in,
    index_in,
    fluid_out,
    picture_out,
    raw,
    palette_ref,
    index_ref,
    u_first,
    u_second,
    u_third,
    prim_a,
    prim_b,
    tend,
    tend_recv,
    x_send,
    x_recv,
    y_send,
    y_recv,
    x_part,
    y_part,
    max_own,
    max_line,
    max_mid,
    max_plane,
    fluid,
    shade,
    shade_index,
    tables,
    sheet,
    pair_recv,
    joined,
    chip_recv,
    picture,
    load_sem,
    store_sem,
    halo_send,
    halo_recv,
    line_send,
    line_recv,
    plane_send,
    plane_recv,
    token,
    pair_send_sem,
    pair_recv_sem,
    chip_send_sem,
    chip_recv_sem,
):
    g, d, i = lax.axis_index("group"), lax.axis_index("depth"), lax.axis_index("image")
    states = [u_first, u_second, u_third]
    prims = [prim_a, prim_b, prim_a]

    loads = [
        pltpu.make_async_copy(density_in, raw.at[0], load_sem.at[0]),
        pltpu.make_async_copy(velocity_in, raw.at[pl.ds(1, 3)], load_sem.at[1]),
        pltpu.make_async_copy(pressure_in, raw.at[4], load_sem.at[2]),
        pltpu.make_async_copy(palette_in, palette_ref, load_sem.at[3]),
        pltpu.make_async_copy(index_in, index_ref, load_sem.at[4]),
    ]
    for load in loads:
        load.start()

    barrier = pltpu.get_barrier_semaphore()
    for o in range(1, ND):
        pl.semaphore_signal(
            barrier, inc=1, device_id={"depth": lax.rem(d + o, ND)}, device_id_type=MESH
        )
    for o in range(1, NG):
        pl.semaphore_signal(
            barrier, inc=1, device_id={"group": lax.rem(g + o, NG)}, device_id_type=MESH
        )
    for o in range(1, NI):
        pl.semaphore_signal(
            barrier, inc=1, device_id={"image": lax.rem(i + o, NI)}, device_id_type=MESH
        )

    lane = lax.broadcasted_iota(jnp.int32, (8, PY), 1)
    even = lax.rem(lane, 2) == 0
    at_first = lane == 0
    at_last = lane == PY - 1

    def pack_edges(s, z, r, new):
        rows = pl.ds(8 * r, 8)
        for c in range(5):
            shift = 16 * c + 2 * z
            turned = pltpu.roll(new[c], shift, 1)
            low = lax.rem(shift + PY - 1, PY)
            pltpu.store(
                y_send.at[s, rows, :], turned, mask=(lane == shift) | (lane == low)
            )
            if r == 0:
                x_send[s, 0, c, pl.ds(z, 1), :] = new[c][0:1]
            if r == NB - 1:
                x_send[s, 1, c, pl.ds(z, 1), :] = new[c][7:8]

    def put(s, z, r, new, derived):
        rows = pl.ds(TOP + 8 * r, 8)
        for c in range(5):
            states[s][c, z + 1, rows, :] = new[c]
            prims[s][c, z + 1, rows, :] = derived[c]
        pack_edges(3 if s == 1 else s, z, r, new)

    def halo(s):
        up_d, down_d = lax.rem(d + 1, ND), lax.rem(d + ND - 1, ND)
        up_g, down_g = lax.rem(g + 1, NG), lax.rem(g + NG - 1, NG)
        up_i, down_i = lax.rem(i + 1, NI), lax.rem(i + NI - 1, NI)
        rows = pl.ds(TOP, PX)
        if s == 1:
            below, above = tend.at[:, 0], tend.at[:, PZ - 1]
            to_above, to_below = tend_recv.at[1], tend_recv.at[0]
        else:
            state = states[s]
            below, above = state.at[:, 1, rows, :], state.at[:, PZ, rows, :]
            to_above, to_below = state.at[:, PZ + 1, rows, :], state.at[:, 0, rows, :]
        plan = [
            (below, to_above, {"depth": down_d}),
            (above, to_below, {"depth": up_d}),
            (y_send.at[s], y_recv.at[s, 1], {"image": down_i}),
            (y_send.at[s], y_recv.at[s, 0], {"image": up_i}),
            (x_send.at[s, 0], x_recv.at[s, 1], {"group": down_g}),
            (x_send.at[s, 1], x_recv.at[s, 0], {"group": up_g}),
        ]
        return [
            pltpu.make_async_remote_copy(
                src_ref=src,
                dst_ref=dst,
                send_sem=halo_send.at[s, k],
                recv_sem=halo_recv.at[s, k],
                device_id=device,
                device_id_type=MESH,
            )
            for k, (src, dst, device) in enumerate(plan)
        ]

    row_of = lax.broadcasted_iota(jnp.int32, (8, PY), 0)
    at_top, at_bottom = row_of == 0, row_of == 7

    def from_outside(inner, outer, component, sign):
        prim_in, prim_out = primitives(inner), primitives(outer)
        fastest = jnp.maximum(
            jnp.abs(prim_in[component - 1]) + prim_in[4],
            jnp.abs(prim_out[component - 1]) + prim_out[4],
        )
        flows = flux(outer, prim_out[component - 1], prim_out[3], component)
        return [sign(flows[c]) + fastest * (outer[c] - inner[c]) for c in range(5)]

    def receive_sides(s, copies):
        s = 3 if s == 1 else s
        if copies is not None:
            copies[4].wait_recv()
            copies[5].wait_recv()
        for side, wall in ((0, g == 0), (1, g == NG - 1)):
            own = [x_send[s, side, c] for c in range(5)]
            near = [
                jnp.where(wall, -own[c] if c == 1 else own[c], x_recv[s, side, c])
                for c in range(5)
            ]
            parts = from_outside(own, near, 1, (lambda f: f) if side == 0 else (lambda f: -f))
            for c in range(5):
                x_part[side, c] = parts[c]
        if copies is not None:
            copies[2].wait_recv()
            copies[3].wait_recv()

        def edge(r, carry):
            rows = pl.ds(pl.multiple_of(8 * r, 8), 8)
            own, left, right = y_send[s, rows, :], y_recv[s, 0, rows, :], y_recv[s, 1, rows, :]
            inner, outer = [], []
            for c in range(5):
                inner.append(pltpu.roll(own, (PY - 16 * c) % PY, 1))
                outer.append(
                    jnp.where(
                        even,
                        pltpu.roll(left, (PY + 1 - 16 * c) % PY, 1),
                        pltpu.roll(right, (PY - 1 - 16 * c) % PY, 1),
                    )
                )
            parts = from_outside(inner, outer, 2, lambda f: jnp.where(even, f, -f))
            for c in range(5):
                y_part[c, rows, :] = parts[c]
            return carry

        lax.fori_loop(0, NB, edge, 0, unroll=NB)

    def receive_planes(s, copies):
        state, derived = states[s], prims[s]
        if copies is not None:
            copies[0].wait_recv()
            copies[1].wait_recv()

        def plane(r, carry):
            rows = pl.ds(pl.multiple_of(TOP + 8 * r, 8), 8)
            for z in (0, PZ + 1):
                values = primitives([state[c, z, rows, :] for c in range(5)])
                for c in range(5):
                    derived[c, z, rows, :] = values[c]
            return carry

        lax.fori_loop(0, NB, plane, 0, unroll=NB // 2)

    def add(total, parts):
        return parts if total is None else [t + p for t, p in zip(total, parts)]

    def along_z(s, z, row, cell, prim, total):
        state, derived = states[s], prims[s]
        here = jnp.abs(prim[2]) + prim[4]
        for side in (-1, 1):
            zz = z + 1 + side
            near = [state[c, zz, row : row + 8, :] for c in range(5)]
            q, p = derived[2, zz, row : row + 8, :], derived[3, zz, row : row + 8, :]
            fastest = jnp.maximum(here, jnp.abs(q) + derived[4, zz, row : row + 8, :])
            flows = flux(near, q, p, 3)
            parts = [fastest * (near[c] - cell[c]) for c in range(5)]
            parts = [a + f if side < 0 else a - f for a, f in zip(parts, flows)]
            total = add(total, parts)
        return total

    def centre(s, z, row):
        cell = [states[s][c, z + 1, row : row + 8, :] for c in range(5)]
        return cell, [prims[s][c, z + 1, row : row + 8, :] for c in range(5)]

    def within(s, z, r, with_z):
        state, derived = states[s], prims[s]
        row = TOP + 8 * r
        cell, prim = centre(s, z, row)
        total = along_z(s, z, row, cell, prim, None) if with_z else None
        here = jnp.abs(prim[0]) + prim[4]
        for side in (-1, 1):
            rr = row + side
            near = [state[c, z + 1, rr : rr + 8, :] for c in range(5)]
            q, p = derived[0, z + 1, rr : rr + 8, :], derived[3, z + 1, rr : rr + 8, :]
            fastest = jnp.maximum(here, jnp.abs(q) + derived[4, z + 1, rr : rr + 8, :])
            flows = flux(near, q, p, 1)
            parts = [fastest * (near[c] - cell[c]) for c in range(5)]
            parts = [a + f if side < 0 else a - f for a, f in zip(parts, flows)]
            if side < 0 and r == 0:
                parts = [jnp.where(at_top, 0.0, a) for a in parts]
            if side > 0 and r == NB - 1:
                parts = [jnp.where(at_bottom, 0.0, a) for a in parts]
            total = add(total, parts)
        here = jnp.abs(prim[1]) + prim[4]
        for side in (-1, 1):
            shift = 1 if side < 0 else PY - 1
            near = [pltpu.roll(cell[c], shift, 1) for c in range(5)]
            q, p = pltpu.roll(prim[1], shift, 1), pltpu.roll(prim[3], shift, 1)
            fastest = jnp.maximum(here, pltpu.roll(here, shift, 1))
            flows = flux(near, q, p, 2)
            parts = [fastest * (near[c] - cell[c]) for c in range(5)]
            parts = [a + f if side < 0 else a - f for a, f in zip(parts, flows)]
            outside = at_first if side < 0 else at_last
            total = add(total, [jnp.where(outside, 0.0, a) for a in parts])
        return total

    def completed(s, z, r, with_z, total=None):
        rows = slice(8 * r, 8 * r + 8)
        if total is None:
            total = [tend[c, z, rows, :] for c in range(5)]
        turn = lax.rem(PY - 2 * z, PY)
        for c in range(5):
            edges = pltpu.roll(y_part[c, rows, :], turn, 1)
            total[c] = total[c] + jnp.where(at_first | at_last, edges, 0.0)
        for side, block, place in ((0, 0, at_top), (1, NB - 1, at_bottom)):
            if r == block:
                for c in range(5):
                    line = jnp.broadcast_to(x_part[side, c, pl.ds(z, 1), :], (8, PY))
                    total[c] = total[c] + jnp.where(place, line, 0.0)
        if with_z:
            row = TOP + 8 * r
            cell, prim = centre(s, z, row)
            total = along_z(s, z, row, cell, prim, total)
        return total

    def middle_planes(visit):
        def one(z, carry):
            for r in range(NB):
                visit(z, r, False)
            return carry

        lax.fori_loop(1, PZ - 1, one, 0)

    def all_planes(visit):
        def one(z, carry):
            for r in range(NB):
                visit(z, r, False)
            return carry

        lax.fori_loop(0, PZ, one, 0, unroll=2)

    def end_planes(visit):
        def one(k, carry):
            for r in range(NB):
                visit((PZ - 1) * k, r, True)
            return carry

        lax.fori_loop(0, 2, one, 0, unroll=2)

    def inside(s):
        def visit(z, r, at_end):
            total = within(s, z, r, not at_end)
            for c in range(5):
                tend[c, z, 8 * r : 8 * r + 8, :] = total[c]

        middle_planes(visit)
        end_planes(visit)

    for load in loads[:3]:
        load.wait()

    def signals(z, most):
        for r in range(NB):
            rho, u, v, w, p = [raw[c, z, 8 * r : 8 * r + 8, :] for c in range(5)]
            sound = jnp.sqrt(HEAT_RATIO * p / rho)
            prims[0][4, z + 1, TOP + 8 * r : TOP + 8 * r + 8, :] = sound
            most = jnp.maximum(most, jnp.abs(u) + jnp.abs(v) + jnp.abs(w) + 3.0 * sound)
        return most

    max_own[...] = lax.fori_loop(0, PZ, signals, jnp.zeros((8, PY), jnp.float32), unroll=2)

    def first(z, carry):
        for r in range(NB):
            rho, u, v, w, p = [raw[c, z, 8 * r : 8 * r + 8, :] for c in range(5)]
            energy = p / (HEAT_RATIO - 1.0) + 0.5 * rho * (u * u + v * v + w * w)
            sound = prims[0][4, z + 1, TOP + 8 * r : TOP + 8 * r + 8, :]
            put(0, z, r, [rho, rho * u, rho * v, rho * w, energy], [u, v, w, p, sound])
        return carry

    pl.semaphore_wait(barrier, ND + NG + NI - 3)

    for o in range(1, NI):
        pl.semaphore_signal(
            token, inc=1, device_id={"image": lax.rem(i + o, NI)}, device_id_type=MESH
        )
    lines = [
        pltpu.make_async_remote_copy(
            src_ref=max_own,
            dst_ref=max_line.at[o - 1],
            send_sem=line_send.at[o - 1],
            recv_sem=line_recv.at[o - 1],
            device_id={"depth": lax.rem(d + o, ND)},
            device_id_type=MESH,
        )
        for o in range(1, ND)
    ]
    for copy in lines:
        copy.start()
    lax.fori_loop(0, PZ, first, 0)
    halos = [halo(0)]
    for copy in halos[0]:
        copy.start()
    inside(0)
    for copy in lines:
        copy.wait_recv()
    most = max_own[...]
    for o in range(ND - 1):
        most = jnp.maximum(most, max_line[o])
    max_mid[...] = most
    planes = [
        pltpu.make_async_remote_copy(
            src_ref=max_mid,
            dst_ref=max_plane.at[k],
            send_sem=plane_send.at[k],
            recv_sem=plane_recv.at[k],
            device_id={"group": lax.rem(g + og, NG), "image": lax.rem(i + oi, NI)},
            device_id_type=MESH,
        )
        for k, (og, oi) in enumerate(PAIRS)
    ]
    pl.semaphore_wait(token, NI - 1)
    for copy in planes:
        copy.start()

    receive_sides(0, halos[0])
    receive_planes(0, halos[0])

    def complete(z, r, at_end):
        total = completed(0, z, r, at_end)
        for c in range(5):
            tend[c, z, 8 * r : 8 * r + 8, :] = total[c]
        pack_edges(1, z, r, total)

    halos.append(halo(1))
    end_planes(complete)
    for copy in halos[1][:2]:
        copy.start()
    middle_planes(complete)
    for copy in halos[1][2:]:
        copy.start()

    for load in loads[3:]:
        load.wait()
    pick = lax.rem(2 * lane, PY)
    low, high = index_ref[:, 0:PY], index_ref[:, PY : 2 * PY]
    half = lane < PY // 2
    bins = [
        jnp.where(half, take(low, pick + k), take(high, pick + k)) for k in range(2)
    ]
    words = []
    for c in range(4):
        pal_low = jnp.broadcast_to(palette_ref[c : c + 1, 0:PY], (8, PY))
        pal_high = jnp.broadcast_to(palette_ref[c : c + 1, PY : 2 * PY], (8, PY))
        levels = []
        for b in bins:
            spot = b & (PY - 1)
            colour = jnp.where(b < PY, take(pal_low, spot), take(pal_high, spot))
            levels.append((colour * (1.0 / STEP) + 0.5).astype(jnp.int32))
        levels.append(pltpu.roll(levels[0], PY - 1, 1))
        words.append(levels)
    for k in range(3):
        for c in range(2):
            tables[2 * k + c] = (words[c][k] - 32768) * 65536 + words[c + 2][k]
    for copy in planes:
        copy.wait_recv()
    most = max_mid[...]
    for k in range(len(PAIRS)):
        most = jnp.maximum(most, max_plane[k])
    half_step = (0.5 * COURANT) / jnp.broadcast_to(
        jnp.max(most, axis=(0, 1), keepdims=True), (8, PY)
    )

    def section_one(z, r, at_end):
        row = TOP + 8 * r
        new = [
            u_first[c, z + 1, row : row + 8, :]
            + half_step * tend[c, z, 8 * r : 8 * r + 8, :]
            for c in range(5)
        ]
        put(1, z, r, new, primitives(new))

    def section_two(z, r, at_end):
        total = completed(1, z, r, False, within(1, z, r, True))
        row = TOP + 8 * r
        new = [
            0.75 * u_first[c, z + 1, row : row + 8, :]
            + 0.25 * (u_second[c, z + 1, row : row + 8, :] + half_step * total[c])
            for c in range(5)
        ]
        put(2, z, r, new, primitives(new))

    def section_three(z, r, at_end):
        total = completed(2, z, r, False)
        row = TOP + 8 * r
        rows = slice(8 * r, 8 * r + 8)
        new = [
            u_first[c, z + 1, row : row + 8, :] * (1.0 / 3.0)
            + (2.0 / 3.0) * (u_third[c, z + 1, row : row + 8, :] + half_step * total[c])
            for c in range(5)
        ]
        for c in range(5):
            fluid[c, z, rows, :] = new[c]
        inverse = 1.0 / new[0]
        kinetic = 0.5 * inverse * (new[1] * new[1] + new[2] * new[2] + new[3] * new[3])
        position = jnp.clip(new[0] - 0.5, 0.0, 1.0) * 255.0
        index = (position * 0.5).astype(jnp.int32)
        past = position - 2.0 * index.astype(jnp.float32)
        shade_index[z, rows, :] = index
        shade[0, z, rows, :] = 1.0 - jnp.minimum(past, 1.0)
        shade[1, z, rows, :] = jnp.maximum(past - 1.0, 0.0)
        shade[2, z, rows, :] = new[0] * (-2.0 * STEP / (PZ * ND))
        shade[3, z, rows, :] = (STEP * (HEAT_RATIO - 1.0)) * (new[4] - kinetic) * inverse

    all_planes(section_one)
    for copy in halos[1]:
        copy.wait_recv()
    for side in range(2):
        for c in range(5):
            x_recv[3, side, c] = x_recv[0, side, c] + half_step * x_recv[1, side, c]
        for r in range(NB):
            rows = slice(8 * r, 8 * r + 8)
            y_recv[3, side, rows, :] = (
                y_recv[0, side, rows, :] + half_step * y_recv[1, side, rows, :]
            )

    def outer_planes(r, carry):
        rows = pl.ds(pl.multiple_of(8 * r, 8), 8)
        padded = pl.ds(pl.multiple_of(TOP + 8 * r, 8), 8)
        for side, z in ((0, 0), (1, PZ + 1)):
            for c in range(5):
                u_second[c, z, padded, :] = (
                    u_first[c, z, padded, :] + half_step * tend_recv[side, c, rows, :]
                )
        return carry

    lax.fori_loop(0, NB, outer_planes, 0, unroll=2)
    receive_sides(1, None)
    receive_planes(1, None)
    halos.append(halo(2))
    end_planes(section_two)
    for copy in halos[2][:2]:
        copy.start()
    middle_planes(section_two)
    for copy in halos[2][2:]:
        copy.start()
    for copy in halos[1]:
        copy.wait_send()
    inside(2)
    receive_planes(2, halos[2])

    def with_planes(z, r, at_end):
        row = TOP + 8 * r
        total = along_z(2, z, row, *centre(2, z, row), [tend[c, z, 8 * r : 8 * r + 8, :] for c in range(5)])
        for c in range(5):
            tend[c, z, 8 * r : 8 * r + 8, :] = total[c]

    end_planes(with_planes)
    receive_sides(2, halos[2])
    all_planes(section_three)
    fluid_store = pltpu.make_async_copy(fluid, fluid_out, store_sem.at[0])
    fluid_store.start()

    chip, core = d // 2, lax.rem(d, 2)

    def render(t):
        rows_of = [
            jnp.broadcast_to(tables[k, pl.ds(t, 1), :], (8, PY)) for k in range(6)
        ]
        for r in range(NB):
            rows = slice(8 * r, 8 * r + 8)
            clear, light = None, None
            for z in range(PZ):
                index = shade_index[z, rows, :]
                scale = [shade[0, z, rows, :], None, shade[1, z, rows, :]]
                scale[1] = 1.0 - scale[0] - scale[2]
                looked = [None] * 4
                for k in range(3):
                    for c in range(2):
                        word = take(rows_of[2 * k + c], index)
                        upper = (word >> 16).astype(jnp.float32) * scale[k]
                        lower = (word & 65535).astype(jnp.float32) * scale[k]
                        looked[c] = upper if k == 0 else looked[c] + upper
                        looked[c + 2] = lower if k == 0 else looked[c + 2] + lower
                looked[0] = looked[0] + 32768.0
                looked[1] = looked[1] + 32768.0
                through = jnp.exp(looked[3] * shade[2, z, rows, :])
                weight = (1.0 - through) * shade[3, z, rows, :]
                if z == 0:
                    light = [weight * looked[c] for c in range(3)]
                    clear = through
                else:
                    weight = weight * clear
                    light = [light[c] + weight * looked[c] for c in range(3)]
                    clear = clear * through
            sheet[t, 0, rows, :] = clear
            for c in range(3):
                sheet[t, c + 1, rows, :] = light[c]

    def pair_copy(slot):
        return pltpu.make_async_remote_copy(
            src_ref=sheet.at[2 * slot + 1 - core],
            dst_ref=pair_recv.at[slot],
            send_sem=pair_send_sem.at[slot],
            recv_sem=pair_recv_sem.at[slot],
            device_id={"depth": 2 * chip + 1 - core},
            device_id_type=MESH,
        )

    def chip_copy(owner, source):
        return pltpu.make_async_remote_copy(
            src_ref=joined.at[owner],
            dst_ref=chip_recv.at[source],
            send_sem=chip_send_sem.at[owner],
            recv_sem=chip_recv_sem.at[source],
            device_id={"depth": 2 * owner + core},
            device_id_type=MESH,
        )

    def turn(k, carry):
        mine = (k == 3) | (k == 4) | (k == 5) | (k == 7)
        offset = jnp.where(k < 6, 1 + lax.rem(k, 3), 0)
        owner = lax.rem(chip + offset, 4)
        t = 2 * owner + jnp.where(mine, core, 1 - core)
        render(t)

        @pl.when(jnp.logical_not(mine))
        def _():
            pair_copy(owner).start()

        @pl.when(mine)
        def _():
            pair_copy(owner).wait_recv()
            for r in range(NB):
                rows = slice(8 * r, 8 * r + 8)
                own_clear, other_clear = sheet[t, 0, rows, :], pair_recv[owner, 0, rows, :]
                own_scale = jnp.where(core == 0, 1.0, other_clear)
                other_scale = jnp.where(core == 0, own_clear, 1.0)
                joined[owner, 0, rows, :] = own_clear * other_clear
                for c in range(1, 4):
                    joined[owner, c, rows, :] = (
                        own_scale * sheet[t, c, rows, :]
                        + other_scale * pair_recv[owner, c, rows, :]
                    )

        @pl.when(mine & (k < 6))
        def _():
            chip_copy(owner, chip).start()

        return carry

    lax.fori_loop(0, 8, turn, 0)
    for o in (1, 3, 2):
        source = lax.rem(chip + o, 4)
        chip_copy(source, source).wait_recv()
    chip_recv[chip] = joined[chip]
    ahead = chip_recv[0, 0]
    light = [chip_recv[0, c] for c in range(1, 4)]
    for k in range(1, 4):
        for c in range(3):
            light[c] = light[c] + ahead * chip_recv[k, c + 1]
        if k < 3:
            ahead = ahead * chip_recv[k, 0]
    for c in range(3):
        picture[c] = light[c]
    picture_store = pltpu.make_async_copy(picture, picture_out, store_sem.at[1])
    picture_store.start()

    for copy in lines + planes + halos[0] + halos[2]:
        copy.wait_send()
    for k in range(4):
        pair_copy(k).wait_send()
    for o in range(1, 4):
        source = lax.rem(chip + o, 4)
        chip_copy(source, source).wait_send()
    fluid_store.wait()
    picture_store.wait()


def shards(density, velocity, pressure, palette, palette_index):
    f32 = jnp.float32
    any_space = pl.BlockSpec(memory_space=pl.ANY)
    padded = (5, PZ + 2, PX + 16, PY)
    dma = pltpu.SemaphoreType.DMA
    fluid_state, picture = pl.pallas_call(
        kernel,
        out_shape=(
            jax.ShapeDtypeStruct((5, PZ, PX, PY), f32),
            jax.ShapeDtypeStruct((3, PX, PY), f32),
        ),
        in_specs=[any_space] * 5,
        out_specs=(any_space, any_space),
        scratch_shapes=[
            pltpu.VMEM((5, PZ, PX, PY), f32),
            pltpu.VMEM((4, 2 * PY), f32),
            pltpu.VMEM((8, 2 * PY), jnp.int32),
            pltpu.VMEM(padded, f32),
            pltpu.VMEM(padded, f32),
            pltpu.VMEM(padded, f32),
            pltpu.VMEM(padded, f32),
            pltpu.VMEM(padded, f32),
            pltpu.VMEM((5, PZ, PX, PY), f32),
            pltpu.VMEM((2, 5, PX, PY), f32),
            pltpu.VMEM((4, 2, 5, PZ, PY), f32),
            pltpu.VMEM((4, 2, 5, PZ, PY), f32),
            pltpu.VMEM((4, PX, PY), f32),
            pltpu.VMEM((4, 2, PX, PY), f32),
            pltpu.VMEM((2, 5, PZ, PY), f32),
            pltpu.VMEM((5, PX, PY), f32),
            pltpu.VMEM((8, PY), f32),
            pltpu.VMEM((ND - 1, 8, PY), f32),
            pltpu.VMEM((8, PY), f32),
            pltpu.VMEM((len(PAIRS), 8, PY), f32),
            pltpu.VMEM((5, PZ, PX, PY), f32),
            pltpu.VMEM((4, PZ, PX, PY), f32),
            pltpu.VMEM((PZ, PX, PY), jnp.int32),
            pltpu.VMEM((6, 8, PY), jnp.int32),
            pltpu.VMEM((8, 4, PX, PY), f32),
            pltpu.VMEM((4, 4, PX, PY), f32),
            pltpu.VMEM((4, 4, PX, PY), f32),
            pltpu.VMEM((4, 4, PX, PY), f32),
            pltpu.VMEM((3, PX, PY), f32),
            dma((5,)),
            dma((2,)),
            dma((3, 6)),
            dma((3, 6)),
            dma((ND - 1,)),
            dma((ND - 1,)),
            dma((len(PAIRS),)),
            dma((len(PAIRS),)),
            pltpu.SemaphoreType.REGULAR,
            dma((4,)),
            dma((4,)),
            dma((4,)),
            dma((4,)),
        ],
        compiler_params=pltpu.CompilerParams(
            collective_id=0, has_side_effects=True, vmem_limit_bytes=60 * 1024 * 1024
        ),
    )(density, velocity, pressure, palette, palette_index)
    return fluid_state, picture[None]


def solution(mesh):
    return jax.shard_map(
        shards,
        mesh=mesh,
        in_specs=(
            P("depth", "group", "image"),
            P(None, "depth", "group", "image"),
            P("depth", "group", "image"),
            P(),
            P(),
        ),
        out_specs=(P(None, "depth", "group", "image"), P("depth", None, "group", "image")),
        check_vma=False,
    )
```

```python
import jax
import jax.numpy as jnp
from jax import lax
from jax.experimental import pallas as pl
from jax.experimental.pallas import tpu as pltpu
from jax.sharding import PartitionSpec as P

MESH = pl.DeviceIdType.MESH
HEAT_RATIO = 1.4
COURANT = 0.8
NG, ND, NI = 4, 8, 4
PZ, PX, PY = 8, 48, 128
NB = PX // 8
TOP = 8
STEP = 2.0 / 65535.0
PAIRS = [(g, i) for g in range(NG) for i in range(NI) if (g, i) != (0, 0)]


def take(table, index):
    return jnp.take_along_axis(table, index, axis=1, mode="promise_in_bounds")


def primitives(state):
    inverse = 1.0 / state[0]
    u, v, w = state[1] * inverse, state[2] * inverse, state[3] * inverse
    kinetic = 0.5 * (state[1] * u + state[2] * v + state[3] * w)
    p = (HEAT_RATIO - 1.0) * (state[4] - kinetic)
    return [u, v, w, p, jnp.sqrt(HEAT_RATIO * p * inverse)]


def flux(state, q, p, component):
    rows = [state[0] * q, state[1] * q, state[2] * q, state[3] * q, (state[4] + p) * q]
    rows[component] = rows[component] + p
    return rows


def kernel(
    density_in,
    velocity_in,
    pressure_in,
    palette_in,
    index_in,
    fluid_out,
    picture_out,
    raw,
    palette_ref,
    index_ref,
    u_first,
    u_second,
    u_third,
    prim_a,
    prim_b,
    tend,
    tend_recv,
    x_send,
    x_recv,
    y_send,
    y_recv,
    x_part,
    y_part,
    max_own,
    max_line,
    max_mid,
    max_plane,
    fluid,
    shade,
    shade_index,
    tables,
    sheet,
    pair_recv,
    joined,
    chip_recv,
    picture,
    load_sem,
    store_sem,
    halo_send,
    halo_recv,
    line_send,
    line_recv,
    plane_send,
    plane_recv,
    token,
    pair_send_sem,
    pair_recv_sem,
    chip_send_sem,
    chip_recv_sem,
):
    g, d, i = lax.axis_index("group"), lax.axis_index("depth"), lax.axis_index("image")
    states = [u_first, u_second, u_third]
    prims = [prim_a, prim_b, prim_a]

    loads = [
        pltpu.make_async_copy(density_in, raw.at[0], load_sem.at[0]),
        pltpu.make_async_copy(velocity_in, raw.at[pl.ds(1, 3)], load_sem.at[1]),
        pltpu.make_async_copy(pressure_in, raw.at[4], load_sem.at[2]),
        pltpu.make_async_copy(palette_in, palette_ref, load_sem.at[3]),
        pltpu.make_async_copy(index_in, index_ref, load_sem.at[4]),
    ]
    for load in loads:
        load.start()

    barrier = pltpu.get_barrier_semaphore()
    for o in range(1, ND):
        pl.semaphore_signal(
            barrier, inc=1, device_id={"depth": lax.rem(d + o, ND)}, device_id_type=MESH
        )
    for o in range(1, NG):
        pl.semaphore_signal(
            barrier, inc=1, device_id={"group": lax.rem(g + o, NG)}, device_id_type=MESH
        )
    for o in range(1, NI):
        pl.semaphore_signal(
            barrier, inc=1, device_id={"image": lax.rem(i + o, NI)}, device_id_type=MESH
        )

    lane = lax.broadcasted_iota(jnp.int32, (8, PY), 1)
    even = lax.rem(lane, 2) == 0
    at_first = lane == 0
    at_last = lane == PY - 1

    def pack_edges(s, z, r, new):
        rows = pl.ds(8 * r, 8)
        for c in range(5):
            shift = 16 * c + 2 * z
            turned = pltpu.roll(new[c], shift, 1)
            low = lax.rem(shift + PY - 1, PY)
            pltpu.store(
                y_send.at[s, rows, :], turned, mask=(lane == shift) | (lane == low)
            )
            if r == 0:
                x_send[s, 0, c, pl.ds(z, 1), :] = new[c][0:1]
            if r == NB - 1:
                x_send[s, 1, c, pl.ds(z, 1), :] = new[c][7:8]

    def put(s, z, r, new, derived):
        rows = pl.ds(TOP + 8 * r, 8)
        for c in range(5):
            states[s][c, z + 1, rows, :] = new[c]
            prims[s][c, z + 1, rows, :] = derived[c]
        pack_edges(3 if s == 1 else s, z, r, new)

    def halo(s):
        up_d, down_d = lax.rem(d + 1, ND), lax.rem(d + ND - 1, ND)
        up_g, down_g = lax.rem(g + 1, NG), lax.rem(g + NG - 1, NG)
        up_i, down_i = lax.rem(i + 1, NI), lax.rem(i + NI - 1, NI)
        rows = pl.ds(TOP, PX)
        if s == 1:
            below, above = tend.at[:, 0], tend.at[:, PZ - 1]
            to_above, to_below = tend_recv.at[1], tend_recv.at[0]
        else:
            state = states[s]
            below, above = state.at[:, 1, rows, :], state.at[:, PZ, rows, :]
            to_above, to_below = state.at[:, PZ + 1, rows, :], state.at[:, 0, rows, :]
        plan = [
            (below, to_above, {"depth": down_d}),
            (above, to_below, {"depth": up_d}),
            (y_send.at[s], y_recv.at[s, 1], {"image": down_i}),
            (y_send.at[s], y_recv.at[s, 0], {"image": up_i}),
            (x_send.at[s, 0], x_recv.at[s, 1], {"group": down_g}),
            (x_send.at[s, 1], x_recv.at[s, 0], {"group": up_g}),
        ]
        return [
            pltpu.make_async_remote_copy(
                src_ref=src,
                dst_ref=dst,
                send_sem=halo_send.at[s, k],
                recv_sem=halo_recv.at[s, k],
                device_id=device,
                device_id_type=MESH,
            )
            for k, (src, dst, device) in enumerate(plan)
        ]

    row_of = lax.broadcasted_iota(jnp.int32, (8, PY), 0)
    at_top, at_bottom = row_of == 0, row_of == 7

    def from_outside(inner, outer, component, sign):
        prim_in, prim_out = primitives(inner), primitives(outer)
        fastest = jnp.maximum(
            jnp.abs(prim_in[component - 1]) + prim_in[4],
            jnp.abs(prim_out[component - 1]) + prim_out[4],
        )
        flows = flux(outer, prim_out[component - 1], prim_out[3], component)
        return [sign(flows[c]) + fastest * (outer[c] - inner[c]) for c in range(5)]

    def receive_sides(s, copies):
        s = 3 if s == 1 else s
        if copies is not None:
            copies[4].wait_recv()
            copies[5].wait_recv()
        for side, wall in ((0, g == 0), (1, g == NG - 1)):
            own = [x_send[s, side, c] for c in range(5)]
            near = [
                jnp.where(wall, -own[c] if c == 1 else own[c], x_recv[s, side, c])
                for c in range(5)
            ]
            parts = from_outside(own, near, 1, (lambda f: f) if side == 0 else (lambda f: -f))
            for c in range(5):
                x_part[side, c] = parts[c]
        if copies is not None:
            copies[2].wait_recv()
            copies[3].wait_recv()

        def edge(r, carry):
            rows = pl.ds(pl.multiple_of(8 * r, 8), 8)
            own, left, right = y_send[s, rows, :], y_recv[s, 0, rows, :], y_recv[s, 1, rows, :]
            inner, outer = [], []
            for c in range(5):
                inner.append(pltpu.roll(own, (PY - 16 * c) % PY, 1))
                outer.append(
                    jnp.where(
                        even,
                        pltpu.roll(left, (PY + 1 - 16 * c) % PY, 1),
                        pltpu.roll(right, (PY - 1 - 16 * c) % PY, 1),
                    )
                )
            parts = from_outside(inner, outer, 2, lambda f: jnp.where(even, f, -f))
            for c in range(5):
                y_part[c, rows, :] = parts[c]
            return carry

        lax.fori_loop(0, NB, edge, 0, unroll=NB)

    def receive_planes(s, copies):
        state, derived = states[s], prims[s]
        if copies is not None:
            copies[0].wait_recv()
            copies[1].wait_recv()

        def plane(r, carry):
            rows = pl.ds(pl.multiple_of(TOP + 8 * r, 8), 8)
            for z in (0, PZ + 1):
                values = primitives([state[c, z, rows, :] for c in range(5)])
                for c in range(5):
                    derived[c, z, rows, :] = values[c]
            return carry

        lax.fori_loop(0, NB, plane, 0, unroll=NB // 2)

    def add(total, parts):
        return parts if total is None else [t + p for t, p in zip(total, parts)]

    def along_z(s, z, row, cell, prim, total):
        state, derived = states[s], prims[s]
        here = jnp.abs(prim[2]) + prim[4]
        for side in (-1, 1):
            zz = z + 1 + side
            near = [state[c, zz, row : row + 8, :] for c in range(5)]
            q, p = derived[2, zz, row : row + 8, :], derived[3, zz, row : row + 8, :]
            fastest = jnp.maximum(here, jnp.abs(q) + derived[4, zz, row : row + 8, :])
            flows = flux(near, q, p, 3)
            parts = [fastest * (near[c] - cell[c]) for c in range(5)]
            parts = [a + f if side < 0 else a - f for a, f in zip(parts, flows)]
            total = add(total, parts)
        return total

    def centre(s, z, row):
        cell = [states[s][c, z + 1, row : row + 8, :] for c in range(5)]
        return cell, [prims[s][c, z + 1, row : row + 8, :] for c in range(5)]

    def within(s, z, r, with_z):
        state, derived = states[s], prims[s]
        row = TOP + 8 * r
        cell, prim = centre(s, z, row)
        total = along_z(s, z, row, cell, prim, None) if with_z else None
        here = jnp.abs(prim[0]) + prim[4]
        for side in (-1, 1):
            rr = row + side
            near = [state[c, z + 1, rr : rr + 8, :] for c in range(5)]
            q, p = derived[0, z + 1, rr : rr + 8, :], derived[3, z + 1, rr : rr + 8, :]
            fastest = jnp.maximum(here, jnp.abs(q) + derived[4, z + 1, rr : rr + 8, :])
            flows = flux(near, q, p, 1)
            parts = [fastest * (near[c] - cell[c]) for c in range(5)]
            parts = [a + f if side < 0 else a - f for a, f in zip(parts, flows)]
            if side < 0 and r == 0:
                parts = [jnp.where(at_top, 0.0, a) for a in parts]
            if side > 0 and r == NB - 1:
                parts = [jnp.where(at_bottom, 0.0, a) for a in parts]
            total = add(total, parts)
        here = jnp.abs(prim[1]) + prim[4]
        for side in (-1, 1):
            shift = 1 if side < 0 else PY - 1
            near = [pltpu.roll(cell[c], shift, 1) for c in range(5)]
            q, p = pltpu.roll(prim[1], shift, 1), pltpu.roll(prim[3], shift, 1)
            fastest = jnp.maximum(here, pltpu.roll(here, shift, 1))
            flows = flux(near, q, p, 2)
            parts = [fastest * (near[c] - cell[c]) for c in range(5)]
            parts = [a + f if side < 0 else a - f for a, f in zip(parts, flows)]
            outside = at_first if side < 0 else at_last
            total = add(total, [jnp.where(outside, 0.0, a) for a in parts])
        return total

    def completed(s, z, r, with_z, total=None):
        rows = slice(8 * r, 8 * r + 8)
        if total is None:
            total = [tend[c, z, rows, :] for c in range(5)]
        turn = lax.rem(PY - 2 * z, PY)
        for c in range(5):
            edges = pltpu.roll(y_part[c, rows, :], turn, 1)
            total[c] = total[c] + jnp.where(at_first | at_last, edges, 0.0)
        for side, block, place in ((0, 0, at_top), (1, NB - 1, at_bottom)):
            if r == block:
                for c in range(5):
                    line = jnp.broadcast_to(x_part[side, c, pl.ds(z, 1), :], (8, PY))
                    total[c] = total[c] + jnp.where(place, line, 0.0)
        if with_z:
            row = TOP + 8 * r
            cell, prim = centre(s, z, row)
            total = along_z(s, z, row, cell, prim, total)
        return total

    def middle_planes(visit):
        def one(z, carry):
            for r in range(NB):
                visit(z, r, False)
            return carry

        lax.fori_loop(1, PZ - 1, one, 0)

    def all_planes(visit):
        def one(z, carry):
            for r in range(NB):
                visit(z, r, False)
            return carry

        lax.fori_loop(0, PZ, one, 0, unroll=4)

    def end_planes(visit):
        def one(k, carry):
            for r in range(NB):
                visit((PZ - 1) * k, r, True)
            return carry

        lax.fori_loop(0, 2, one, 0, unroll=2)

    def inside(s):
        def visit(z, r, at_end):
            total = within(s, z, r, not at_end)
            for c in range(5):
                tend[c, z, 8 * r : 8 * r + 8, :] = total[c]

        middle_planes(visit)
        end_planes(visit)

    for load in loads[:3]:
        load.wait()

    def signals(z, most):
        for r in range(NB):
            rho, u, v, w, p = [raw[c, z, 8 * r : 8 * r + 8, :] for c in range(5)]
            sound = jnp.sqrt(HEAT_RATIO * p / rho)
            prims[0][4, z + 1, TOP + 8 * r : TOP + 8 * r + 8, :] = sound
            most = jnp.maximum(most, jnp.abs(u) + jnp.abs(v) + jnp.abs(w) + 3.0 * sound)
        return most

    max_own[...] = lax.fori_loop(0, PZ, signals, jnp.zeros((8, PY), jnp.float32), unroll=2)

    def first(z, carry):
        for r in range(NB):
            rho, u, v, w, p = [raw[c, z, 8 * r : 8 * r + 8, :] for c in range(5)]
            energy = p / (HEAT_RATIO - 1.0) + 0.5 * rho * (u * u + v * v + w * w)
            sound = prims[0][4, z + 1, TOP + 8 * r : TOP + 8 * r + 8, :]
            put(0, z, r, [rho, rho * u, rho * v, rho * w, energy], [u, v, w, p, sound])
        return carry

    pl.semaphore_wait(barrier, ND + NG + NI - 3)

    for o in range(1, NI):
        pl.semaphore_signal(
            token, inc=1, device_id={"image": lax.rem(i + o, NI)}, device_id_type=MESH
        )
    lines = [
        pltpu.make_async_remote_copy(
            src_ref=max_own,
            dst_ref=max_line.at[o - 1],
            send_sem=line_send.at[o - 1],
            recv_sem=line_recv.at[o - 1],
            device_id={"depth": lax.rem(d + o, ND)},
            device_id_type=MESH,
        )
        for o in range(1, ND)
    ]
    for copy in lines:
        copy.start()
    lax.fori_loop(0, PZ, first, 0)
    halos = [halo(0)]
    for copy in halos[0]:
        copy.start()
    inside(0)
    for copy in lines:
        copy.wait_recv()
    most = max_own[...]
    for o in range(ND - 1):
        most = jnp.maximum(most, max_line[o])
    max_mid[...] = most
    planes = [
        pltpu.make_async_remote_copy(
            src_ref=max_mid,
            dst_ref=max_plane.at[k],
            send_sem=plane_send.at[k],
            recv_sem=plane_recv.at[k],
            device_id={"group": lax.rem(g + og, NG), "image": lax.rem(i + oi, NI)},
            device_id_type=MESH,
        )
        for k, (og, oi) in enumerate(PAIRS)
    ]
    pl.semaphore_wait(token, NI - 1)
    for copy in planes:
        copy.start()

    receive_sides(0, halos[0])
    receive_planes(0, halos[0])

    def complete(z, r, at_end):
        total = completed(0, z, r, at_end)
        for c in range(5):
            tend[c, z, 8 * r : 8 * r + 8, :] = total[c]
        pack_edges(1, z, r, total)

    halos.append(halo(1))
    end_planes(complete)
    for copy in halos[1][:2]:
        copy.start()
    middle_planes(complete)
    for copy in halos[1][2:]:
        copy.start()

    for load in loads[3:]:
        load.wait()
    pick = lax.rem(2 * lane, PY)
    low, high = index_ref[:, 0:PY], index_ref[:, PY : 2 * PY]
    half = lane < PY // 2
    bins = [
        jnp.where(half, take(low, pick + k), take(high, pick + k)) for k in range(2)
    ]
    words = []
    for c in range(4):
        pal_low = jnp.broadcast_to(palette_ref[c : c + 1, 0:PY], (8, PY))
        pal_high = jnp.broadcast_to(palette_ref[c : c + 1, PY : 2 * PY], (8, PY))
        levels = []
        for b in bins:
            spot = b & (PY - 1)
            colour = jnp.where(b < PY, take(pal_low, spot), take(pal_high, spot))
            levels.append((colour * (1.0 / STEP) + 0.5).astype(jnp.int32))
        levels.append(pltpu.roll(levels[0], PY - 1, 1))
        words.append(levels)
    for k in range(3):
        for c in range(2):
            tables[2 * k + c] = (words[c][k] - 32768) * 65536 + words[c + 2][k]
    for copy in planes:
        copy.wait_recv()
    most = max_mid[...]
    for k in range(len(PAIRS)):
        most = jnp.maximum(most, max_plane[k])
    half_step = (0.5 * COURANT) / jnp.broadcast_to(
        jnp.max(most, axis=(0, 1), keepdims=True), (8, PY)
    )

    def section_one(z, r, at_end):
        row = TOP + 8 * r
        new = [
            u_first[c, z + 1, row : row + 8, :]
            + half_step * tend[c, z, 8 * r : 8 * r + 8, :]
            for c in range(5)
        ]
        put(1, z, r, new, primitives(new))

    def section_two(z, r, at_end):
        total = completed(1, z, r, False, within(1, z, r, True))
        row = TOP + 8 * r
        new = [
            0.75 * u_first[c, z + 1, row : row + 8, :]
            + 0.25 * (u_second[c, z + 1, row : row + 8, :] + half_step * total[c])
            for c in range(5)
        ]
        put(2, z, r, new, primitives(new))

    def section_three(z, r, at_end):
        total = completed(2, z, r, False)
        row = TOP + 8 * r
        rows = slice(8 * r, 8 * r + 8)
        new = [
            u_first[c, z + 1, row : row + 8, :] * (1.0 / 3.0)
            + (2.0 / 3.0) * (u_third[c, z + 1, row : row + 8, :] + half_step * total[c])
            for c in range(5)
        ]
        for c in range(5):
            fluid[c, z, rows, :] = new[c]
        inverse = 1.0 / new[0]
        kinetic = 0.5 * inverse * (new[1] * new[1] + new[2] * new[2] + new[3] * new[3])
        position = jnp.clip(new[0] - 0.5, 0.0, 1.0) * 255.0
        index = (position * 0.5).astype(jnp.int32)
        past = position - 2.0 * index.astype(jnp.float32)
        shade_index[z, rows, :] = index
        shade[0, z, rows, :] = 1.0 - jnp.minimum(past, 1.0)
        shade[1, z, rows, :] = jnp.maximum(past - 1.0, 0.0)
        shade[2, z, rows, :] = new[0] * (-2.0 * STEP / (PZ * ND))
        shade[3, z, rows, :] = (STEP * (HEAT_RATIO - 1.0)) * (new[4] - kinetic) * inverse

    all_planes(section_one)
    for copy in halos[1]:
        copy.wait_recv()
    for side in range(2):
        for c in range(5):
            x_recv[3, side, c] = x_recv[0, side, c] + half_step * x_recv[1, side, c]
        for r in range(NB):
            rows = slice(8 * r, 8 * r + 8)
            y_recv[3, side, rows, :] = (
                y_recv[0, side, rows, :] + half_step * y_recv[1, side, rows, :]
            )

    def outer_planes(r, carry):
        rows = pl.ds(pl.multiple_of(8 * r, 8), 8)
        padded = pl.ds(pl.multiple_of(TOP + 8 * r, 8), 8)
        for side, z in ((0, 0), (1, PZ + 1)):
            for c in range(5):
                u_second[c, z, padded, :] = (
                    u_first[c, z, padded, :] + half_step * tend_recv[side, c, rows, :]
                )
        return carry

    lax.fori_loop(0, NB, outer_planes, 0, unroll=2)
    receive_sides(1, None)
    receive_planes(1, None)
    halos.append(halo(2))
    end_planes(section_two)
    for copy in halos[2][:2]:
        copy.start()
    middle_planes(section_two)
    for copy in halos[2][2:]:
        copy.start()
    for copy in halos[1]:
        copy.wait_send()
    inside(2)
    receive_planes(2, halos[2])

    def with_planes(z, r, at_end):
        row = TOP + 8 * r
        total = along_z(2, z, row, *centre(2, z, row), [tend[c, z, 8 * r : 8 * r + 8, :] for c in range(5)])
        for c in range(5):
            tend[c, z, 8 * r : 8 * r + 8, :] = total[c]

    end_planes(with_planes)
    receive_sides(2, halos[2])
    all_planes(section_three)
    fluid_store = pltpu.make_async_copy(fluid, fluid_out, store_sem.at[0])
    fluid_store.start()

    chip, core = d // 2, lax.rem(d, 2)

    def render(t):
        rows_of = [
            jnp.broadcast_to(tables[k, pl.ds(t, 1), :], (8, PY)) for k in range(6)
        ]
        for r in range(NB):
            rows = slice(8 * r, 8 * r + 8)
            clear, light = None, None
            for z in range(PZ):
                index = shade_index[z, rows, :]
                scale = [shade[0, z, rows, :], None, shade[1, z, rows, :]]
                scale[1] = 1.0 - scale[0] - scale[2]
                looked = [None] * 4
                for k in range(3):
                    for c in range(2):
                        word = take(rows_of[2 * k + c], index)
                        upper = (word >> 16).astype(jnp.float32) * scale[k]
                        lower = (word & 65535).astype(jnp.float32) * scale[k]
                        looked[c] = upper if k == 0 else looked[c] + upper
                        looked[c + 2] = lower if k == 0 else looked[c + 2] + lower
                looked[0] = looked[0] + 32768.0
                looked[1] = looked[1] + 32768.0
                through = jnp.exp(looked[3] * shade[2, z, rows, :])
                weight = (1.0 - through) * shade[3, z, rows, :]
                if z == 0:
                    light = [weight * looked[c] for c in range(3)]
                    clear = through
                else:
                    weight = weight * clear
                    light = [light[c] + weight * looked[c] for c in range(3)]
                    clear = clear * through
            sheet[t, 0, rows, :] = clear
            for c in range(3):
                sheet[t, c + 1, rows, :] = light[c]

    def pair_copy(slot):
        return pltpu.make_async_remote_copy(
            src_ref=sheet.at[2 * slot + 1 - core],
            dst_ref=pair_recv.at[slot],
            send_sem=pair_send_sem.at[slot],
            recv_sem=pair_recv_sem.at[slot],
            device_id={"depth": 2 * chip + 1 - core},
            device_id_type=MESH,
        )

    def chip_copy(owner, source):
        return pltpu.make_async_remote_copy(
            src_ref=joined.at[owner],
            dst_ref=chip_recv.at[source],
            send_sem=chip_send_sem.at[owner],
            recv_sem=chip_recv_sem.at[source],
            device_id={"depth": 2 * owner + core},
            device_id_type=MESH,
        )

    def turn(k, carry):
        mine = (k == 3) | (k == 4) | (k == 5) | (k == 7)
        offset = jnp.where(k < 6, 1 + lax.rem(k, 3), 0)
        owner = lax.rem(chip + offset, 4)
        t = 2 * owner + jnp.where(mine, core, 1 - core)
        render(t)

        @pl.when(jnp.logical_not(mine))
        def _():
            pair_copy(owner).start()

        @pl.when(mine)
        def _():
            pair_copy(owner).wait_recv()
            for r in range(NB):
                rows = slice(8 * r, 8 * r + 8)
                own_clear, other_clear = sheet[t, 0, rows, :], pair_recv[owner, 0, rows, :]
                own_scale = jnp.where(core == 0, 1.0, other_clear)
                other_scale = jnp.where(core == 0, own_clear, 1.0)
                joined[owner, 0, rows, :] = own_clear * other_clear
                for c in range(1, 4):
                    joined[owner, c, rows, :] = (
                        own_scale * sheet[t, c, rows, :]
                        + other_scale * pair_recv[owner, c, rows, :]
                    )

        @pl.when(mine & (k < 6))
        def _():
            chip_copy(owner, chip).start()

        return carry

    lax.fori_loop(0, 8, turn, 0)
    for o in (1, 3, 2):
        source = lax.rem(chip + o, 4)
        chip_copy(source, source).wait_recv()
    chip_recv[chip] = joined[chip]
    ahead = chip_recv[0, 0]
    light = [chip_recv[0, c] for c in range(1, 4)]
    for k in range(1, 4):
        for c in range(3):
            light[c] = light[c] + ahead * chip_recv[k, c + 1]
        if k < 3:
            ahead = ahead * chip_recv[k, 0]
    for c in range(3):
        picture[c] = light[c]
    picture_store = pltpu.make_async_copy(picture, picture_out, store_sem.at[1])
    picture_store.start()

    for copy in lines + planes + halos[0] + halos[2]:
        copy.wait_send()
    for k in range(4):
        pair_copy(k).wait_send()
    for o in range(1, 4):
        source = lax.rem(chip + o, 4)
        chip_copy(source, source).wait_send()
    fluid_store.wait()
    picture_store.wait()


def shards(density, velocity, pressure, palette, palette_index):
    f32 = jnp.float32
    any_space = pl.BlockSpec(memory_space=pl.ANY)
    padded = (5, PZ + 2, PX + 16, PY)
    dma = pltpu.SemaphoreType.DMA
    fluid_state, picture = pl.pallas_call(
        kernel,
        out_shape=(
            jax.ShapeDtypeStruct((5, PZ, PX, PY), f32),
            jax.ShapeDtypeStruct((3, PX, PY), f32),
        ),
        in_specs=[any_space] * 5,
        out_specs=(any_space, any_space),
        scratch_shapes=[
            pltpu.VMEM((5, PZ, PX, PY), f32),
            pltpu.VMEM((4, 2 * PY), f32),
            pltpu.VMEM((8, 2 * PY), jnp.int32),
            pltpu.VMEM(padded, f32),
            pltpu.VMEM(padded, f32),
            pltpu.VMEM(padded, f32),
            pltpu.VMEM(padded, f32),
            pltpu.VMEM(padded, f32),
            pltpu.VMEM((5, PZ, PX, PY), f32),
            pltpu.VMEM((2, 5, PX, PY), f32),
            pltpu.VMEM((4, 2, 5, PZ, PY), f32),
            pltpu.VMEM((4, 2, 5, PZ, PY), f32),
            pltpu.VMEM((4, PX, PY), f32),
            pltpu.VMEM((4, 2, PX, PY), f32),
            pltpu.VMEM((2, 5, PZ, PY), f32),
            pltpu.VMEM((5, PX, PY), f32),
            pltpu.VMEM((8, PY), f32),
            pltpu.VMEM((ND - 1, 8, PY), f32),
            pltpu.VMEM((8, PY), f32),
            pltpu.VMEM((len(PAIRS), 8, PY), f32),
            pltpu.VMEM((5, PZ, PX, PY), f32),
            pltpu.VMEM((4, PZ, PX, PY), f32),
            pltpu.VMEM((PZ, PX, PY), jnp.int32),
            pltpu.VMEM((6, 8, PY), jnp.int32),
            pltpu.VMEM((8, 4, PX, PY), f32),
            pltpu.VMEM((4, 4, PX, PY), f32),
            pltpu.VMEM((4, 4, PX, PY), f32),
            pltpu.VMEM((4, 4, PX, PY), f32),
            pltpu.VMEM((3, PX, PY), f32),
            dma((5,)),
            dma((2,)),
            dma((3, 6)),
            dma((3, 6)),
            dma((ND - 1,)),
            dma((ND - 1,)),
            dma((len(PAIRS),)),
            dma((len(PAIRS),)),
            pltpu.SemaphoreType.REGULAR,
            dma((4,)),
            dma((4,)),
            dma((4,)),
            dma((4,)),
        ],
        compiler_params=pltpu.CompilerParams(
            collective_id=0, has_side_effects=True, vmem_limit_bytes=60 * 1024 * 1024
        ),
    )(density, velocity, pressure, palette, palette_index)
    return fluid_state, picture[None]


def solution(mesh):
    return jax.shard_map(
        shards,
        mesh=mesh,
        in_specs=(
            P("depth", "group", "image"),
            P(None, "depth", "group", "image"),
            P("depth", "group", "image"),
            P(),
            P(),
        ),
        out_specs=(P(None, "depth", "group", "image"), P("depth", None, "group", "image")),
        check_vma=False,
    )
```
